32 devices in a mesh: subj: 2 (over y), band: 4 (over z), lon: 2 (over x), pop: 2 (over core).
Axes of the slice: x: 2, y: 2, z: 4, core: 2. Of those that a mesh axis runs over, the one named last changes fastest.
Arguments:
- activity: float32 [16, 640, 1280], P(('subj', 'pop'), 'band', 'lon'), parts along dimension 0, may hold values from -6 to 6
- drive: bfloat16 [16, 640, 1280], P(('subj', 'pop'), 'band', 'lon'), parts along dimension 0, may hold values from -6 to 6
- basis: bfloat16 [1280, 320, 640], P(('subj', 'band', 'lon')), parts along dimension 0, may hold values from -6 to 6
- kernels: float32 [4, 640], replicated, may hold values from 0.2 to 2
- conn_block: int32 [8, 8], replicated, may hold values from 0 to 3
- coupling: float32 [16, 8], P('subj'), parts along dimension 0, may hold values from -2.5 to 2.5
- rate_params: float32 [8, 8], P('subj'), parts along dimension 0, may hold values from 0.5 to 2
Outputs:
- activity_next: float32 [16, 640, 1280], P(('subj', 'pop'), 'band', 'lon'), parts along dimension 0
The draws below stay inside these ranges and needn't reach their ends.
There are 2 independent parts, one for each index of `subj`. The reference program is written for one: setup_inputs(seed, part) draws one part's arguments, and reference() takes and returns one part's arrays. A program takes and returns all parts, laid end to end along the dimension named above; an argument that names none is the same for every part. Nothing has to cross between parts.
All inputs are finite; a program needn't handle non-finite values.
Results may differ from the reference program's by a relative error of at most 0.0095.
Values may be sent and summed in bfloat16 or wider, within the bound.
No kernel may reach another device: no remote copies, remote signals or barrier semaphores. Data moves between devices by JAX's collectives and lax.ppermute only.
A program may use at most 192 MiB of HBM per device.

```python
import math
import jax
import jax.numpy as jnp
from jax import lax

POP = 8
NK = 4
NLAT = 640
NLON = 1280
DEG = 640
STEPS = 2


def place_ends(values, key, least, top_value):
    dims = values.shape
    index_at = [jax.random.randint(jax.random.fold_in(key, axis), (), 0, dims[axis]) for axis in range(len(dims))]
    values = values.at[tuple(index_at)].set(least)
    longest = dims.index(max(dims))
    index_at[longest] = (index_at[longest] + 1) % dims[longest]
    return values.at[tuple(index_at)].set(top_value)


def levels(key, shape, cuts, least, high):
    level = 1.0
    for dim, blocks in cuts:
        heights = jax.random.uniform(jax.random.fold_in(jax.random.fold_in(key, 6), dim), (blocks,), jnp.float32, least / len(cuts), high / len(cuts))
        level = level * jnp.repeat(jnp.exp(heights), shape[dim] // blocks).reshape((-1,) + (1,) * (len(shape) - 1 - dim))
    return level


def noise(rng, shape, spread, bound, cuts=(), kind=jnp.bfloat16):
    array = spread * jax.random.normal(rng, shape, jnp.float32)
    if cuts:
        array = array * levels(rng, shape, cuts, -0.22, 0.18)
    return jnp.clip(array, -bound, bound).astype(kind)


def setup_inputs(seed: int = 0, part: int = 0) -> dict:
    splits = jax.random.split(jax.random.key(seed), 8)
    part_splits = jax.random.split(jax.random.fold_in(splits[7], part), 8)
    activity = noise(part_splits[0], (POP, NLAT, NLON), 1.0, 6.0, ((0, 2), (1, 4), (2, 2)), jnp.float32)
    drive = noise(part_splits[1], (POP, NLAT, NLON), 1.0, 6.0, ((0, 2), (1, 4), (2, 2)))
    basis = noise(part_splits[2], (DEG, NLAT // 2, DEG), 1.0, 6.0, ((0, 8),))
    kernels = jnp.clip(jnp.exp(jax.random.uniform(splits[3], (NK, DEG), jnp.float32, math.log(0.2), math.log(2.0))), 0.2, 2.0)
    conn_block = place_ends(jax.random.randint(splits[4], (POP, POP), 0, NK), jax.random.fold_in(splits[4], 1), 0, NK - 1).astype(jnp.int32)
    coupling = noise(part_splits[5], (POP, POP), 0.35, 2.5, (), jnp.float32)
    rate_params = jnp.clip(jax.random.uniform(part_splits[6], (4, POP), jnp.float32, 0.5, 2.0), 0.5, 2.0)
    return {"activity": activity, "drive": drive, "basis": basis, "kernels": kernels, "conn_block": conn_block, "coupling": coupling, "rate_params": rate_params}


time_step = 0.5


def fourier_table():
    longitude = jnp.arange(NLON, dtype=jnp.int32)
    wavenumber = jnp.arange(DEG, dtype=jnp.int32)
    phase = (longitude[:, None] * wavenumber[None, :]) % NLON
    angle = phase.astype(jnp.float32) * (2.0 * math.pi / NLON)
    return jnp.stack([jnp.cos(angle), jnp.sin(angle)], axis=1).astype(jnp.bfloat16)


def lat_weights():
    row_index = jnp.arange(NLAT // 2, dtype=jnp.float32)
    colatitude = math.pi * (4.0 * row_index + 3.0) / (4.0 * NLAT + 2.0)
    return math.pi * jnp.sin(colatitude) / NLAT


def round_trip(values):
    return lax.optimization_barrier(values.astype(jnp.bfloat16)).astype(jnp.float32)


def reference(activity, drive, basis, kernels, conn_block, coupling, rate_params):
    highest = lax.Precision.HIGHEST
    cos_sin = fourier_table().astype(jnp.float32)
    weights = lat_weights()
    half_lat = NLAT // 2
    quarter = DEG // 2
    gain_row, thresh, decay_row, lateral = rate_params[0], rate_params[1], rate_params[2], rate_params[3]
    onehot = (conn_block[..., None] == jnp.arange(kernels.shape[0], dtype=jnp.int32)).astype(jnp.float32)
    mixing = coupling[..., None] * jnp.einsum('ijb,bn->ijn', onehot, kernels, precision=highest)
    wavenumber = jnp.arange(DEG, dtype=jnp.int32)
    degree = jnp.arange(DEG, dtype=jnp.int32)
    amplitude = jnp.where(wavenumber == 0, 1.0, 2.0).astype(jnp.float32)
    slots = jnp.arange(2, dtype=jnp.int32)

    def analyse(block_item):
        spectrum, basis_block, wavenum = block_item
        northern = spectrum[..., :half_lat]
        southern = jnp.flip(spectrum[..., half_lat:], axis=-1)
        even_part = round_trip(weights * (northern + southern))
        odd_part = round_trip(weights * (northern - southern))
        parity_pick = slots == wavenum % 2
        operand = jnp.where(parity_pick[None, None, :, None], even_part[:, :, None, :], odd_part[:, :, None, :])
        basis_split = basis_block.astype(jnp.float32).reshape(half_lat, quarter, 2)
        coefficients = jnp.einsum('icsj,jqs->icqs', operand, basis_split, precision=highest)
        coefficients = coefficients.reshape(POP, 2, DEG)
        return jnp.where(degree >= wavenum, coefficients, 0.0)

    def synthesise(block_item):
        spectrum, basis_block, wavenum = block_item
        basis_split = basis_block.astype(jnp.float32).reshape(half_lat, quarter, 2)
        degree_parts = jnp.einsum('icqs,jqs->icsj', spectrum.reshape(POP, 2, quarter, 2), basis_split, precision=highest)
        parity_pick = (slots == wavenum % 2)[None, None, :, None]
        same_parity = jnp.sum(jnp.where(parity_pick, degree_parts, 0.0), axis=2)
        other_parity = jnp.sum(jnp.where(parity_pick, 0.0, degree_parts), axis=2)
        joined = jnp.concatenate([same_parity + other_parity, jnp.flip(same_parity - other_parity, axis=-1)], axis=-1)
        return joined.astype(jnp.bfloat16)

    activity_now = activity
    for step_index in range(STEPS):
        rates = jax.nn.sigmoid(gain_row[:, None, None] * (activity_now - thresh[:, None, None]))
        rates_f32 = round_trip(rates)
        fourier = jnp.einsum('ijk,kcm->micj', rates_f32, cos_sin, precision=highest)
        fourier = round_trip(fourier)
        coeffs = lax.map(analyse, (fourier, basis, wavenumber))
        mixed_spec = jnp.einsum('ijn,mjcn->micn', mixing, coeffs, precision=highest)
        mixed_spec = round_trip(mixed_spec)
        synthesis = lax.map(synthesise, (mixed_spec, basis, wavenumber))
        scaled = synthesis.astype(jnp.float32) * amplitude[:, None, None, None]
        synth_field = jnp.einsum('micj,kcm->ijk', scaled, cos_sin, precision=highest) / NLON
        padded = jnp.pad(rates_f32, ((0, 0), (1, 1), (0, 0)))
        lateral_term = (jnp.roll(rates_f32, 1, axis=2) + jnp.roll(rates_f32, -1, axis=2)
                        + padded[:, 2:, :] + padded[:, :-2, :] - 4.0 * rates_f32)
        forcing = (-decay_row[:, None, None] * activity_now + synth_field
                   + lateral[:, None, None] * lateral_term + drive.astype(jnp.float32))
        activity_now = activity_now + time_step * forcing
    return activity_now
```

```python
import functools
import math

import jax
import jax.numpy as jnp
import ml_dtypes
import numpy as np
from jax import lax
from jax.experimental import pallas as pl
from jax.experimental.pallas import tpu as pltpu
from jax.sharding import PartitionSpec as P

STEPS = 2
time_step = 0.5
F32 = jnp.float32
BF16 = jnp.bfloat16
OWNERS = ("band", "lon")
EVERYONE = ("band", "lon", "pop")
MIB = 1 << 20


def call(body, out_shape, vmem_mib, flops=0, nbytes=0, **kw):
    return pl.pallas_call(
        body,
        out_shape=out_shape,
        compiler_params=pltpu.CompilerParams(vmem_limit_bytes=vmem_mib * MIB),
        cost_estimate=pl.CostEstimate(flops=flops, bytes_accessed=nbytes, transcendentals=0),
        **kw,
    )


def whole():
    return pl.BlockSpec(memory_space=pltpu.VMEM)


def scalars():
    return pl.BlockSpec(memory_space=pltpu.SMEM)


def shape(*dims, dtype=BF16):
    return jax.ShapeDtypeStruct(dims, dtype)


def nt_dot(a, b):
    return lax.dot_general(a, b, (((1,), (1,)), ((), ())), preferred_element_type=F32)


def fourier_table(nlon, deg):
    phase = np.arange(deg, dtype=np.int64)[:, None] * np.arange(nlon, dtype=np.int64)[None, :] % nlon
    angle = phase.astype(np.float32) * np.float32(2.0 * math.pi / nlon)
    return np.stack([np.cos(angle), np.sin(angle)]).astype(ml_dtypes.bfloat16)


def lat_weights(nlat):
    row_index = np.arange(nlat // 2, dtype=np.float32)
    colatitude = np.float32(math.pi) * (4.0 * row_index + 3.0) / np.float32(4.0 * nlat + 2.0)
    return (np.float32(math.pi) * np.sin(colatitude) / np.float32(nlat)).astype(np.float32)


def grid_rates_body(params, flip, act, drive, rates, carried):
    i = pl.program_id(0)
    gain, thresh, decay = params[0, i], params[1, i], params[2, i]
    halves, rows = rates.shape[0], rates.shape[2]
    for h in range(halves):
        u = act[0, h * rows : (h + 1) * rows, :]
        d = drive[0, h * rows : (h + 1) * rows, :].astype(F32)
        r = jax.nn.sigmoid(gain * (u - thresh)).astype(BF16)
        c = ((1.0 - time_step * decay) * u + time_step * d).astype(BF16)
        rates[h, 0] = jnp.dot(flip[...], r, preferred_element_type=F32).astype(BF16)
        carried[h, 0] = jnp.dot(flip[...], c, preferred_element_type=F32).astype(BF16)


def put_fourier(table, rates, fourier, groups_at_once):
    halves, pops, rows, cols = rates.shape
    groups, count, lanes = fourier.shape
    block = groups_at_once * count
    for b in range(groups // groups_at_once):
        parts = []
        for c in range(2):
            total = None
            for h in range(halves):
                t = table[c, b * block : (b + 1) * block, h * cols : (h + 1) * cols]
                term = nt_dot(t, rates[h].reshape(pops * rows, cols))
                total = term if total is None else total + term
            parts.append(total)
        joined = jnp.concatenate(parts, axis=1)
        for g in range(groups_at_once):
            fourier[b * groups_at_once + g] = joined[g * count : (g + 1) * count].astype(BF16)


def put_edges(rates, polar, inner_edge):
    halves, pops, rows, cols = rates.shape
    for h in range(halves):
        strips = [rates[h, i].astype(F32) for i in range(pops)]
        at = slice(h * cols, (h + 1) * cols)
        polar[:, at] = jnp.concatenate([v[0:1] for v in strips], axis=0).astype(BF16)
        last = jnp.concatenate([v[rows - 1 : rows] for v in strips], axis=0)
        inner_edge[:, at] = last.astype(BF16)


def first_fourier_body(table, rates, fourier, polar, inner_edge):
    put_edges(rates, polar, inner_edge)
    put_fourier(table, rates, fourier, 4)


def lateral_body(params, rates, from_pole, from_equator, across, *refs):
    out = refs[-1]
    halves, pops, rows, cols = rates.shape
    nlon = halves * cols
    before = from_pole[...].astype(F32)
    after = from_equator[...].astype(F32) + across[...].astype(F32)
    for i in range(pops):
        r = jnp.concatenate([rates[h, i].astype(F32) for h in range(halves)], axis=1)
        east = pltpu.roll(r, 1, 1)
        west = pltpu.roll(r, nlon - 1, 1)
        row = lax.broadcasted_iota(jnp.int32, (rows, nlon), 0)
        up = jnp.where(row == 0, before[i : i + 1], pltpu.roll(r, 1, 0))
        down = jnp.where(row == rows - 1, after[i : i + 1], pltpu.roll(r, rows - 1, 0))
        term = (time_step * params[3, i]) * (east + west + up + down - 4.0 * r)
        if len(refs) == 2:
            term = term + (1.0 - time_step * params[2, i]) * refs[0][i]
        out[i] = term


def legendre_body(
    first, spectrum, weight, mixing, basis, out, even_s, odd_s, north_s, south_s
):
    groups, count, lanes = spectrum.shape
    tiles = even_s.shape[0]
    block, half_lat, deg = basis.shape
    pops = mixing.shape[0]
    src = weight.shape[0]
    cores = groups // (2 * src)
    piece = half_lat // src
    slots = lanes // piece
    pops_here = slots // 2
    pad = tiles * 128 - half_lat
    step = pl.program_id(0)

    def rows_of(p, q):
        b = (q // pops_here) * pops + p * pops_here + q % pops_here
        return slice(b * count, (b + 1) * count)

    @pl.when(step == 0)
    def _():
        for p in range(cores):
            evens, odds = [], []
            for s in range(src):
                north = spectrum[s * cores + p].astype(F32)
                south = spectrum[(2 * src - 1 - s) * cores + p].astype(F32)
                w = weight[s : s + 1]
                evens.append((w * (north + south)).astype(BF16).astype(F32))
                odds.append((w * (north - south)).astype(BF16).astype(F32))
            for q in range(slots):
                for parts, scratch in ((evens, even_s), (odds, odd_s)):
                    strips = [v[:, q * piece : (q + 1) * piece] for v in parts]
                    if pad:
                        strips.append(jnp.zeros((count, pad), F32))
                    joined = jnp.concatenate(strips, axis=1)
                    for t in range(tiles):
                        scratch[t, rows_of(p, q), :] = joined[:, t * 128 : (t + 1) * 128]

    degree = lax.broadcasted_iota(jnp.int32, (2 * pops, deg), 1)
    for at in range(block):
        r = step * block + at
        m = first[0] + r
        rows = pl.ds(r, 2 * pops, stride=count)
        lhs = jnp.concatenate(
            [
                jnp.concatenate([scratch[t, rows, :] for t in range(tiles)], axis=1)
                for scratch in (even_s, odd_s)
            ],
            axis=0,
        )[:, :half_lat].astype(BF16)
        both = jnp.dot(lhs, basis[at], preferred_element_type=F32)
        odd = ((degree - m) & 1) == 1
        coeffs = jnp.where(odd, both[2 * pops :], both[: 2 * pops])
        coeffs = jnp.where(degree >= m, coeffs, 0.0)
        mixed = []
        for c in range(2):
            total = None
            for j in range(pops):
                term = mixing[j] * coeffs[c * pops + j : c * pops + j + 1]
                total = term if total is None else total + term
            mixed.append(total)
        mixed = jnp.concatenate(mixed, axis=0)
        amplitude = jnp.where(m == 0, 1.0, 2.0)
        lhs2 = jnp.concatenate([mixed, jnp.where(odd, -mixed, mixed)], axis=0).astype(BF16)
        field = nt_dot(lhs2, basis[at]) * amplitude
        if pad:
            field = jnp.concatenate([field, jnp.zeros((4 * pops, pad), F32)], axis=1)
        for t in range(tiles):
            north_s[t, rows, :] = field[: 2 * pops, t * 128 : (t + 1) * 128]
            south_s[t, rows, :] = field[2 * pops :, t * 128 : (t + 1) * 128]

    @pl.when(step == pl.num_programs(0) - 1)
    def _():
        for scratch, south in ((north_s, False), (south_s, True)):
            for p in range(cores):
                wide = [
                    jnp.concatenate(
                        [scratch[t, rows_of(p, q), :] for t in range(tiles)], axis=1
                    )
                    for q in range(slots)
                ]
                for s in range(src):
                    to = (2 * src - 1 - s if south else s) * cores + p
                    strips = [v[:, s * piece : (s + 1) * piece] for v in wide]
                    out[to] = jnp.concatenate(strips, axis=1).astype(BF16)


def synth_of(spectrum, table, cols, h):
    _, both = spectrum
    half = both.shape[0] // 2
    total = None
    for c in range(2):
        term = jnp.dot(
            both[c * half : (c + 1) * half, :],
            table[c, :, h * cols : (h + 1) * cols],
            preferred_element_type=F32,
        )
        total = term if total is None else total + term
    return total


def turned(spectrum, turned_s):
    groups = spectrum.shape[0]
    stacked = jnp.concatenate([spectrum[g].astype(F32) for g in range(groups)], axis=0)
    turned_s[...] = stacked.T.astype(BF16)


def middle_body(
    params, table, spectrum, lateral, carried, fourier, rates, polar, inner_edge, inner, turned_s
):
    halves, pops, rows, cols = rates.shape
    turned(spectrum, turned_s)
    for h in range(halves):
        synth = synth_of((None, turned_s), table, cols, h) * (time_step / (halves * cols))
        for i in range(pops):
            v = lateral[i, :, h * cols : (h + 1) * cols] + synth[i * rows : (i + 1) * rows]
            inner[i, :, h * cols : (h + 1) * cols] = v
            u = carried[h, i].astype(F32) + v
            rates[h, i] = jax.nn.sigmoid(params[0, i] * (u - params[1, i])).astype(BF16)
    put_edges(rates, polar, inner_edge)
    put_fourier(table, rates, fourier, 4)


def last_body(table, spectrum, lateral, out, turned_s):
    halves, pops, rows, cols = out.shape
    turned(spectrum, turned_s)
    for h in range(halves):
        synth = synth_of((None, turned_s), table, cols, h) * (time_step / (halves * cols))
        for i in range(pops):
            v = lateral[i, :, h * cols : (h + 1) * cols] + synth[i * rows : (i + 1) * rows]
            out[h, i] = v.astype(BF16)


def grid_update_body(params, flip, act, drive, inner, out):
    i = pl.program_id(0)
    keep = 1.0 - time_step * params[2, i]
    halves, rows = inner.shape[0], inner.shape[2]
    for h in range(halves):
        at = slice(h * rows, (h + 1) * rows)
        d = time_step * drive[0, at, :].astype(F32)
        back = jnp.dot(flip[...], inner[h, 0], preferred_element_type=F32)
        out[0, at, :] = keep * (keep * act[0, at, :] + d) + d + back


def by_parts(activity, drive, basis, kernels, conn_block, coupling, rate_params):
    pops_here, lat_here, cols = activity.shape
    owned, half_lat, deg = basis.shape
    bands, lons, cores = (lax.axis_size(a) for a in ("band", "lon", "pop"))
    owners = bands * lons
    groups = owners * cores
    count = owned // cores
    rows = lat_here // lons
    nlat, nlon = bands * lat_here, lons * cols
    pops = pops_here * cores
    lanes = 2 * pops_here * rows
    band, lon, core = (lax.axis_index(a) for a in ("band", "lon", "pop"))
    owner = band * lons + lon
    southern = band >= bands // 2
    params = lax.dynamic_slice_in_dim(rate_params, core * pops_here, pops_here, 1)
    table = jnp.asarray(fourier_table(nlon, deg))
    weights = lat_weights(nlat).reshape(owners // 2, 1, rows)
    weights = jnp.asarray(np.tile(weights, (1, 2 * pops_here, 1)).reshape(owners // 2, lanes))
    onehot = (conn_block[..., None] == jnp.arange(kernels.shape[0], dtype=jnp.int32)).astype(F32)
    mixing = coupling[..., None] * jnp.einsum(
        "ijb,bn->ijn", onehot, kernels, precision=lax.Precision.HIGHEST
    )
    mixing = jnp.swapaxes(mixing, 0, 1)
    row = jnp.arange(rows, dtype=jnp.int32)
    flip = jnp.where(southern, row[::-1], row)[:, None] == row[None, :]
    flip = flip.astype(BF16)
    first_wave = (owner * owned + core * count).astype(jnp.int32)
    first = jnp.stack([first_wave, core * (count // 4)]).astype(jnp.int32)
    half = owners // 2
    poleward = [(o, o - 1) for o in range(1, half)] + [(o, o + 1) for o in range(half, owners - 1)]
    equatorward = [(o, o + 1) for o in range(half - 1)]
    equatorward += [(o, o - 1) for o in range(half + 1, owners)]
    over_equator = [(half - 1, half), (half, half - 1)]

    def one(lead, tail):
        return pl.BlockSpec((lead, 1) + tail, lambda i: (0, i, 0, 0))

    rates, carried = call(
        grid_rates_body,
        (shape(lons, pops_here, rows, cols), shape(lons, pops_here, rows, cols)),
        32,
        grid=(pops_here,),
        in_specs=[
            scalars(),
            whole(),
            pl.BlockSpec((1, lat_here, cols), lambda i: (i, 0, 0)),
            pl.BlockSpec((1, lat_here, cols), lambda i: (i, 0, 0)),
        ],
        out_specs=(one(lons, (rows, cols)), one(lons, (rows, cols))),
    )(params, flip, activity, drive)
    rates = lax.all_to_all(rates, "lon", 0, 0, tiled=True)
    carried = lax.all_to_all(carried, "lon", 0, 0, tiled=True)

    edge = shape(pops_here, nlon)
    fourier, polar, inner_edge = call(
        first_fourier_body,
        (shape(groups, count, lanes), edge, edge),
        32,
        in_specs=[whole(), whole()],
        out_specs=(whole(),) * 3,
    )(table, rates)

    def coupled(fourier):
        spectrum = lax.all_to_all(fourier, EVERYONE, 0, 0, tiled=True)
        tiles = -(-half_lat // 128)
        block = 4
        scratch = pltpu.VMEM((tiles, 2 * pops * count, 128), F32)
        synthesis = call(
            legendre_body,
            shape(groups, count, lanes),
            40,
            grid_spec=pltpu.PrefetchScalarGridSpec(
                num_scalar_prefetch=1,
                grid=(count // block,),
                in_specs=[
                    whole(),
                    whole(),
                    whole(),
                    pl.BlockSpec((block, half_lat, deg), lambda i, f: (f[1] + i, 0, 0)),
                ],
                out_specs=whole(),
                scratch_shapes=[scratch] * 4,
            ),
        )(first, spectrum, weights, mixing, basis)
        return lax.all_to_all(synthesis, EVERYONE, 0, 0, tiled=True)

    def lateral(rates, polar, inner_edge, *more):
        from_pole = lax.ppermute(inner_edge, OWNERS, equatorward)
        from_equator = lax.ppermute(polar, OWNERS, poleward)
        across = lax.ppermute(inner_edge, OWNERS, over_equator)
        return call(
            lateral_body,
            shape(pops_here, rows, nlon, dtype=F32),
            32,
            in_specs=[scalars()] + [whole()] * (4 + len(more)),
            out_specs=whole(),
        )(params, rates, from_pole, from_equator, across, *more)

    back = coupled(fourier)
    beside = lateral(rates, polar, inner_edge)
    turned_s = pltpu.VMEM((lanes, deg), BF16)
    fourier, rates, polar, inner_edge, inner = call(
        middle_body,
        (
            shape(groups, count, lanes),
            shape(lons, pops_here, rows, cols),
            edge,
            edge,
            shape(pops_here, rows, nlon, dtype=F32),
        ),
        48,
        in_specs=[scalars()] + [whole()] * 4,
        out_specs=(whole(),) * 5,
        scratch_shapes=[turned_s],
    )(params, table, back, beside, carried)
    back = coupled(fourier)
    beside = lateral(rates, polar, inner_edge, inner)
    inner = call(
        last_body,
        shape(lons, pops_here, rows, cols),
        48,
        in_specs=[whole()] * 3,
        out_specs=whole(),
        scratch_shapes=[turned_s],
    )(table, back, beside)
    inner = lax.all_to_all(inner, "lon", 0, 0, tiled=True)
    return call(
        grid_update_body,
        shape(*activity.shape, dtype=F32),
        32,
        grid=(pops_here,),
        in_specs=[
            scalars(),
            whole(),
            pl.BlockSpec((1, lat_here, cols), lambda i: (i, 0, 0)),
            pl.BlockSpec((1, lat_here, cols), lambda i: (i, 0, 0)),
            one(lons, (rows, cols)),
        ],
        out_specs=pl.BlockSpec((1, lat_here, cols), lambda i: (i, 0, 0)),
    )(params, flip, activity, drive, inner)


def with_halo(shard, sides, width):
    for axis, dim in sides:
        size, length = (lax.axis_size(axis), shard.shape[dim])
        up = [(i, (i + 1) % size) for i in range(size - 1)]
        down = [(j, i) for i, j in up]
        last = lax.slice_in_dim(shard, length - width, length, axis=dim)
        leading = lax.slice_in_dim(shard, 0, width, axis=dim)
        before = lax.ppermute(last, axis, up)
        after = lax.ppermute(leading, axis, down)
        shard = jnp.concatenate([before, shard, after], axis=dim)
    return shard


def plain_table(nlon, deg):
    longitude = jnp.arange(nlon, dtype=jnp.int32)
    wavenumber = jnp.arange(deg, dtype=jnp.int32)
    phase = longitude[:, None] * wavenumber[None, :] % nlon
    angle = phase.astype(jnp.float32) * (2.0 * math.pi / nlon)
    return jnp.stack([jnp.cos(angle), jnp.sin(angle)], axis=1).astype(jnp.bfloat16)


def to_owners(fourier):
    return lax.all_to_all(fourier, ("band", "lon"), split_axis=2, concat_axis=3, tiled=True)


def to_latitudes(synthesis):
    return lax.all_to_all(synthesis, ("band", "lon"), split_axis=3, concat_axis=2, tiled=True)


def by_arrays(activity, drive, basis, kernels, conn_block, coupling, rate_params):
    pop_here = activity.shape[0]
    owned_count = basis.shape[0]
    half_lat = basis.shape[1]
    deg = basis.shape[2]
    nlon = activity.shape[2] * lax.axis_size("lon")
    quarter = deg // 2
    owner_index = lax.axis_index("band") * lax.axis_size("lon") + lax.axis_index("lon")
    pop_first = lax.axis_index("pop") * pop_here
    params = lax.dynamic_slice_in_dim(rate_params, pop_first, pop_here, 1)
    gain_row, thresh, decay_row, lateral = (params[0], params[1], params[2], params[3])
    cos_sin = plain_table(nlon, deg)
    weights = jnp.asarray(lat_weights(2 * half_lat))
    wavenumber = owner_index * owned_count + jnp.arange(owned_count, dtype=jnp.int32)
    degree = jnp.arange(deg, dtype=jnp.int32)
    triangle = degree[None, :] >= wavenumber[:, None]
    slots = jnp.arange(2, dtype=jnp.int32)
    parity_pick = (slots[None, :] == (wavenumber % 2)[:, None])[None, None, :, :, None]
    every_wave = jnp.arange(deg, dtype=jnp.int32)
    amplitude = jnp.where(every_wave == 0, 1.0, 2.0).astype(jnp.bfloat16)
    coup_own = lax.dynamic_slice_in_dim(coupling, pop_first, pop_here, 0)
    block_own = lax.dynamic_slice_in_dim(conn_block, pop_first, pop_here, 0)
    onehot = (block_own[..., None] == jnp.arange(kernels.shape[0], dtype=jnp.int32)).astype(
        jnp.float32
    )
    mixing = coup_own[..., None] * jnp.einsum(
        "ijb,bn->ijn", onehot, kernels, precision=lax.Precision.HIGHEST
    )
    basis_split = basis.reshape(owned_count, half_lat, quarter, 2)
    drive_f32 = drive.astype(jnp.float32)
    activity_now = activity
    for step_index in range(STEPS):
        rates = jax.nn.sigmoid(
            gain_row[:, None, None] * (activity_now - thresh[:, None, None])
        ).astype(jnp.bfloat16)
        lat_rows = lax.all_to_all(rates, "lon", split_axis=1, concat_axis=2, tiled=True)
        fourier = jnp.einsum(
            "ijk,kcm->icmj", lat_rows, cos_sin, preferred_element_type=jnp.float32
        ).astype(jnp.bfloat16)
        spectrum = to_owners(fourier)
        northern = spectrum[..., :half_lat].astype(jnp.float32)
        southern = jnp.flip(spectrum[..., half_lat:], axis=3).astype(jnp.float32)
        even_part = (weights * (northern + southern)).astype(jnp.bfloat16)
        odd_part = (weights * (northern - southern)).astype(jnp.bfloat16)
        operand = jnp.where(parity_pick, even_part[:, :, :, None, :], odd_part[:, :, :, None, :])
        coeffs = jnp.einsum(
            "icmsj,mjqs->icmqs", operand, basis_split, preferred_element_type=jnp.float32
        )
        coeffs = coeffs.reshape(pop_here, 2, owned_count, deg)
        coeffs = jnp.where(triangle[None, None], coeffs, 0.0)
        gathered = lax.all_gather(coeffs.astype(jnp.bfloat16), "pop", axis=0, tiled=True).astype(
            coeffs.dtype
        )
        mixed_spec = jnp.sum(mixing[:, :, None, None, :] * gathered[None], axis=1).astype(
            jnp.bfloat16
        )
        degree_parts = jnp.einsum(
            "icmqs,mjqs->icmsj",
            mixed_spec.reshape(pop_here, 2, owned_count, quarter, 2),
            basis_split,
            preferred_element_type=jnp.float32,
        )
        same_parity = jnp.sum(jnp.where(parity_pick, degree_parts, 0.0), axis=3)
        other_parity = jnp.sum(jnp.where(parity_pick, 0.0, degree_parts), axis=3)
        synthesis = jnp.concatenate(
            [same_parity + other_parity, jnp.flip(same_parity - other_parity, axis=3)], axis=3
        ).astype(jnp.bfloat16)
        returned = to_latitudes(synthesis)
        scaled = returned * amplitude[None, None, :, None]
        synth_field = jnp.einsum(
            "icmj,kcm->ijk", scaled, cos_sin, preferred_element_type=jnp.float32
        ) * (1.0 / nlon)
        padded = with_halo(lat_rows, ((("band", "lon"), 1),), 1).astype(jnp.float32)
        rates_f32 = lat_rows.astype(jnp.float32)
        lateral_term = (
            jnp.roll(rates_f32, 1, axis=2)
            + jnp.roll(rates_f32, -1, axis=2)
            + padded[:, 2:, :]
            + padded[:, :-2, :]
            - 4.0 * rates_f32
        )
        coupled = synth_field + lateral[:, None, None] * lateral_term
        coupled_grid = lax.all_to_all(
            coupled.astype(jnp.bfloat16), "lon", split_axis=2, concat_axis=1, tiled=True
        ).astype(coupled.dtype)
        forcing = -decay_row[:, None, None] * activity_now + coupled_grid + drive_f32
        activity_now = activity_now + time_step * forcing
    return activity_now


def solution(mesh):
    bands, lons, cores = (mesh.shape[a] for a in ("band", "lon", "pop"))

    def local(activity, drive, basis, *rest):
        rows, owned = activity.shape[1] // lons, basis.shape[0]
        fits = (
            bands % 2 == 0
            and owned % (4 * cores) == 0
            and (owned // cores) % 8 == 0
            and rows % 16 == 0
            and activity.shape[2] % 128 == 0
            and 2 * activity.shape[0] * rows % 128 == 0
        )
        return (by_parts if fits else by_arrays)(activity, drive, basis, *rest)

    in_specs = (
        P(("subj", "pop"), "band", "lon"),
        P(("subj", "pop"), "band", "lon"),
        P(("subj", "band", "lon"), None, None),
        P(),
        P(),
        P("subj", None),
        P("subj", None),
    )
    out_specs = P(("subj", "pop"), "band", "lon")
    return jax.shard_map(local, mesh=mesh, in_specs=in_specs, out_specs=out_specs, check_vma=False)
```

```python
import functools
import math

import jax
import jax.numpy as jnp
import ml_dtypes
import numpy as np
from jax import lax
from jax.experimental import pallas as pl
from jax.experimental.pallas import tpu as pltpu
from jax.sharding import PartitionSpec as P

STEPS = 2
time_step = 0.5
F32 = jnp.float32
BF16 = jnp.bfloat16
OWNERS = ("band", "lon")
EVERYONE = ("band", "lon", "pop")
MIB = 1 << 20


def call(body, out_shape, vmem_mib, flops=0, nbytes=0, **kw):
    return pl.pallas_call(
        body,
        out_shape=out_shape,
        compiler_params=pltpu.CompilerParams(vmem_limit_bytes=vmem_mib * MIB),
        cost_estimate=pl.CostEstimate(flops=flops, bytes_accessed=nbytes, transcendentals=0),
        **kw,
    )


def whole():
    return pl.BlockSpec(memory_space=pltpu.VMEM)


def scalars():
    return pl.BlockSpec(memory_space=pltpu.SMEM)


def shape(*dims, dtype=BF16):
    return jax.ShapeDtypeStruct(dims, dtype)


def nt_dot(a, b):
    return lax.dot_general(a, b, (((1,), (1,)), ((), ())), preferred_element_type=F32)


def fourier_table(nlon, deg):
    phase = np.arange(deg, dtype=np.int64)[:, None] * np.arange(nlon, dtype=np.int64)[None, :] % nlon
    angle = phase.astype(np.float32) * np.float32(2.0 * math.pi / nlon)
    return np.stack([np.cos(angle), np.sin(angle)]).astype(ml_dtypes.bfloat16)


def lat_weights(nlat):
    row_index = np.arange(nlat // 2, dtype=np.float32)
    colatitude = np.float32(math.pi) * (4.0 * row_index + 3.0) / np.float32(4.0 * nlat + 2.0)
    return (np.float32(math.pi) * np.sin(colatitude) / np.float32(nlat)).astype(np.float32)


def here():
    bands, lons = lax.axis_size("band"), lax.axis_size("lon")
    band, lon = lax.axis_index("band"), lax.axis_index("lon")
    owner, half = band * lons + lon, bands * lons // 2
    at_equator = jnp.logical_or(owner == half - 1, owner == half)
    at_pole = jnp.logical_or(owner == 0, owner == 2 * half - 1)
    return lon, owner >= half, at_equator, at_pole


def in_wire_order(block):
    rows = block.shape[0]
    a = lax.broadcasted_iota(jnp.int32, (rows, rows), 0)
    b = lax.broadcasted_iota(jnp.int32, (rows, rows), 1)
    move = jnp.where(a == jnp.where(here()[1], rows - 1 - b, b), 1.0, 0.0).astype(BF16)
    return jnp.dot(move, block, preferred_element_type=F32)


def rate_of(params, i, u):
    return jax.nn.sigmoid(params[0, i] * (u - params[1, i])).astype(BF16)


def half_of(ref, lead, half, rows):
    return ref[lead, pl.ds(pl.multiple_of(half * rows, 16), rows), :]


def sent_rates_body(params, act, rates):
    first = lax.axis_index("pop") * act.shape[0]
    for i in range(act.shape[0]):
        rates[i] = in_wire_order(rate_of(params, first + i, act[i])).astype(BF16)


def own_half_body(params, table, act, drive, rates, sent, kept, part):
    pops, rows, cols = rates.shape
    first = lax.axis_index("pop") * pops
    lon = here()[0]
    for i in range(pops):
        decay = params[2, first + i]
        for half, out in ((1 - lon, sent), (lon, kept)):
            u = half_of(act, i, half, rows)
            d = half_of(drive, i, half, rows).astype(F32)
            c = ((1.0 - time_step * decay) * u + time_step * d).astype(BF16)
            out[i] = in_wire_order(c).astype(BF16)
        r = rate_of(params, first + i, half_of(act, i, lon, rows))
        rates[i] = in_wire_order(r).astype(BF16)
    block = part.shape[0] // 4
    columns = [pl.ds(pl.multiple_of(lon * cols, 128), cols)]
    flat = [rates[...].reshape(pops * rows, cols)]
    for b in range(4):
        part[b * block : (b + 1) * block] = joined_fourier(table, b * block, block, columns, flat)


def joined_fourier(table, first, block, columns, rates):
    parts = []
    for c in range(2):
        total = None
        for at, r in zip(columns, rates):
            term = nt_dot(table[c, first : first + block, at], r)
            total = term if total is None else total + term
        parts.append(total)
    return jnp.concatenate(parts, axis=1)


def put_fourier(table, columns, flat, rates, fourier, part=None):
    halves, pops, rows, cols = rates.shape
    groups, total, lanes = fourier.shape
    extra = halves * pops * cols // lanes
    count = total - extra
    pack = 4
    block = pack * count
    strips = [rates[h, i].astype(F32) for h in range(halves) for i in range(pops)]
    polar = jnp.concatenate([v[0:1] for v in strips], axis=0)
    inner = jnp.concatenate([v[rows - 1 : rows] for v in strips], axis=0)
    _, southern, _, _ = here()
    owner = lax.axis_index("band") * lax.axis_size("lon") + lax.axis_index("lon")
    poleward = jnp.where(southern, owner + 1, owner - 1)
    cores = lax.axis_size("pop")
    for b in range(groups // pack):
        joined = joined_fourier(table, b * block, block, columns, flat)
        if part is not None:
            joined = joined + part[b * block : (b + 1) * block]
        for g in range(pack):
            to = b * pack + g
            edge = jnp.where(poleward == to // cores, polar, inner)
            sums = joined[g * count : (g + 1) * count]
            fourier[to] = jnp.concatenate([sums, edge], axis=0).astype(BF16)


def fourier_of(table, rates, fourier):
    halves, pops, rows, cols = rates.shape
    columns = [slice(h * cols, (h + 1) * cols) for h in range(halves)]
    flat = [rates[h].reshape(pops * rows, cols) for h in range(halves)]
    put_fourier(table, columns, flat, rates, fourier)


def first_fourier_body(table, part, kept, got, fourier, rates):
    pops, rows, cols = got.shape
    lon = here()[0]
    rates[lon] = kept[...]
    rates[1 - lon] = got[...]
    columns = [pl.ds(pl.multiple_of((1 - lon) * cols, 128), cols)]
    put_fourier(table, columns, [got[...].reshape(pops * rows, cols)], rates, fourier, part)


def lateral_of(rates, half, halo):
    _, pops, rows, cols = rates.shape
    before, after = halo[0, half], halo[1, half]
    row = lax.broadcasted_iota(jnp.int32, (rows, cols), 0)
    lane = lax.broadcasted_iota(jnp.int32, (rows, cols), 1)
    terms = []
    for i in range(pops):
        r = rates[half, i].astype(F32)
        other = rates[1 - half, i].astype(F32)
        east = jnp.where(lane == 0, other[:, cols - 1 :], pltpu.roll(r, 1, 1))
        west = jnp.where(lane == cols - 1, other[:, :1], pltpu.roll(r, cols - 1, 1))
        up = jnp.where(row == 0, before[i : i + 1], pltpu.roll(r, 1, 0))
        down = jnp.where(row == rows - 1, after[i : i + 1], pltpu.roll(r, rows - 1, 0))
        terms.append(east + west + up + down - 4.0 * r)
    return terms


def legendre_body(
    spectrum, weight, mixing, basis, out, halo, held, arrived, even_s, odd_s, north_s, south_s
):
    groups, count, lanes = out.shape
    tiles = even_s.shape[0]
    _, half_lat, deg = basis.shape
    pops = mixing.shape[0]
    src = weight.shape[0]
    cores = groups // (2 * src)
    piece = half_lat // src
    slots = lanes // piece
    pops_here = slots // 2
    pad = tiles * 128 - half_lat
    block = 8
    owner = lax.axis_index("band") * lax.axis_size("lon") + lax.axis_index("lon")
    here_first = lax.axis_index("pop") * count
    first_wave = owner * basis.shape[0] + here_first

    def fetch(r):
        return pltpu.make_async_copy(basis.at[here_first + r], held.at[r], arrived.at[r])

    @pl.loop(0, count)
    def _(r):
        fetch(r).start()

    _, southern, _, at_pole = here()
    outward = jnp.where(southern, owner + 1, owner - 1)
    inward = jnp.where(southern, owner - 1, owner + 1)
    outward = jnp.where(at_pole, owner, outward)
    for side, neighbour in ((0, outward), (1, inward)):
        rows = spectrum[neighbour * cores + lax.axis_index("pop")].astype(F32)[count:]
        if side == 0:
            rows = jnp.where(at_pole, 0.0, rows)
        for h in range(halo.shape[1]):
            halo[side, h] = rows[h * halo.shape[2] : (h + 1) * halo.shape[2]]

    def rows_of(p, q):
        b = (q // pops_here) * pops + p * pops_here + q % pops_here
        return slice(b * count, (b + 1) * count)

    for p in range(cores):
        evens, odds = [], []
        for s in range(src):
            north = spectrum[s * cores + p].astype(F32)[:count]
            south = spectrum[(2 * src - 1 - s) * cores + p].astype(F32)[:count]
            w = weight[s : s + 1]
            evens.append((w * (north + south)).astype(BF16).astype(F32))
            odds.append((w * (north - south)).astype(BF16).astype(F32))
        for q in range(slots):
            for parts, scratch in ((evens, even_s), (odds, odd_s)):
                strips = [v[:, q * piece : (q + 1) * piece] for v in parts]
                if pad:
                    strips.append(jnp.zeros((count, pad), F32))
                joined = jnp.concatenate(strips, axis=1)
                for t in range(tiles):
                    scratch[t, rows_of(p, q), :] = joined[:, t * 128 : (t + 1) * 128]

    degree = lax.broadcasted_iota(jnp.int32, (2 * pops, deg), 1)

    @pl.loop(0, count // block)
    def _(step):
        for at in range(block):
            fetch(step * block + at).wait()
        for at in range(block):
            r = step * block + at
            m = first_wave + r
            rows = pl.ds(r, 2 * pops, stride=count)
            lhs = jnp.concatenate(
                [
                    jnp.concatenate([scratch[t, rows, :] for t in range(tiles)], axis=1)
                    for scratch in (even_s, odd_s)
                ],
                axis=0,
            )[:, :half_lat].astype(BF16)
            both = jnp.dot(lhs, held[r], preferred_element_type=F32)
            odd = ((degree - m) & 1) == 1
            coeffs = jnp.where(odd, both[2 * pops :], both[: 2 * pops])
            coeffs = jnp.where(degree >= m, coeffs, 0.0)
            mixed = []
            for c in range(2):
                total = None
                for j in range(pops):
                    term = mixing[j] * coeffs[c * pops + j : c * pops + j + 1]
                    total = term if total is None else total + term
                mixed.append(total)
            mixed = jnp.concatenate(mixed, axis=0)
            amplitude = jnp.where(m == 0, 1.0, 2.0)
            lhs2 = jnp.concatenate([mixed, jnp.where(odd, -mixed, mixed)], axis=0).astype(BF16)
            field = nt_dot(lhs2, held[r]) * amplitude
            if pad:
                field = jnp.concatenate([field, jnp.zeros((4 * pops, pad), F32)], axis=1)
            for t in range(tiles):
                north_s[t, rows, :] = field[: 2 * pops, t * 128 : (t + 1) * 128]
                south_s[t, rows, :] = field[2 * pops :, t * 128 : (t + 1) * 128]

    for scratch, south in ((north_s, False), (south_s, True)):
        for p in range(cores):
            wide = [
                jnp.concatenate(
                    [scratch[t, rows_of(p, q), :] for t in range(tiles)], axis=1
                )
                for q in range(slots)
            ]
            for s in range(src):
                to = (2 * src - 1 - s if south else s) * cores + p
                strips = [v[:, s * piece : (s + 1) * piece] for v in wide]
                out[to] = jnp.concatenate(strips, axis=1).astype(BF16)


def turned(spectrum, turned_s):
    groups = spectrum.shape[0]
    stacked = jnp.concatenate([spectrum[g].astype(F32) for g in range(groups)], axis=0)
    turned_s[...] = stacked.T.astype(BF16)


def synth_of(both, table, columns):
    half = both.shape[0] // 2
    total = None
    for c in range(2):
        term = jnp.dot(
            both[c * half : (c + 1) * half, :], table[c, :, columns], preferred_element_type=F32
        )
        total = term if total is None else total + term
    return total


def middle_body(
    params, table, spectrum, old, halo, kept, got, fourier, rates, inner, turned_s
):
    halves, pops, rows, cols = rates.shape
    first = lax.axis_index("pop") * pops
    turned(spectrum, turned_s)
    for h in range(halves):
        at = slice(h * cols, (h + 1) * cols)
        synth = synth_of(turned_s, table, at) * (time_step / (halves * cols))
        lateral = lateral_of(old, h, halo)
        for i in range(pops):
            v = synth[i * rows : (i + 1) * rows]
            v = v + (time_step * params[3, first + i]) * lateral[i]
            inner[i, :, at] = v
            u = jnp.where(here()[0] == h, kept[i], got[i]).astype(F32) + v
            rates[h, i] = rate_of(params, first + i, u)
    fourier_of(table, rates, fourier)


def put_inner(params, table, rates, halo, inner, both, half, out):
    pops, rows, cols = out.shape
    first = lax.axis_index("pop") * pops
    at = pl.ds(pl.multiple_of(half * cols, 128), cols)
    synth = synth_of(both, table, at) * (time_step / table.shape[2])
    lateral = lateral_of(rates, half, halo)
    for i in range(pops):
        v = synth[i * rows : (i + 1) * rows]
        v = v + (time_step * params[3, first + i]) * lateral[i]
        v = v + (1.0 - time_step * params[2, first + i]) * inner[i, :, at]
        out[i] = v.astype(BF16)


def sent_inner_body(params, table, spectrum, rates, halo, inner, out, both):
    turned(spectrum, both)
    put_inner(params, table, rates, halo, inner, both, 1 - here()[0], out)


def kept_inner_body(params, table, both, rates, halo, inner, out):
    put_inner(params, table, rates, halo, inner, both, here()[0], out)


def grid_update_body(params, act, drive, kept, got, out):
    i = lax.axis_index("pop") * pl.num_programs(0) + pl.program_id(0)
    keep = 1.0 - time_step * params[2, i]
    rows = kept.shape[1]
    lon = here()[0]
    for half, inner in ((lon, kept), (1 - lon, got)):
        d = time_step * half_of(drive, 0, half, rows).astype(F32)
        at = pl.ds(pl.multiple_of(half * rows, 16), rows)
        out[0, at, :] = keep * (keep * act[0, at, :] + d) + d + in_wire_order(inner[0])


def by_parts(activity, drive, basis, kernels, conn_block, coupling, rate_params):
    pops_here, lat_here, cols = activity.shape
    owned, half_lat, deg = basis.shape
    bands, lons, cores = (lax.axis_size(a) for a in ("band", "lon", "pop"))
    owners = bands * lons
    groups = owners * cores
    count = owned // cores
    rows = lat_here // lons
    nlat, nlon = bands * lat_here, lons * cols
    pops = pops_here * cores
    lanes = 2 * pops_here * rows
    band, lon, core = (lax.axis_index(a) for a in ("band", "lon", "pop"))
    owner = band * lons + lon
    table = jnp.asarray(fourier_table(nlon, deg))
    weights = lat_weights(nlat).reshape(owners // 2, 1, rows)
    weights = jnp.asarray(np.tile(weights, (1, 2 * pops_here, 1)).reshape(owners // 2, lanes))
    onehot = (conn_block[..., None] == jnp.arange(kernels.shape[0], dtype=jnp.int32)).astype(F32)
    mixing = coupling[..., None] * jnp.einsum(
        "ijb,bn->ijn", onehot, kernels, precision=lax.Precision.HIGHEST
    )
    mixing = jnp.swapaxes(mixing, 0, 1)
    swap = [(0, 1), (1, 0)]

    by_pop = pl.BlockSpec((1, rows, cols), lambda i: (i, 0, 0))
    on_grid = pl.BlockSpec((1, lat_here, cols), lambda i: (i, 0, 0))
    piece = shape(pops_here, rows, cols)
    wire = shape(groups, count, lanes)
    wire_edge = shape(groups, count + pops_here * nlon // lanes, lanes)
    ends = shape(2, lons, pops_here, cols, dtype=F32)
    both_halves = shape(lons, pops_here, rows, cols)
    state = shape(pops_here, rows, nlon, dtype=F32)

    sent = call(
        sent_rates_body,
        piece,
        60,
        grid=(1,),
        in_specs=[
            scalars(),
            pl.BlockSpec((pops_here, rows, cols), lambda i: (0, 1 - lax.axis_index("lon"), 0)),
        ],
        out_specs=pl.BlockSpec((pops_here, rows, cols), lambda i: (0, 0, 0)),
    )(rate_params, activity)
    got = lax.ppermute(sent, "lon", swap)
    kept, carried_sent, carried_kept, part = call(
        own_half_body,
        (piece,) * 3 + (shape(deg, lanes, dtype=F32),),
        24,
        2 * 10**9,
        10**7,
        in_specs=[scalars()] + [whole()] * 3,
        out_specs=(whole(),) * 4,
    )(rate_params, table, activity, drive)
    got, mixing = lax.optimization_barrier((got, mixing))
    fourier, rates = call(
        first_fourier_body,
        (wire_edge, both_halves),
        16,
        in_specs=[whole()] * 4,
        out_specs=(whole(),) * 2,
    )(table, part, kept, got)

    def coupled(fourier, *more):
        spectrum = lax.all_to_all(fourier, EVERYONE, 0, 0, tiled=True)
        spectrum, *more = lax.optimization_barrier((spectrum, *more))
        more = [lax.ppermute(v, "lon", swap) for v in more]
        tiles = -(-half_lat // 128)
        scratch = pltpu.VMEM((tiles, 2 * pops * count, 128), F32)
        synthesis, halo = call(
            legendre_body,
            (wire, ends),
            40,
            5 * 10**9,
            2 * 10**7,
            in_specs=[whole()] * 3 + [pl.BlockSpec(memory_space=pl.ANY)],
            out_specs=(whole(),) * 2,
            scratch_shapes=[
                pltpu.VMEM((count, half_lat, deg), BF16),
                pltpu.SemaphoreType.DMA((count,)),
            ]
            + [scratch] * 4,
        )(spectrum, weights, mixing, basis)
        synthesis, more = lax.optimization_barrier((synthesis, more))
        back = lax.all_to_all(synthesis, EVERYONE, 0, 0, tiled=True)
        return back, halo, more

    back, halo, (carried_got,) = coupled(fourier, carried_sent)
    both = shape(lanes, deg)
    fourier, rates, inner = call(
        middle_body,
        (wire_edge, both_halves, state),
        32,
        in_specs=[scalars()] + [whole()] * 6,
        out_specs=(whole(),) * 3,
        scratch_shapes=[pltpu.VMEM(both.shape, BF16)],
    )(rate_params, table, back, rates, halo, carried_kept, carried_got)
    back, halo, _ = coupled(fourier)
    sent, both = call(
        sent_inner_body,
        (piece, both),
        24,
        in_specs=[scalars()] + [whole()] * 5,
        out_specs=(whole(),) * 2,
    )(rate_params, table, back, rates, halo, inner)
    got = lax.ppermute(sent, "lon", swap)
    kept = call(
        kept_inner_body,
        piece,
        16,
        10**9,
        5 * 10**6,
        in_specs=[scalars()] + [whole()] * 5,
        out_specs=whole(),
    )(rate_params, table, both, rates, halo, inner)
    return call(
        grid_update_body,
        shape(*activity.shape, dtype=F32),
        24,
        grid=(pops_here,),
        in_specs=[scalars(), on_grid, on_grid, by_pop, by_pop],
        out_specs=on_grid,
    )(rate_params, activity, drive, kept, got)


def with_halo(shard, sides, width):
    for axis, dim in sides:
        size, length = (lax.axis_size(axis), shard.shape[dim])
        up = [(i, (i + 1) % size) for i in range(size - 1)]
        down = [(j, i) for i, j in up]
        last = lax.slice_in_dim(shard, length - width, length, axis=dim)
        leading = lax.slice_in_dim(shard, 0, width, axis=dim)
        before = lax.ppermute(last, axis, up)
        after = lax.ppermute(leading, axis, down)
        shard = jnp.concatenate([before, shard, after], axis=dim)
    return shard


def plain_table(nlon, deg):
    longitude = jnp.arange(nlon, dtype=jnp.int32)
    wavenumber = jnp.arange(deg, dtype=jnp.int32)
    phase = longitude[:, None] * wavenumber[None, :] % nlon
    angle = phase.astype(jnp.float32) * (2.0 * math.pi / nlon)
    return jnp.stack([jnp.cos(angle), jnp.sin(angle)], axis=1).astype(jnp.bfloat16)


def to_owners(fourier):
    return lax.all_to_all(fourier, ("band", "lon"), split_axis=2, concat_axis=3, tiled=True)


def to_latitudes(synthesis):
    return lax.all_to_all(synthesis, ("band", "lon"), split_axis=3, concat_axis=2, tiled=True)


def by_arrays(activity, drive, basis, kernels, conn_block, coupling, rate_params):
    pop_here = activity.shape[0]
    owned_count = basis.shape[0]
    half_lat = basis.shape[1]
    deg = basis.shape[2]
    nlon = activity.shape[2] * lax.axis_size("lon")
    quarter = deg // 2
    owner_index = lax.axis_index("band") * lax.axis_size("lon") + lax.axis_index("lon")
    pop_first = lax.axis_index("pop") * pop_here
    params = lax.dynamic_slice_in_dim(rate_params, pop_first, pop_here, 1)
    gain_row, thresh, decay_row, lateral = (params[0], params[1], params[2], params[3])
    cos_sin = plain_table(nlon, deg)
    weights = jnp.asarray(lat_weights(2 * half_lat))
    wavenumber = owner_index * owned_count + jnp.arange(owned_count, dtype=jnp.int32)
    degree = jnp.arange(deg, dtype=jnp.int32)
    triangle = degree[None, :] >= wavenumber[:, None]
    slots = jnp.arange(2, dtype=jnp.int32)
    parity_pick = (slots[None, :] == (wavenumber % 2)[:, None])[None, None, :, :, None]
    every_wave = jnp.arange(deg, dtype=jnp.int32)
    amplitude = jnp.where(every_wave == 0, 1.0, 2.0).astype(jnp.bfloat16)
    coup_own = lax.dynamic_slice_in_dim(coupling, pop_first, pop_here, 0)
    block_own = lax.dynamic_slice_in_dim(conn_block, pop_first, pop_here, 0)
    onehot = (block_own[..., None] == jnp.arange(kernels.shape[0], dtype=jnp.int32)).astype(
        jnp.float32
    )
    mixing = coup_own[..., None] * jnp.einsum(
        "ijb,bn->ijn", onehot, kernels, precision=lax.Precision.HIGHEST
    )
    basis_split = basis.reshape(owned_count, half_lat, quarter, 2)
    drive_f32 = drive.astype(jnp.float32)
    activity_now = activity
    for step_index in range(STEPS):
        rates = jax.nn.sigmoid(
            gain_row[:, None, None] * (activity_now - thresh[:, None, None])
        ).astype(jnp.bfloat16)
        lat_rows = lax.all_to_all(rates, "lon", split_axis=1, concat_axis=2, tiled=True)
        fourier = jnp.einsum(
            "ijk,kcm->icmj", lat_rows, cos_sin, preferred_element_type=jnp.float32
        ).astype(jnp.bfloat16)
        spectrum = to_owners(fourier)
        northern = spectrum[..., :half_lat].astype(jnp.float32)
        southern = jnp.flip(spectrum[..., half_lat:], axis=3).astype(jnp.float32)
        even_part = (weights * (northern + southern)).astype(jnp.bfloat16)
        odd_part = (weights * (northern - southern)).astype(jnp.bfloat16)
        operand = jnp.where(parity_pick, even_part[:, :, :, None, :], odd_part[:, :, :, None, :])
        coeffs = jnp.einsum(
            "icmsj,mjqs->icmqs", operand, basis_split, preferred_element_type=jnp.float32
        )
        coeffs = coeffs.reshape(pop_here, 2, owned_count, deg)
        coeffs = jnp.where(triangle[None, None], coeffs, 0.0)
        gathered = lax.all_gather(coeffs.astype(jnp.bfloat16), "pop", axis=0, tiled=True).astype(
            coeffs.dtype
        )
        mixed_spec = jnp.sum(mixing[:, :, None, None, :] * gathered[None], axis=1).astype(
            jnp.bfloat16
        )
        degree_parts = jnp.einsum(
            "icmqs,mjqs->icmsj",
            mixed_spec.reshape(pop_here, 2, owned_count, quarter, 2),
            basis_split,
            preferred_element_type=jnp.float32,
        )
        same_parity = jnp.sum(jnp.where(parity_pick, degree_parts, 0.0), axis=3)
        other_parity = jnp.sum(jnp.where(parity_pick, 0.0, degree_parts), axis=3)
        synthesis = jnp.concatenate(
            [same_parity + other_parity, jnp.flip(same_parity - other_parity, axis=3)], axis=3
        ).astype(jnp.bfloat16)
        returned = to_latitudes(synthesis)
        scaled = returned * amplitude[None, None, :, None]
        synth_field = jnp.einsum(
            "icmj,kcm->ijk", scaled, cos_sin, preferred_element_type=jnp.float32
        ) * (1.0 / nlon)
        padded = with_halo(lat_rows, ((("band", "lon"), 1),), 1).astype(jnp.float32)
        rates_f32 = lat_rows.astype(jnp.float32)
        lateral_term = (
            jnp.roll(rates_f32, 1, axis=2)
            + jnp.roll(rates_f32, -1, axis=2)
            + padded[:, 2:, :]
            + padded[:, :-2, :]
            - 4.0 * rates_f32
        )
        coupled = synth_field + lateral[:, None, None] * lateral_term
        coupled_grid = lax.all_to_all(
            coupled.astype(jnp.bfloat16), "lon", split_axis=2, concat_axis=1, tiled=True
        ).astype(coupled.dtype)
        forcing = -decay_row[:, None, None] * activity_now + coupled_grid + drive_f32
        activity_now = activity_now + time_step * forcing
    return activity_now


def solution(mesh):
    bands, lons, cores = (mesh.shape[a] for a in ("band", "lon", "pop"))

    def local(activity, drive, basis, *rest):
        rows, owned = activity.shape[1] // lons, basis.shape[0]
        fits = (
            bands % 2 == 0
            and lons == 2
            and bands * lons * cores % 4 == 0
            and owned % (8 * cores) == 0
            and rows % 16 == 0
            and activity.shape[2] % 128 == 0
            and 2 * activity.shape[0] * rows % 128 == 0
        )
        return (by_parts if fits else by_arrays)(activity, drive, basis, *rest)

    in_specs = (
        P(("subj", "pop"), "band", "lon"),
        P(("subj", "pop"), "band", "lon"),
        P(("subj", "band", "lon"), None, None),
        P(),
        P(),
        P("subj", None),
        P("subj", None),
    )
    out_specs = P(("subj", "pop"), "band", "lon")
    return jax.shard_map(local, mesh=mesh, in_specs=in_specs, out_specs=out_specs, check_vma=False)
```

```python
import functools
import math

import jax
import jax.numpy as jnp
import ml_dtypes
import numpy as np
from jax import lax
from jax.experimental import pallas as pl
from jax.experimental.pallas import tpu as pltpu
from jax.sharding import PartitionSpec as P

STEPS = 2
time_step = 0.5
F32 = jnp.float32
BF16 = jnp.bfloat16
OWNERS = ("band", "lon")
EVERYONE = ("band", "lon", "pop")
MIB = 1 << 20


def call(body, out_shape, vmem_mib, flops=0, nbytes=0, **kw):
    return pl.pallas_call(
        body,
        out_shape=out_shape,
        compiler_params=pltpu.CompilerParams(vmem_limit_bytes=vmem_mib * MIB),
        cost_estimate=pl.CostEstimate(flops=flops, bytes_accessed=nbytes, transcendentals=0),
        **kw,
    )


def whole():
    return pl.BlockSpec(memory_space=pltpu.VMEM)


def scalars():
    return pl.BlockSpec(memory_space=pltpu.SMEM)


def shape(*dims, dtype=BF16):
    return jax.ShapeDtypeStruct(dims, dtype)


def nt_dot(a, b):
    return lax.dot_general(a, b, (((1,), (1,)), ((), ())), preferred_element_type=F32)


def fourier_table(nlon, deg):
    phase = np.arange(deg, dtype=np.int64)[:, None] * np.arange(nlon, dtype=np.int64)[None, :] % nlon
    angle = phase.astype(np.float32) * np.float32(2.0 * math.pi / nlon)
    return np.stack([np.cos(angle), np.sin(angle)]).astype(ml_dtypes.bfloat16)


def lat_weights(nlat):
    row_index = np.arange(nlat // 2, dtype=np.float32)
    colatitude = np.float32(math.pi) * (4.0 * row_index + 3.0) / np.float32(4.0 * nlat + 2.0)
    return (np.float32(math.pi) * np.sin(colatitude) / np.float32(nlat)).astype(np.float32)


def here():
    bands, lons = lax.axis_size("band"), lax.axis_size("lon")
    band, lon = lax.axis_index("band"), lax.axis_index("lon")
    owner, half = band * lons + lon, bands * lons // 2
    at_equator = jnp.logical_or(owner == half - 1, owner == half)
    at_pole = jnp.logical_or(owner == 0, owner == 2 * half - 1)
    return lon, owner >= half, at_equator, at_pole


def in_wire_order(block):
    rows = block.shape[0]
    a = lax.broadcasted_iota(jnp.int32, (rows, rows), 0)
    b = lax.broadcasted_iota(jnp.int32, (rows, rows), 1)
    move = jnp.where(a == jnp.where(here()[1], rows - 1 - b, b), 1.0, 0.0).astype(BF16)
    return jnp.dot(move, block, preferred_element_type=F32)


def rate_of(params, i, u):
    return jax.nn.sigmoid(params[0, i] * (u - params[1, i])).astype(BF16)


def half_of(ref, lead, half, rows):
    return ref[lead, pl.ds(pl.multiple_of(half * rows, 16), rows), :]


def sent_rates_body(begin, params, act, rates):
    count = act.shape[0]
    pops = params.shape[1] // lax.axis_size("pop")
    first = lax.axis_index("pop") * pops + begin
    for i in range(count):
        rates[i] = in_wire_order(rate_of(params, first + i, act[i])).astype(BF16)


def own_half_body(params, table, act, drive, rates, sent, kept, part):
    pops, rows, cols = rates.shape
    first = lax.axis_index("pop") * pops
    lon = here()[0]
    for i in range(pops):
        decay = params[2, first + i]
        for half, out in ((1 - lon, sent), (lon, kept)):
            u = half_of(act, i, half, rows)
            d = half_of(drive, i, half, rows).astype(F32)
            c = ((1.0 - time_step * decay) * u + time_step * d).astype(BF16)
            out[i] = in_wire_order(c).astype(BF16)
        r = rate_of(params, first + i, half_of(act, i, lon, rows))
        rates[i] = in_wire_order(r).astype(BF16)
    block = part.shape[0] // 4
    columns = [pl.ds(pl.multiple_of(lon * cols, 128), cols)]
    flat = [rates[...].reshape(pops * rows, cols)]
    for b in range(4):
        part[b * block : (b + 1) * block] = joined_fourier(table, b * block, block, columns, flat)


def joined_fourier(table, first, block, columns, rates):
    parts = []
    for c in range(2):
        total = None
        for at, r in zip(columns, rates):
            term = nt_dot(table[c, first : first + block, at], r)
            total = term if total is None else total + term
        parts.append(total)
    return jnp.concatenate(parts, axis=1)


def edge_slots(pops, nlon, groups):
    return -(-pops * (nlon // 128) // groups)


def wire_rows(count, lanes, slots):
    return -(-(count * (lanes // 128) + 2 * slots) // 16) * 16


def packed(sums, extra, total):
    parts = [sums[:, t * 128 : (t + 1) * 128] for t in range(sums.shape[1] // 128)] + extra
    missing = total - sum(v.shape[0] for v in parts)
    if missing:
        parts.append(jnp.zeros((missing, 128), F32))
    return jnp.concatenate(parts, axis=0).astype(BF16)


def unpacked(block, count, lanes):
    block = block.astype(F32)
    parts = [block[t * count : (t + 1) * count] for t in range(lanes // 128)]
    return jnp.concatenate(parts, axis=1)


def put_fourier(table, columns, flat, rates, fourier, part=None):
    halves, pops, rows, cols = rates.shape
    groups, total, _ = fourier.shape
    lanes = 2 * pops * rows
    count = table.shape[1] // groups
    slots = edge_slots(pops, halves * cols, groups)
    pack = 4
    block = pack * count
    polar, inner = [], []
    for i in range(pops):
        for h in range(halves):
            strip = rates[h, i].astype(F32)
            for t in range(cols // 128):
                at = slice(t * 128, (t + 1) * 128)
                polar.append(strip[:1, at])
                inner.append(strip[rows - 1 :, at])
    nothing = [jnp.zeros((1, 128), F32)] * (slots * groups - len(polar))
    polar, inner = polar + nothing, inner + nothing
    for b in range(groups // pack):
        joined = joined_fourier(table, b * block, block, columns, flat)
        if part is not None:
            joined = joined + part[b * block : (b + 1) * block]
        for g in range(pack):
            to = b * pack + g
            at = slice(to * slots, (to + 1) * slots)
            sums = joined[g * count : (g + 1) * count]
            fourier[to] = packed(sums, polar[at] + inner[at], total)


def fourier_of(table, rates, fourier):
    halves, pops, rows, cols = rates.shape
    columns = [slice(h * cols, (h + 1) * cols) for h in range(halves)]
    flat = [rates[h].reshape(pops * rows, cols) for h in range(halves)]
    put_fourier(table, columns, flat, rates, fourier)


def first_fourier_body(table, part, kept, got, got_more, fourier, rates):
    some, _, cols = got.shape
    lon = here()[0]
    rates[lon] = kept[...]
    rates[1 - lon, :some] = got[...]
    rates[1 - lon, some:] = got_more[...]
    columns = [pl.ds(pl.multiple_of((1 - lon) * cols, 128), cols)]
    there = [v[...].reshape(-1, cols) for v in (got, got_more)]
    flat = [jnp.concatenate(there, axis=0)]
    put_fourier(table, columns, flat, rates, fourier, part)


def lateral_of(rates, half, halo, some=None):
    _, pops, rows, cols = rates.shape
    before, after = halo[0, half], halo[1, half]
    row = lax.broadcasted_iota(jnp.int32, (rows, cols), 0)
    lane = lax.broadcasted_iota(jnp.int32, (rows, cols), 1)
    terms = []
    for i in some or range(pops):
        r = rates[half, i].astype(F32)
        other = rates[1 - half, i].astype(F32)
        east = jnp.where(lane == 0, other[:, cols - 1 :], pltpu.roll(r, 1, 1))
        west = jnp.where(lane == cols - 1, other[:, :1], pltpu.roll(r, cols - 1, 1))
        up = jnp.where(row == 0, before[i : i + 1], pltpu.roll(r, 1, 0))
        down = jnp.where(row == rows - 1, after[i : i + 1], pltpu.roll(r, rows - 1, 0))
        terms.append(east + west + up + down - 4.0 * r)
    return terms


def legendre_body(
    nlon, spectrum, weight, mixing, basis, out, held, arrived, even_s, odd_s, north_s, south_s
):
    groups, total, _ = out.shape
    count = held.shape[0]
    lanes = weight.shape[1]
    tiles = even_s.shape[0]
    _, half_lat, deg = basis.shape
    pops = mixing.shape[0]
    src = weight.shape[0]
    cores = groups // (2 * src)
    piece = half_lat // src
    lots = lanes // piece
    pops_here = lots // 2
    slots = edge_slots(pops_here, nlon, groups)
    pad = tiles * 128 - half_lat
    block = 8
    owner = lax.axis_index("band") * lax.axis_size("lon") + lax.axis_index("lon")
    here_first = lax.axis_index("pop") * count
    first_wave = owner * basis.shape[0] + here_first

    def fetch(r):
        return pltpu.make_async_copy(basis.at[here_first + r], held.at[r], arrived.at[r])

    @pl.loop(0, count)
    def _(r):
        fetch(r).start()

    wide = lanes // 128 * count
    pieces = [spectrum[g].astype(F32)[wide:] for g in range(groups)]
    passed = []
    for to in range(2 * src):
        step = 1 if to < src else -1
        outward, inward = to - step, to + step
        crossing = to in (src - 1, src)
        for p in range(cores):
            if 0 <= outward < 2 * src:
                before = pieces[outward * cores + p][slots : 2 * slots]
            else:
                before = jnp.zeros((slots, 128), F32)
            after = pieces[inward * cores + p]
            after = after[slots : 2 * slots] if crossing else after[:slots]
            passed.append([before, after])

    def rows_of(p, q):
        b = (q // pops_here) * pops + p * pops_here + q % pops_here
        return slice(b * count, (b + 1) * count)

    for p in range(cores):
        evens, odds = [], []
        for s in range(src):
            north = unpacked(spectrum[s * cores + p], count, lanes)
            south = unpacked(spectrum[(2 * src - 1 - s) * cores + p], count, lanes)
            w = weight[s : s + 1]
            evens.append((w * (north + south)).astype(BF16).astype(F32))
            odds.append((w * (north - south)).astype(BF16).astype(F32))
        for q in range(lots):
            for parts, scratch in ((evens, even_s), (odds, odd_s)):
                strips = [v[:, q * piece : (q + 1) * piece] for v in parts]
                if pad:
                    strips.append(jnp.zeros((count, pad), F32))
                joined = jnp.concatenate(strips, axis=1)
                for t in range(tiles):
                    scratch[t, rows_of(p, q), :] = joined[:, t * 128 : (t + 1) * 128]

    degree = lax.broadcasted_iota(jnp.int32, (2 * pops, deg), 1)

    @pl.loop(0, count // block)
    def _(step):
        for at in range(block):
            fetch(step * block + at).wait()
        for at in range(block):
            r = step * block + at
            m = first_wave + r
            rows = pl.ds(r, 2 * pops, stride=count)
            lhs = jnp.concatenate(
                [
                    jnp.concatenate([scratch[t, rows, :] for t in range(tiles)], axis=1)
                    for scratch in (even_s, odd_s)
                ],
                axis=0,
            )[:, :half_lat].astype(BF16)
            both = jnp.dot(lhs, held[r], preferred_element_type=F32)
            odd = ((degree - m) & 1) == 1
            coeffs = jnp.where(odd, both[2 * pops :], both[: 2 * pops])
            coeffs = jnp.where(degree >= m, coeffs, 0.0)
            mixed = []
            for c in range(2):
                total = None
                for j in range(pops):
                    term = mixing[j] * coeffs[c * pops + j : c * pops + j + 1]
                    total = term if total is None else total + term
                mixed.append(total)
            mixed = jnp.concatenate(mixed, axis=0)
            amplitude = jnp.where(m == 0, 1.0, 2.0)
            lhs2 = jnp.concatenate([mixed, jnp.where(odd, -mixed, mixed)], axis=0).astype(BF16)
            field = nt_dot(lhs2, held[r]) * amplitude
            if pad:
                field = jnp.concatenate([field, jnp.zeros((4 * pops, pad), F32)], axis=1)
            for t in range(tiles):
                north_s[t, rows, :] = field[: 2 * pops, t * 128 : (t + 1) * 128]
                south_s[t, rows, :] = field[2 * pops :, t * 128 : (t + 1) * 128]

    for scratch, south in ((north_s, False), (south_s, True)):
        for p in range(cores):
            wide = [
                jnp.concatenate(
                    [scratch[t, rows_of(p, q), :] for t in range(tiles)], axis=1
                )
                for q in range(lots)
            ]
            for s in range(src):
                to = (2 * src - 1 - s if south else s) * cores + p
                strips = [v[:, s * piece : (s + 1) * piece] for v in wide]
                out[to] = packed(jnp.concatenate(strips, axis=1), passed[to], total)


def turned(spectrum, turned_s):
    groups = spectrum.shape[0]
    lanes, deg = turned_s.shape
    blocks = [unpacked(spectrum[g], deg // groups, lanes) for g in range(groups)]
    turned_s[...] = jnp.concatenate(blocks, axis=0).T.astype(BF16)


def put_ends(spectrum, turned_s, halo):
    groups = spectrum.shape[0]
    lanes, deg = turned_s.shape
    _, halves, pops, cols = halo.shape
    slots = edge_slots(pops, halves * cols, groups)
    wide = lanes // 128 * (deg // groups)
    pieces = [spectrum[g].astype(F32)[wide:] for g in range(groups)]
    per = cols // 128
    for side in range(2):
        for i in range(pops):
            for h in range(halves):
                for t in range(per):
                    at = (i * halves + h) * per + t
                    row = side * slots + at % slots
                    halo[side, h, i : i + 1, t * 128 : (t + 1) * 128] = pieces[at // slots][
                        row : row + 1
                    ]


def synth_of(both, table, columns, first=0, count=None):
    half = both.shape[0] // 2
    count = half if count is None else count
    total = None
    for c in range(2):
        term = jnp.dot(
            both[c * half + first : c * half + first + count, :],
            table[c, :, columns],
            preferred_element_type=F32,
        )
        total = term if total is None else total + term
    return total


def middle_body(
    params, table, spectrum, old, kept, got, fourier, rates, inner, turned_s, halo
):
    halves, pops, rows, cols = rates.shape
    first = lax.axis_index("pop") * pops
    turned(spectrum, turned_s)
    put_ends(spectrum, turned_s, halo)
    for h in range(halves):
        at = slice(h * cols, (h + 1) * cols)
        synth = synth_of(turned_s, table, at) * (time_step / (halves * cols))
        lateral = lateral_of(old, h, halo)
        for i in range(pops):
            v = synth[i * rows : (i + 1) * rows]
            v = v + (time_step * params[3, first + i]) * lateral[i]
            inner[i, :, at] = v
            u = jnp.where(here()[0] == h, kept[i], got[i]).astype(F32) + v
            rates[h, i] = rate_of(params, first + i, u)
    fourier_of(table, rates, fourier)


def put_inner(params, table, rates, halo, inner, both, half, some, out):
    _, pops, rows, cols = rates.shape
    first = lax.axis_index("pop") * pops
    at = pl.ds(pl.multiple_of(half * cols, 128), cols)
    synth = synth_of(both, table, at, some[0] * rows, len(some) * rows)
    synth = synth * (time_step / table.shape[2])
    lateral = lateral_of(rates, half, halo, some)
    for k, i in enumerate(some):
        v = synth[k * rows : (k + 1) * rows]
        v = v + (time_step * params[3, first + i]) * lateral[k]
        v = v + (1.0 - time_step * params[2, first + i]) * inner[i, :, at]
        out[k] = v.astype(BF16)


def sent_inner_body(some, params, table, spectrum, rates, inner, out, both, halo):
    turned(spectrum, both)
    put_ends(spectrum, both, halo)
    put_inner(params, table, rates, halo, inner, both, 1 - here()[0], some, out)


def more_inner_body(some, params, table, both, rates, halo, inner, out):
    put_inner(params, table, rates, halo, inner, both, 1 - here()[0], some, out)


def kept_inner_body(some, params, table, both, rates, halo, inner, out):
    put_inner(params, table, rates, halo, inner, both, here()[0], some, out)


def grid_update_body(begin, params, act, drive, kept, got, *refs):
    out = refs[-1]
    pops = begin + pl.num_programs(0) if begin else 2 * pl.num_programs(0)
    i = lax.axis_index("pop") * pops + begin + pl.program_id(0)
    keep = 1.0 - time_step * params[2, i]
    rows = kept.shape[1]
    lon = here()[0]
    for half, inner in ((lon, kept), (1 - lon, got)):
        d = time_step * half_of(drive, 0, half, rows).astype(F32)
        at = pl.ds(pl.multiple_of(half * rows, 16), rows)
        out[0, at, :] = keep * (keep * act[0, at, :] + d) + d + in_wire_order(inner[0])


def by_parts(activity, drive, basis, kernels, conn_block, coupling, rate_params):
    pops_here, lat_here, cols = activity.shape
    owned, half_lat, deg = basis.shape
    bands, lons, cores = (lax.axis_size(a) for a in ("band", "lon", "pop"))
    owners = bands * lons
    groups = owners * cores
    count = owned // cores
    rows = lat_here // lons
    nlat, nlon = bands * lat_here, lons * cols
    pops = pops_here * cores
    lanes = 2 * pops_here * rows
    band, lon, core = (lax.axis_index(a) for a in ("band", "lon", "pop"))
    owner = band * lons + lon
    table = jnp.asarray(fourier_table(nlon, deg))
    weights = lat_weights(nlat).reshape(owners // 2, 1, rows)
    weights = jnp.asarray(np.tile(weights, (1, 2 * pops_here, 1)).reshape(owners // 2, lanes))
    onehot = (conn_block[..., None] == jnp.arange(kernels.shape[0], dtype=jnp.int32)).astype(F32)
    mixing = coupling[..., None] * jnp.einsum(
        "ijb,bn->ijn", onehot, kernels, precision=lax.Precision.HIGHEST
    )
    mixing = jnp.swapaxes(mixing, 0, 1)
    swap = [(0, 1), (1, 0)]

    by_pop = pl.BlockSpec((1, rows, cols), lambda i: (i, 0, 0))
    on_grid = pl.BlockSpec((1, lat_here, cols), lambda i: (i, 0, 0))
    piece = shape(pops_here, rows, cols)
    wire = shape(groups, wire_rows(count, lanes, edge_slots(pops_here, nlon, groups)), 128)
    ends = shape(2, lons, pops_here, cols, dtype=F32)
    both_halves = shape(lons, pops_here, rows, cols)
    state = shape(pops_here, rows, nlon, dtype=F32)

    some = pops_here // 2
    pairs = (list(range(some)), list(range(some, pops_here)))
    got = []
    for k, pair in enumerate(pairs):
        sent = call(
            functools.partial(sent_rates_body, pair[0]),
            shape(some, rows, cols),
            60,
            grid=(1,),
            in_specs=[
                scalars(),
                pl.BlockSpec((some, rows, cols), lambda i, k=k: (k, 1 - lax.axis_index("lon"), 0)),
            ],
            out_specs=pl.BlockSpec((some, rows, cols), lambda i: (0, 0, 0)),
        )(rate_params, activity)
        got.append(lax.ppermute(sent, "lon", swap))
    kept, carried_sent, carried_kept, part = call(
        own_half_body,
        (piece,) * 3 + (shape(deg, lanes, dtype=F32),),
        24,
        2 * 10**9,
        10**7,
        in_specs=[scalars()] + [whole()] * 3,
        out_specs=(whole(),) * 4,
    )(rate_params, table, activity, drive)
    *got, mixing = lax.optimization_barrier((*got, mixing))
    fourier, rates = call(
        first_fourier_body,
        (wire, both_halves),
        16,
        in_specs=[whole()] * 5,
        out_specs=(whole(),) * 2,
    )(table, part, kept, *got)

    def coupled(fourier, *more):
        spectrum = lax.all_to_all(fourier, EVERYONE, 0, 0, tiled=True)
        spectrum, *more = lax.optimization_barrier((spectrum, *more))
        more = [lax.ppermute(v, "lon", swap) for v in more]
        tiles = -(-half_lat // 128)
        scratch = pltpu.VMEM((tiles, 2 * pops * count, 128), F32)
        synthesis = call(
            functools.partial(legendre_body, nlon),
            wire,
            40,
            5 * 10**9,
            2 * 10**7,
            in_specs=[whole()] * 3 + [pl.BlockSpec(memory_space=pl.ANY)],
            out_specs=whole(),
            scratch_shapes=[
                pltpu.VMEM((count, half_lat, deg), BF16),
                pltpu.SemaphoreType.DMA((count,)),
            ]
            + [scratch] * 4,
        )(spectrum, weights, mixing, basis)
        synthesis, more = lax.optimization_barrier((synthesis, more))
        back = lax.all_to_all(synthesis, EVERYONE, 0, 0, tiled=True)
        return back, more

    back, (carried_got,) = coupled(fourier, carried_sent)
    both = shape(lanes, deg)
    fourier, rates, inner = call(
        middle_body,
        (wire, both_halves, state),
        32,
        in_specs=[scalars()] + [whole()] * 5,
        out_specs=(whole(),) * 3,
        scratch_shapes=[pltpu.VMEM(both.shape, BF16), pltpu.VMEM(ends.shape, F32)],
    )(rate_params, table, back, rates, carried_kept, carried_got)
    back, _ = coupled(fourier)
    sent, both, halo = call(
        functools.partial(sent_inner_body, pairs[0]),
        (shape(some, rows, cols), both, ends),
        24,
        in_specs=[scalars()] + [whole()] * 4,
        out_specs=(whole(),) * 3,
    )(rate_params, table, back, rates, inner)

    def inner_of(body, some, count):
        return call(
            functools.partial(body, some),
            shape(count, rows, cols),
            16,
            10**9,
            5 * 10**6,
            in_specs=[scalars()] + [whole()] * 5,
            out_specs=whole(),
        )(rate_params, table, both, rates, halo, inner)

    got = [lax.ppermute(sent, "lon", swap)]
    got.append(lax.ppermute(inner_of(more_inner_body, pairs[1], len(pairs[1])), "lon", swap))
    kept = inner_of(kept_inner_body, pairs[0] + pairs[1], pops_here)
    out = None
    for pair, there in zip(pairs, got):
        begin = pair[0]

        def on(tail, begin=begin):
            return pl.BlockSpec((1,) + tail, lambda i: (begin + i, 0, 0))

        earlier = [] if out is None else [out]
        out = call(
            functools.partial(grid_update_body, begin),
            shape(*activity.shape, dtype=F32),
            24,
            10**7,
            4 * 10**6,
            grid=(len(pair),),
            in_specs=[
                scalars(),
                on((lat_here, cols)),
                on((lat_here, cols)),
                on((rows, cols)),
                by_pop,
            ]
            + [pl.BlockSpec(memory_space=pl.ANY)] * len(earlier),
            out_specs=on((lat_here, cols)),
            input_output_aliases={5: 0} if earlier else {},
        )(rate_params, activity, drive, kept, there, *earlier)
    return out


def with_halo(shard, sides, width):
    for axis, dim in sides:
        size, length = (lax.axis_size(axis), shard.shape[dim])
        up = [(i, (i + 1) % size) for i in range(size - 1)]
        down = [(j, i) for i, j in up]
        last = lax.slice_in_dim(shard, length - width, length, axis=dim)
        leading = lax.slice_in_dim(shard, 0, width, axis=dim)
        before = lax.ppermute(last, axis, up)
        after = lax.ppermute(leading, axis, down)
        shard = jnp.concatenate([before, shard, after], axis=dim)
    return shard


def plain_table(nlon, deg):
    longitude = jnp.arange(nlon, dtype=jnp.int32)
    wavenumber = jnp.arange(deg, dtype=jnp.int32)
    phase = longitude[:, None] * wavenumber[None, :] % nlon
    angle = phase.astype(jnp.float32) * (2.0 * math.pi / nlon)
    return jnp.stack([jnp.cos(angle), jnp.sin(angle)], axis=1).astype(jnp.bfloat16)


def to_owners(fourier):
    return lax.all_to_all(fourier, ("band", "lon"), split_axis=2, concat_axis=3, tiled=True)


def to_latitudes(synthesis):
    return lax.all_to_all(synthesis, ("band", "lon"), split_axis=3, concat_axis=2, tiled=True)


def by_arrays(activity, drive, basis, kernels, conn_block, coupling, rate_params):
    pop_here = activity.shape[0]
    owned_count = basis.shape[0]
    half_lat = basis.shape[1]
    deg = basis.shape[2]
    nlon = activity.shape[2] * lax.axis_size("lon")
    quarter = deg // 2
    owner_index = lax.axis_index("band") * lax.axis_size("lon") + lax.axis_index("lon")
    pop_first = lax.axis_index("pop") * pop_here
    params = lax.dynamic_slice_in_dim(rate_params, pop_first, pop_here, 1)
    gain_row, thresh, decay_row, lateral = (params[0], params[1], params[2], params[3])
    cos_sin = plain_table(nlon, deg)
    weights = jnp.asarray(lat_weights(2 * half_lat))
    wavenumber = owner_index * owned_count + jnp.arange(owned_count, dtype=jnp.int32)
    degree = jnp.arange(deg, dtype=jnp.int32)
    triangle = degree[None, :] >= wavenumber[:, None]
    slots = jnp.arange(2, dtype=jnp.int32)
    parity_pick = (slots[None, :] == (wavenumber % 2)[:, None])[None, None, :, :, None]
    every_wave = jnp.arange(deg, dtype=jnp.int32)
    amplitude = jnp.where(every_wave == 0, 1.0, 2.0).astype(jnp.bfloat16)
    coup_own = lax.dynamic_slice_in_dim(coupling, pop_first, pop_here, 0)
    block_own = lax.dynamic_slice_in_dim(conn_block, pop_first, pop_here, 0)
    onehot = (block_own[..., None] == jnp.arange(kernels.shape[0], dtype=jnp.int32)).astype(
        jnp.float32
    )
    mixing = coup_own[..., None] * jnp.einsum(
        "ijb,bn->ijn", onehot, kernels, precision=lax.Precision.HIGHEST
    )
    basis_split = basis.reshape(owned_count, half_lat, quarter, 2)
    drive_f32 = drive.astype(jnp.float32)
    activity_now = activity
    for step_index in range(STEPS):
        rates = jax.nn.sigmoid(
            gain_row[:, None, None] * (activity_now - thresh[:, None, None])
        ).astype(jnp.bfloat16)
        lat_rows = lax.all_to_all(rates, "lon", split_axis=1, concat_axis=2, tiled=True)
        fourier = jnp.einsum(
            "ijk,kcm->icmj", lat_rows, cos_sin, preferred_element_type=jnp.float32
        ).astype(jnp.bfloat16)
        spectrum = to_owners(fourier)
        northern = spectrum[..., :half_lat].astype(jnp.float32)
        southern = jnp.flip(spectrum[..., half_lat:], axis=3).astype(jnp.float32)
        even_part = (weights * (northern + southern)).astype(jnp.bfloat16)
        odd_part = (weights * (northern - southern)).astype(jnp.bfloat16)
        operand = jnp.where(parity_pick, even_part[:, :, :, None, :], odd_part[:, :, :, None, :])
        coeffs = jnp.einsum(
            "icmsj,mjqs->icmqs", operand, basis_split, preferred_element_type=jnp.float32
        )
        coeffs = coeffs.reshape(pop_here, 2, owned_count, deg)
        coeffs = jnp.where(triangle[None, None], coeffs, 0.0)
        gathered = lax.all_gather(coeffs.astype(jnp.bfloat16), "pop", axis=0, tiled=True).astype(
            coeffs.dtype
        )
        mixed_spec = jnp.sum(mixing[:, :, None, None, :] * gathered[None], axis=1).astype(
            jnp.bfloat16
        )
        degree_parts = jnp.einsum(
            "icmqs,mjqs->icmsj",
            mixed_spec.reshape(pop_here, 2, owned_count, quarter, 2),
            basis_split,
            preferred_element_type=jnp.float32,
        )
        same_parity = jnp.sum(jnp.where(parity_pick, degree_parts, 0.0), axis=3)
        other_parity = jnp.sum(jnp.where(parity_pick, 0.0, degree_parts), axis=3)
        synthesis = jnp.concatenate(
            [same_parity + other_parity, jnp.flip(same_parity - other_parity, axis=3)], axis=3
        ).astype(jnp.bfloat16)
        returned = to_latitudes(synthesis)
        scaled = returned * amplitude[None, None, :, None]
        synth_field = jnp.einsum(
            "icmj,kcm->ijk", scaled, cos_sin, preferred_element_type=jnp.float32
        ) * (1.0 / nlon)
        padded = with_halo(lat_rows, ((("band", "lon"), 1),), 1).astype(jnp.float32)
        rates_f32 = lat_rows.astype(jnp.float32)
        lateral_term = (
            jnp.roll(rates_f32, 1, axis=2)
            + jnp.roll(rates_f32, -1, axis=2)
            + padded[:, 2:, :]
            + padded[:, :-2, :]
            - 4.0 * rates_f32
        )
        coupled = synth_field + lateral[:, None, None] * lateral_term
        coupled_grid = lax.all_to_all(
            coupled.astype(jnp.bfloat16), "lon", split_axis=2, concat_axis=1, tiled=True
        ).astype(coupled.dtype)
        forcing = -decay_row[:, None, None] * activity_now + coupled_grid + drive_f32
        activity_now = activity_now + time_step * forcing
    return activity_now


def solution(mesh):
    bands, lons, cores = (mesh.shape[a] for a in ("band", "lon", "pop"))

    def local(activity, drive, basis, *rest):
        rows, owned = activity.shape[1] // lons, basis.shape[0]
        fits = (
            bands % 2 == 0
            and activity.shape[0] % 2 == 0
            and lons == 2
            and bands * lons * cores % 4 == 0
            and owned % (8 * cores) == 0
            and rows % 16 == 0
            and activity.shape[2] % 128 == 0
            and 2 * activity.shape[0] * rows % 128 == 0
        )
        return (by_parts if fits else by_arrays)(activity, drive, basis, *rest)

    in_specs = (
        P(("subj", "pop"), "band", "lon"),
        P(("subj", "pop"), "band", "lon"),
        P(("subj", "band", "lon"), None, None),
        P(),
        P(),
        P("subj", None),
        P("subj", None),
    )
    out_specs = P(("subj", "pop"), "band", "lon")
    return jax.shard_map(local, mesh=mesh, in_specs=in_specs, out_specs=out_specs, check_vma=False)
```

```python
import functools
import math

import jax
import jax.numpy as jnp
import ml_dtypes
import numpy as np
from jax import lax
from jax.experimental import pallas as pl
from jax.experimental.pallas import tpu as pltpu
from jax.sharding import PartitionSpec as P

STEPS = 2
time_step = 0.5
F32 = jnp.float32
BF16 = jnp.bfloat16
OWNERS = ("band", "lon")
EVERYONE = ("band", "lon", "pop")
MIB = 1 << 20


def call(body, out_shape, vmem_mib, flops=0, nbytes=0, **kw):
    return pl.pallas_call(
        body,
        out_shape=out_shape,
        compiler_params=pltpu.CompilerParams(vmem_limit_bytes=vmem_mib * MIB),
        cost_estimate=pl.CostEstimate(flops=flops, bytes_accessed=nbytes, transcendentals=0),
        **kw,
    )


def whole():
    return pl.BlockSpec(memory_space=pltpu.VMEM)


def scalars():
    return pl.BlockSpec(memory_space=pltpu.SMEM)


def shape(*dims, dtype=BF16):
    return jax.ShapeDtypeStruct(dims, dtype)


def nt_dot(a, b):
    return lax.dot_general(a, b, (((1,), (1,)), ((), ())), preferred_element_type=F32)


def fourier_table(nlon, owners, owned):
    wave = np.arange(owners * owned, dtype=np.int64).reshape(-1, 2).T.reshape(-1)
    phase = wave[:, None] * np.arange(nlon // 2, dtype=np.int64)[None, :] % nlon
    angle = phase.astype(np.float32) * np.float32(2.0 * math.pi / nlon)
    table = np.stack([np.cos(angle), np.sin(angle)]).astype(ml_dtypes.bfloat16)
    return table.reshape(2, 2, -1, nlon // 2)


def lat_weights(nlat):
    row_index = np.arange(nlat // 2, dtype=np.float32)
    colatitude = np.float32(math.pi) * (4.0 * row_index + 3.0) / np.float32(4.0 * nlat + 2.0)
    return (np.float32(math.pi) * np.sin(colatitude) / np.float32(nlat)).astype(np.float32)


def here():
    bands, lons = lax.axis_size("band"), lax.axis_size("lon")
    band, lon = lax.axis_index("band"), lax.axis_index("lon")
    owner, half = band * lons + lon, bands * lons // 2
    at_equator = jnp.logical_or(owner == half - 1, owner == half)
    at_pole = jnp.logical_or(owner == 0, owner == 2 * half - 1)
    return lon, owner >= half, at_equator, at_pole


def in_wire_order(block):
    rows = block.shape[0]
    a = lax.broadcasted_iota(jnp.int32, (rows, rows), 0)
    b = lax.broadcasted_iota(jnp.int32, (rows, rows), 1)
    move = jnp.where(a == jnp.where(here()[1], rows - 1 - b, b), 1.0, 0.0).astype(BF16)
    return jnp.dot(move, block, preferred_element_type=F32)


def rate_of(params, i, u):
    return jax.nn.sigmoid(params[0, i] * (u - params[1, i])).astype(BF16)


def half_of(ref, lead, half, rows):
    return ref[lead, pl.ds(pl.multiple_of(half * rows, 16), rows), :]


def sent_rates_body(begin, params, act, rates):
    count = act.shape[0]
    pops = params.shape[1] // lax.axis_size("pop")
    first = lax.axis_index("pop") * pops + begin
    for i in range(count):
        rates[i] = in_wire_order(rate_of(params, first + i, act[i])).astype(BF16)


def own_half_body(params, act, drive, rates, sent, kept):
    pops, rows, cols = rates.shape
    first = lax.axis_index("pop") * pops
    lon = here()[0]
    for i in range(pops):
        decay = params[2, first + i]
        for half, out in ((1 - lon, sent), (lon, kept)):
            u = half_of(act, i, half, rows)
            d = half_of(drive, i, half, rows).astype(F32)
            c = ((1.0 - time_step * decay) * u + time_step * d).astype(BF16)
            out[i] = in_wire_order(c).astype(BF16)
        r = rate_of(params, first + i, half_of(act, i, lon, rows))
        rates[i] = in_wire_order(r).astype(BF16)


def edge_slots(pops, nlon, groups):
    return -(-pops * (nlon // 128) // groups)


def wire_rows(count, lanes, slots):
    return -(-(count * (lanes // 128) + 2 * slots) // 16) * 16


def packed(sums, extra, total):
    parts = [sums[:, t * 128 : (t + 1) * 128] for t in range(sums.shape[1] // 128)] + extra
    missing = total - sum(v.shape[0] for v in parts)
    if missing:
        parts.append(jnp.zeros((missing, 128), F32))
    return jnp.concatenate(parts, axis=0).astype(BF16)


def unpacked(block, count, lanes):
    block = block.astype(F32)
    parts = [block[t * count : (t + 1) * count] for t in range(lanes // 128)]
    return jnp.concatenate(parts, axis=1)


def put_fourier(table, rates, fourier):
    halves, pops, rows, cols = rates.shape
    groups, total, _ = fourier.shape
    lanes = 2 * pops * rows
    waves = table.shape[2]
    count = 2 * waves // groups
    slots = edge_slots(pops, halves * cols, groups)
    polar, inner = [], []
    for i in range(pops):
        for h in range(halves):
            strip = rates[h, i].astype(F32)
            for t in range(cols // 128):
                at = slice(t * 128, (t + 1) * 128)
                polar.append(strip[:1, at])
                inner.append(strip[rows - 1 :, at])
    nothing = [jnp.zeros((1, 128), F32)] * (slots * groups - len(polar))
    polar, inner = polar + nothing, inner + nothing
    one, two = rates[0].astype(F32), rates[1].astype(F32)
    pack = groups // 4
    block = pack * count
    for p, mix in enumerate((one + two - 1.0, one - two)):
        flat = mix.astype(BF16).reshape(pops * rows, cols)
        for b in range(waves // block):
            parts = []
            for c in range(2):
                t = table[c, p, b * block : (b + 1) * block]
                sums = nt_dot(t, flat)
                if p == 0:
                    sums = sums + jnp.sum(t.astype(F32), axis=1, keepdims=True)
                parts.append(sums)
            joined = jnp.concatenate(parts, axis=1)
            for k in range(pack):
                to = (b * pack + k) * 2 + p
                at = slice(to * slots, (to + 1) * slots)
                sums = joined[k * count : (k + 1) * count]
                fourier[to] = packed(sums, polar[at] + inner[at], total)


def first_fourier_body(table, kept, got, got_more, fourier, rates):
    some = got.shape[0]
    lon = here()[0]
    rates[lon] = kept[...]
    rates[1 - lon, :some] = got[...]
    rates[1 - lon, some:] = got_more[...]
    put_fourier(table, rates, fourier)


def lateral_of(rates, half, halo, some=None):
    _, pops, rows, cols = rates.shape
    before, after = halo[0, half], halo[1, half]
    row = lax.broadcasted_iota(jnp.int32, (rows, cols), 0)
    lane = lax.broadcasted_iota(jnp.int32, (rows, cols), 1)
    terms = []
    for i in some or range(pops):
        r = rates[half, i].astype(F32)
        other = rates[1 - half, i].astype(F32)
        east = jnp.where(lane == 0, other[:, cols - 1 :], pltpu.roll(r, 1, 1))
        west = jnp.where(lane == cols - 1, other[:, :1], pltpu.roll(r, cols - 1, 1))
        up = jnp.where(row == 0, before[i : i + 1], pltpu.roll(r, 1, 0))
        down = jnp.where(row == rows - 1, after[i : i + 1], pltpu.roll(r, rows - 1, 0))
        terms.append(east + west + up + down - 4.0 * r)
    return terms


def legendre_body(
    nlon, spectrum, weight, mixing, basis, out, held, arrived, even_s, odd_s, north_s, south_s
):
    groups, total, _ = out.shape
    count = held.shape[0]
    lanes = weight.shape[1]
    tiles = even_s.shape[0]
    _, half_lat, deg = basis.shape
    pops = mixing.shape[0]
    src = weight.shape[0]
    cores = groups // (2 * src)
    piece = half_lat // src
    lots = lanes // piece
    pops_here = lots // 2
    slots = edge_slots(pops_here, nlon, groups)
    pad = tiles * 128 - half_lat
    block = 8
    owner = lax.axis_index("band") * lax.axis_size("lon") + lax.axis_index("lon")
    core = lax.axis_index("pop")
    first_wave = owner * basis.shape[0] + core

    def fetch(r):
        return pltpu.make_async_copy(basis.at[cores * r + core], held.at[r], arrived.at[r])

    @pl.loop(0, count)
    def _(r):
        fetch(r).start()

    wide = lanes // 128 * count
    pieces = [spectrum[g].astype(F32)[wide:] for g in range(groups)]
    passed = []
    for to in range(2 * src):
        step = 1 if to < src else -1
        outward, inward = to - step, to + step
        crossing = to in (src - 1, src)
        for p in range(cores):
            if 0 <= outward < 2 * src:
                before = pieces[outward * cores + p][slots : 2 * slots]
            else:
                before = jnp.zeros((slots, 128), F32)
            after = pieces[inward * cores + p]
            after = after[slots : 2 * slots] if crossing else after[:slots]
            passed.append([before, after])

    def rows_of(p, q):
        b = (q // pops_here) * pops + p * pops_here + q % pops_here
        return slice(b * count, (b + 1) * count)

    for p in range(cores):
        evens, odds = [], []
        for s in range(src):
            north = unpacked(spectrum[s * cores + p], count, lanes)
            south = unpacked(spectrum[(2 * src - 1 - s) * cores + p], count, lanes)
            w = weight[s : s + 1]
            evens.append((w * (north + south)).astype(BF16).astype(F32))
            odds.append((w * (north - south)).astype(BF16).astype(F32))
        for q in range(lots):
            for parts, scratch in ((evens, even_s), (odds, odd_s)):
                strips = [v[:, q * piece : (q + 1) * piece] for v in parts]
                if pad:
                    strips.append(jnp.zeros((count, pad), F32))
                joined = jnp.concatenate(strips, axis=1)
                for t in range(tiles):
                    scratch[t, rows_of(p, q), :] = joined[:, t * 128 : (t + 1) * 128]

    degree = lax.broadcasted_iota(jnp.int32, (2 * pops, deg), 1)

    @pl.loop(0, count // block)
    def _(step):
        for at in range(block):
            fetch(step * block + at).wait()
        for at in range(block):
            r = step * block + at
            m = first_wave + cores * r
            rows = pl.ds(r, 2 * pops, stride=count)
            lhs = jnp.concatenate(
                [
                    jnp.concatenate([scratch[t, rows, :] for t in range(tiles)], axis=1)
                    for scratch in (even_s, odd_s)
                ],
                axis=0,
            )[:, :half_lat].astype(BF16)
            both = jnp.dot(lhs, held[r], preferred_element_type=F32)
            odd = ((degree - m) & 1) == 1
            coeffs = jnp.where(odd, both[2 * pops :], both[: 2 * pops])
            coeffs = jnp.where(degree >= m, coeffs, 0.0)
            mixed = []
            for c in range(2):
                total = None
                for j in range(pops):
                    term = mixing[j] * coeffs[c * pops + j : c * pops + j + 1]
                    total = term if total is None else total + term
                mixed.append(total)
            mixed = jnp.concatenate(mixed, axis=0)
            amplitude = jnp.where(m == 0, 1.0, 2.0)
            lhs2 = jnp.concatenate([mixed, jnp.where(odd, -mixed, mixed)], axis=0).astype(BF16)
            field = nt_dot(lhs2, held[r]) * amplitude
            if pad:
                field = jnp.concatenate([field, jnp.zeros((4 * pops, pad), F32)], axis=1)
            for t in range(tiles):
                north_s[t, rows, :] = field[: 2 * pops, t * 128 : (t + 1) * 128]
                south_s[t, rows, :] = field[2 * pops :, t * 128 : (t + 1) * 128]

    for scratch, south in ((north_s, False), (south_s, True)):
        for p in range(cores):
            wide = [
                jnp.concatenate(
                    [scratch[t, rows_of(p, q), :] for t in range(tiles)], axis=1
                )
                for q in range(lots)
            ]
            for s in range(src):
                to = (2 * src - 1 - s if south else s) * cores + p
                strips = [v[:, s * piece : (s + 1) * piece] for v in wide]
                out[to] = packed(jnp.concatenate(strips, axis=1), passed[to], total)


def turned(spectrum, turned_s):
    groups = spectrum.shape[0]
    lanes, deg = turned_s.shape
    order = list(range(0, groups, 2)) + list(range(1, groups, 2))
    blocks = [unpacked(spectrum[g], deg // groups, lanes) for g in order]
    turned_s[...] = jnp.concatenate(blocks, axis=0).T.astype(BF16)


def put_ends(spectrum, turned_s, halo):
    groups = spectrum.shape[0]
    lanes, deg = turned_s.shape
    _, halves, pops, cols = halo.shape
    slots = edge_slots(pops, halves * cols, groups)
    wide = lanes // 128 * (deg // groups)
    pieces = [spectrum[g].astype(F32)[wide:] for g in range(groups)]
    per = cols // 128
    for side in range(2):
        for i in range(pops):
            for h in range(halves):
                for t in range(per):
                    at = (i * halves + h) * per + t
                    row = side * slots + at % slots
                    halo[side, h, i : i + 1, t * 128 : (t + 1) * 128] = pieces[at // slots][
                        row : row + 1
                    ]


def synth_of(both, table, first=0, count=None):
    half = both.shape[0] // 2
    count = half if count is None else count
    waves, cols = table.shape[2:]
    sums = []
    for p in range(2):
        total = None
        for c in range(2):
            at = c * half + first
            some = both[at : at + count, p * waves : (p + 1) * waves]
            term = jnp.dot(some, table[c, p], preferred_element_type=F32)
            total = term if total is None else total + term
        sums.append(total * (time_step / (2 * cols)))
    return sums


def middle_body(
    params, table, spectrum, old, kept, got, fourier, rates, inner, turned_s, halo
):
    halves, pops, rows, cols = rates.shape
    first = lax.axis_index("pop") * pops
    turned(spectrum, turned_s)
    put_ends(spectrum, turned_s, halo)
    even, odd = synth_of(turned_s, table)
    for h in range(halves):
        at = slice(h * cols, (h + 1) * cols)
        lateral = lateral_of(old, h, halo)
        for i in range(pops):
            here_rows = slice(i * rows, (i + 1) * rows)
            v = even[here_rows] + odd[here_rows] if h == 0 else even[here_rows] - odd[here_rows]
            v = v + (time_step * params[3, first + i]) * lateral[i]
            inner[i, :, at] = v
            u = jnp.where(here()[0] == h, kept[i], got[i]).astype(F32) + v
            rates[h, i] = rate_of(params, first + i, u)
    put_fourier(table, rates, fourier)


def put_inner(params, table, rates, halo, inner, both, half, some, out):
    _, pops, rows, cols = rates.shape
    first = lax.axis_index("pop") * pops
    at = pl.ds(pl.multiple_of(half * cols, 128), cols)
    even, odd = synth_of(both, table, some[0] * rows, len(some) * rows)
    synth = even + jnp.where(half == 1, -1.0, 1.0) * odd
    lateral = lateral_of(rates, half, halo, some)
    for k, i in enumerate(some):
        v = synth[k * rows : (k + 1) * rows]
        v = v + (time_step * params[3, first + i]) * lateral[k]
        v = v + (1.0 - time_step * params[2, first + i]) * inner[i, :, at]
        out[k] = v.astype(BF16)


def sent_inner_body(some, params, table, spectrum, rates, inner, out, both, halo):
    turned(spectrum, both)
    put_ends(spectrum, both, halo)
    put_inner(params, table, rates, halo, inner, both, 1 - here()[0], some, out)


def more_inner_body(some, params, table, both, rates, halo, inner, out):
    put_inner(params, table, rates, halo, inner, both, 1 - here()[0], some, out)


def kept_inner_body(some, params, table, both, rates, halo, inner, out):
    put_inner(params, table, rates, halo, inner, both, here()[0], some, out)


def grid_update_body(begin, params, act, drive, kept, got, *refs):
    out = refs[-1]
    pops = begin + pl.num_programs(0) if begin else 2 * pl.num_programs(0)
    i = lax.axis_index("pop") * pops + begin + pl.program_id(0)
    keep = 1.0 - time_step * params[2, i]
    rows = kept.shape[1]
    lon = here()[0]
    for half, inner in ((lon, kept), (1 - lon, got)):
        d = time_step * half_of(drive, 0, half, rows).astype(F32)
        at = pl.ds(pl.multiple_of(half * rows, 16), rows)
        out[0, at, :] = keep * (keep * act[0, at, :] + d) + d + in_wire_order(inner[0])


def by_parts(activity, drive, basis, kernels, conn_block, coupling, rate_params):
    pops_here, lat_here, cols = activity.shape
    owned, half_lat, deg = basis.shape
    bands, lons, cores = (lax.axis_size(a) for a in ("band", "lon", "pop"))
    owners = bands * lons
    groups = owners * cores
    count = owned // cores
    rows = lat_here // lons
    nlat, nlon = bands * lat_here, lons * cols
    pops = pops_here * cores
    lanes = 2 * pops_here * rows
    band, lon, core = (lax.axis_index(a) for a in ("band", "lon", "pop"))
    owner = band * lons + lon
    table = jnp.asarray(fourier_table(nlon, owners, owned))
    weights = lat_weights(nlat).reshape(owners // 2, 1, rows)
    weights = jnp.asarray(np.tile(weights, (1, 2 * pops_here, 1)).reshape(owners // 2, lanes))
    onehot = (conn_block[..., None] == jnp.arange(kernels.shape[0], dtype=jnp.int32)).astype(F32)
    mixing = coupling[..., None] * jnp.einsum(
        "ijb,bn->ijn", onehot, kernels, precision=lax.Precision.HIGHEST
    )
    mixing = jnp.swapaxes(mixing, 0, 1)
    swap = [(0, 1), (1, 0)]

    by_pop = pl.BlockSpec((1, rows, cols), lambda i: (i, 0, 0))
    on_grid = pl.BlockSpec((1, lat_here, cols), lambda i: (i, 0, 0))
    piece = shape(pops_here, rows, cols)
    wire = shape(groups, wire_rows(count, lanes, edge_slots(pops_here, nlon, groups)), 128)
    ends = shape(2, lons, pops_here, cols, dtype=F32)
    both_halves = shape(lons, pops_here, rows, cols)
    state = shape(pops_here, rows, nlon, dtype=F32)

    some = pops_here // 2
    pairs = (list(range(some)), list(range(some, pops_here)))
    got = []
    for k, pair in enumerate(pairs):
        sent = call(
            functools.partial(sent_rates_body, pair[0]),
            shape(some, rows, cols),
            60,
            grid=(1,),
            in_specs=[
                scalars(),
                pl.BlockSpec((some, rows, cols), lambda i, k=k: (k, 1 - lax.axis_index("lon"), 0)),
            ],
            out_specs=pl.BlockSpec((some, rows, cols), lambda i: (0, 0, 0)),
        )(rate_params, activity)
        got.append(lax.ppermute(sent, "lon", swap))
    kept, carried_sent, carried_kept = call(
        own_half_body,
        (piece,) * 3,
        24,
        2 * 10**9,
        10**7,
        in_specs=[scalars()] + [whole()] * 2,
        out_specs=(whole(),) * 3,
    )(rate_params, activity, drive)
    *got, mixing = lax.optimization_barrier((*got, mixing))
    fourier, rates = call(
        first_fourier_body,
        (wire, both_halves),
        24,
        in_specs=[whole()] * 4,
        out_specs=(whole(),) * 2,
    )(table, kept, *got)

    def coupled(fourier, *more):
        spectrum = lax.all_to_all(fourier, EVERYONE, 0, 0, tiled=True)
        spectrum, *more = lax.optimization_barrier((spectrum, *more))
        more = [lax.ppermute(v, "lon", swap) for v in more]
        tiles = -(-half_lat // 128)
        scratch = pltpu.VMEM((tiles, 2 * pops * count, 128), F32)
        synthesis = call(
            functools.partial(legendre_body, nlon),
            wire,
            40,
            5 * 10**9,
            2 * 10**7,
            in_specs=[whole()] * 3 + [pl.BlockSpec(memory_space=pl.ANY)],
            out_specs=whole(),
            scratch_shapes=[
                pltpu.VMEM((count, half_lat, deg), BF16),
                pltpu.SemaphoreType.DMA((count,)),
            ]
            + [scratch] * 4,
        )(spectrum, weights, mixing, basis)
        synthesis, more = lax.optimization_barrier((synthesis, more))
        back = lax.all_to_all(synthesis, EVERYONE, 0, 0, tiled=True)
        return back, more

    back, (carried_got,) = coupled(fourier, carried_sent)
    both = shape(lanes, deg)
    fourier, rates, inner = call(
        middle_body,
        (wire, both_halves, state),
        32,
        in_specs=[scalars()] + [whole()] * 5,
        out_specs=(whole(),) * 3,
        scratch_shapes=[pltpu.VMEM(both.shape, BF16), pltpu.VMEM(ends.shape, F32)],
    )(rate_params, table, back, rates, carried_kept, carried_got)
    back, _ = coupled(fourier)
    sent, both, halo = call(
        functools.partial(sent_inner_body, pairs[0]),
        (shape(some, rows, cols), both, ends),
        24,
        in_specs=[scalars()] + [whole()] * 4,
        out_specs=(whole(),) * 3,
    )(rate_params, table, back, rates, inner)

    def inner_of(body, some, count):
        return call(
            functools.partial(body, some),
            shape(count, rows, cols),
            16,
            10**9,
            5 * 10**6,
            in_specs=[scalars()] + [whole()] * 5,
            out_specs=whole(),
        )(rate_params, table, both, rates, halo, inner)

    got = [lax.ppermute(sent, "lon", swap)]
    got.append(lax.ppermute(inner_of(more_inner_body, pairs[1], len(pairs[1])), "lon", swap))
    kept = inner_of(kept_inner_body, pairs[0] + pairs[1], pops_here)
    out = None
    for pair, there in zip(pairs, got):
        begin = pair[0]

        def on(tail, begin=begin):
            return pl.BlockSpec((1,) + tail, lambda i: (begin + i, 0, 0))

        earlier = [] if out is None else [out]
        out = call(
            functools.partial(grid_update_body, begin),
            shape(*activity.shape, dtype=F32),
            24,
            10**7,
            4 * 10**6,
            grid=(len(pair),),
            in_specs=[
                scalars(),
                on((lat_here, cols)),
                on((lat_here, cols)),
                on((rows, cols)),
                by_pop,
            ]
            + [pl.BlockSpec(memory_space=pl.ANY)] * len(earlier),
            out_specs=on((lat_here, cols)),
            input_output_aliases={5: 0} if earlier else {},
        )(rate_params, activity, drive, kept, there, *earlier)
    return out


def with_halo(shard, sides, width):
    for axis, dim in sides:
        size, length = (lax.axis_size(axis), shard.shape[dim])
        up = [(i, (i + 1) % size) for i in range(size - 1)]
        down = [(j, i) for i, j in up]
        last = lax.slice_in_dim(shard, length - width, length, axis=dim)
        leading = lax.slice_in_dim(shard, 0, width, axis=dim)
        before = lax.ppermute(last, axis, up)
        after = lax.ppermute(leading, axis, down)
        shard = jnp.concatenate([before, shard, after], axis=dim)
    return shard


def plain_table(nlon, deg):
    longitude = jnp.arange(nlon, dtype=jnp.int32)
    wavenumber = jnp.arange(deg, dtype=jnp.int32)
    phase = longitude[:, None] * wavenumber[None, :] % nlon
    angle = phase.astype(jnp.float32) * (2.0 * math.pi / nlon)
    return jnp.stack([jnp.cos(angle), jnp.sin(angle)], axis=1).astype(jnp.bfloat16)


def to_owners(fourier):
    return lax.all_to_all(fourier, ("band", "lon"), split_axis=2, concat_axis=3, tiled=True)


def to_latitudes(synthesis):
    return lax.all_to_all(synthesis, ("band", "lon"), split_axis=3, concat_axis=2, tiled=True)


def by_arrays(activity, drive, basis, kernels, conn_block, coupling, rate_params):
    pop_here = activity.shape[0]
    owned_count = basis.shape[0]
    half_lat = basis.shape[1]
    deg = basis.shape[2]
    nlon = activity.shape[2] * lax.axis_size("lon")
    quarter = deg // 2
    owner_index = lax.axis_index("band") * lax.axis_size("lon") + lax.axis_index("lon")
    pop_first = lax.axis_index("pop") * pop_here
    params = lax.dynamic_slice_in_dim(rate_params, pop_first, pop_here, 1)
    gain_row, thresh, decay_row, lateral = (params[0], params[1], params[2], params[3])
    cos_sin = plain_table(nlon, deg)
    weights = jnp.asarray(lat_weights(2 * half_lat))
    wavenumber = owner_index * owned_count + jnp.arange(owned_count, dtype=jnp.int32)
    degree = jnp.arange(deg, dtype=jnp.int32)
    triangle = degree[None, :] >= wavenumber[:, None]
    slots = jnp.arange(2, dtype=jnp.int32)
    parity_pick = (slots[None, :] == (wavenumber % 2)[:, None])[None, None, :, :, None]
    every_wave = jnp.arange(deg, dtype=jnp.int32)
    amplitude = jnp.where(every_wave == 0, 1.0, 2.0).astype(jnp.bfloat16)
    coup_own = lax.dynamic_slice_in_dim(coupling, pop_first, pop_here, 0)
    block_own = lax.dynamic_slice_in_dim(conn_block, pop_first, pop_here, 0)
    onehot = (block_own[..., None] == jnp.arange(kernels.shape[0], dtype=jnp.int32)).astype(
        jnp.float32
    )
    mixing = coup_own[..., None] * jnp.einsum(
        "ijb,bn->ijn", onehot, kernels, precision=lax.Precision.HIGHEST
    )
    basis_split = basis.reshape(owned_count, half_lat, quarter, 2)
    drive_f32 = drive.astype(jnp.float32)
    activity_now = activity
    for step_index in range(STEPS):
        rates = jax.nn.sigmoid(
            gain_row[:, None, None] * (activity_now - thresh[:, None, None])
        ).astype(jnp.bfloat16)
        lat_rows = lax.all_to_all(rates, "lon", split_axis=1, concat_axis=2, tiled=True)
        fourier = jnp.einsum(
            "ijk,kcm->icmj", lat_rows, cos_sin, preferred_element_type=jnp.float32
        ).astype(jnp.bfloat16)
        spectrum = to_owners(fourier)
        northern = spectrum[..., :half_lat].astype(jnp.float32)
        southern = jnp.flip(spectrum[..., half_lat:], axis=3).astype(jnp.float32)
        even_part = (weights * (northern + southern)).astype(jnp.bfloat16)
        odd_part = (weights * (northern - southern)).astype(jnp.bfloat16)
        operand = jnp.where(parity_pick, even_part[:, :, :, None, :], odd_part[:, :, :, None, :])
        coeffs = jnp.einsum(
            "icmsj,mjqs->icmqs", operand, basis_split, preferred_element_type=jnp.float32
        )
        coeffs = coeffs.reshape(pop_here, 2, owned_count, deg)
        coeffs = jnp.where(triangle[None, None], coeffs, 0.0)
        gathered = lax.all_gather(coeffs.astype(jnp.bfloat16), "pop", axis=0, tiled=True).astype(
            coeffs.dtype
        )
        mixed_spec = jnp.sum(mixing[:, :, None, None, :] * gathered[None], axis=1).astype(
            jnp.bfloat16
        )
        degree_parts = jnp.einsum(
            "icmqs,mjqs->icmsj",
            mixed_spec.reshape(pop_here, 2, owned_count, quarter, 2),
            basis_split,
            preferred_element_type=jnp.float32,
        )
        same_parity = jnp.sum(jnp.where(parity_pick, degree_parts, 0.0), axis=3)
        other_parity = jnp.sum(jnp.where(parity_pick, 0.0, degree_parts), axis=3)
        synthesis = jnp.concatenate(
            [same_parity + other_parity, jnp.flip(same_parity - other_parity, axis=3)], axis=3
        ).astype(jnp.bfloat16)
        returned = to_latitudes(synthesis)
        scaled = returned * amplitude[None, None, :, None]
        synth_field = jnp.einsum(
            "icmj,kcm->ijk", scaled, cos_sin, preferred_element_type=jnp.float32
        ) * (1.0 / nlon)
        padded = with_halo(lat_rows, ((("band", "lon"), 1),), 1).astype(jnp.float32)
        rates_f32 = lat_rows.astype(jnp.float32)
        lateral_term = (
            jnp.roll(rates_f32, 1, axis=2)
            + jnp.roll(rates_f32, -1, axis=2)
            + padded[:, 2:, :]
            + padded[:, :-2, :]
            - 4.0 * rates_f32
        )
        coupled = synth_field + lateral[:, None, None] * lateral_term
        coupled_grid = lax.all_to_all(
            coupled.astype(jnp.bfloat16), "lon", split_axis=2, concat_axis=1, tiled=True
        ).astype(coupled.dtype)
        forcing = -decay_row[:, None, None] * activity_now + coupled_grid + drive_f32
        activity_now = activity_now + time_step * forcing
    return activity_now


def solution(mesh):
    bands, lons, cores = (mesh.shape[a] for a in ("band", "lon", "pop"))

    def local(activity, drive, basis, *rest):
        rows, owned = activity.shape[1] // lons, basis.shape[0]
        fits = (
            bands % 2 == 0
            and activity.shape[0] % 2 == 0
            and lons == 2
            and cores == 2
            and bands * lons * cores % 4 == 0
            and owned % (8 * cores) == 0
            and rows % 16 == 0
            and activity.shape[2] % 128 == 0
            and 2 * activity.shape[0] * rows % 128 == 0
        )
        return (by_parts if fits else by_arrays)(activity, drive, basis, *rest)

    in_specs = (
        P(("subj", "pop"), "band", "lon"),
        P(("subj", "pop"), "band", "lon"),
        P(("subj", "band", "lon"), None, None),
        P(),
        P(),
        P("subj", None),
        P("subj", None),
    )
    out_specs = P(("subj", "pop"), "band", "lon")
    return jax.shard_map(local, mesh=mesh, in_specs=in_specs, out_specs=out_specs, check_vma=False)
```

```python
import functools
import math

import jax
import jax.numpy as jnp
import ml_dtypes
import numpy as np
from jax import lax
from jax.experimental import pallas as pl
from jax.experimental.pallas import tpu as pltpu
from jax.sharding import PartitionSpec as P

STEPS = 2
time_step = 0.5
F32 = jnp.float32
BF16 = jnp.bfloat16
OWNERS = ("band", "lon")
EVERYONE = ("band", "lon", "pop")
MIB = 1 << 20


def call(body, out_shape, vmem_mib, flops=0, nbytes=0, **kw):
    return pl.pallas_call(
        body,
        out_shape=out_shape,
        compiler_params=pltpu.CompilerParams(vmem_limit_bytes=vmem_mib * MIB),
        cost_estimate=pl.CostEstimate(flops=flops, bytes_accessed=nbytes, transcendentals=0),
        **kw,
    )


def whole():
    return pl.BlockSpec(memory_space=pltpu.VMEM)


def scalars():
    return pl.BlockSpec(memory_space=pltpu.SMEM)


def shape(*dims, dtype=BF16):
    return jax.ShapeDtypeStruct(dims, dtype)


def nt_dot(a, b):
    return lax.dot_general(a, b, (((1,), (1,)), ((), ())), preferred_element_type=F32)


def fourier_table(nlon, owners, owned):
    wave = np.arange(owners * owned, dtype=np.int64).reshape(-1, 2).T.reshape(-1)
    phase = wave[:, None] * np.arange(nlon // 2, dtype=np.int64)[None, :] % nlon
    angle = phase.astype(np.float32) * np.float32(2.0 * math.pi / nlon)
    table = np.stack([np.cos(angle), np.sin(angle)]).astype(ml_dtypes.bfloat16)
    return table.reshape(2, 2, -1, nlon // 2)


def lat_weights(nlat):
    row_index = np.arange(nlat // 2, dtype=np.float32)
    colatitude = np.float32(math.pi) * (4.0 * row_index + 3.0) / np.float32(4.0 * nlat + 2.0)
    return (np.float32(math.pi) * np.sin(colatitude) / np.float32(nlat)).astype(np.float32)


def here():
    bands, lons = lax.axis_size("band"), lax.axis_size("lon")
    band, lon = lax.axis_index("band"), lax.axis_index("lon")
    owner, half = band * lons + lon, bands * lons // 2
    at_equator = jnp.logical_or(owner == half - 1, owner == half)
    at_pole = jnp.logical_or(owner == 0, owner == 2 * half - 1)
    return lon, owner >= half, at_equator, at_pole


def in_wire_order(block):
    rows = block.shape[0]
    a = lax.broadcasted_iota(jnp.int32, (rows, rows), 0)
    b = lax.broadcasted_iota(jnp.int32, (rows, rows), 1)
    move = jnp.where(a == jnp.where(here()[1], rows - 1 - b, b), 1.0, 0.0).astype(BF16)
    return jnp.dot(move, block, preferred_element_type=F32)


def rate_of(params, i, u):
    return jax.nn.sigmoid(params[0, i] * (u - params[1, i])).astype(BF16)


def half_of(ref, lead, half, rows):
    return ref[lead, pl.ds(pl.multiple_of(half * rows, 16), rows), :]


def sent_rates_body(begin, params, act, rates):
    count = act.shape[0]
    pops = params.shape[1] // lax.axis_size("pop")
    first = lax.axis_index("pop") * pops + begin
    for i in range(count):
        rates[i] = in_wire_order(rate_of(params, first + i, act[i])).astype(BF16)


def own_half_body(params, act, drive, rates, sent, kept):
    pops, rows, cols = rates.shape
    first = lax.axis_index("pop") * pops
    lon = here()[0]
    for i in range(pops):
        decay = params[2, first + i]
        for half, out in ((1 - lon, sent), (lon, kept)):
            u = half_of(act, i, half, rows)
            d = half_of(drive, i, half, rows).astype(F32)
            c = ((1.0 - time_step * decay) * u + time_step * d).astype(BF16)
            out[i] = in_wire_order(c).astype(BF16)
        r = rate_of(params, first + i, half_of(act, i, lon, rows))
        rates[i] = in_wire_order(r).astype(BF16)


def edge_slots(pops, nlon, groups):
    return -(-pops * (nlon // 128) // groups)


def wire_rows(count, lanes, slots):
    return -(-(count * (lanes // 128) + 2 * slots) // 16) * 16


def packed(sums, extra, total):
    parts = [sums[:, t * 128 : (t + 1) * 128] for t in range(sums.shape[1] // 128)] + extra
    missing = total - sum(v.shape[0] for v in parts)
    if missing:
        parts.append(jnp.zeros((missing, 128), F32))
    return jnp.concatenate(parts, axis=0).astype(BF16)


def unpacked(block, count, lanes):
    block = block.astype(F32)
    parts = [block[t * count : (t + 1) * count] for t in range(lanes // 128)]
    return jnp.concatenate(parts, axis=1)


def put_fourier(table, rates, fourier):
    halves, pops, rows, cols = rates.shape
    groups, total, _ = fourier.shape
    lanes = 2 * pops * rows
    waves = table.shape[2]
    count = 2 * waves // groups
    slots = edge_slots(pops, halves * cols, groups)
    polar, inner = [], []
    for i in range(pops):
        for h in range(halves):
            strip = rates[h, i].astype(F32)
            for t in range(cols // 128):
                at = slice(t * 128, (t + 1) * 128)
                polar.append(strip[:1, at])
                inner.append(strip[rows - 1 :, at])
    nothing = [jnp.zeros((1, 128), F32)] * (slots * groups - len(polar))
    polar, inner = polar + nothing, inner + nothing
    one, two = rates[0].astype(F32), rates[1].astype(F32)
    pack = groups // 4
    block = pack * count
    for p, mix in enumerate((one + two - 1.0, one - two)):
        flat = mix.astype(BF16).reshape(pops * rows, cols)
        for b in range(waves // block):
            parts = []
            for c in range(2):
                t = table[c, p, b * block : (b + 1) * block]
                sums = nt_dot(t, flat)
                if p == 0:
                    sums = sums + jnp.sum(t.astype(F32), axis=1, keepdims=True)
                parts.append(sums)
            joined = jnp.concatenate(parts, axis=1)
            for k in range(pack):
                to = (b * pack + k) * 2 + p
                at = slice(to * slots, (to + 1) * slots)
                sums = joined[k * count : (k + 1) * count]
                fourier[to] = packed(sums, polar[at] + inner[at], total)


def first_fourier_body(table, kept, got, got_more, fourier, rates):
    some = got.shape[0]
    lon = here()[0]
    rates[lon] = kept[...]
    rates[1 - lon, :some] = got[...]
    rates[1 - lon, some:] = got_more[...]
    put_fourier(table, rates, fourier)


def lateral_of(rates, half, halo, some=None):
    _, pops, rows, cols = rates.shape
    before, after = halo[0, half], halo[1, half]
    row = lax.broadcasted_iota(jnp.int32, (rows, cols), 0)
    lane = lax.broadcasted_iota(jnp.int32, (rows, cols), 1)
    terms = []
    for i in some or range(pops):
        r = rates[half, i].astype(F32)
        other = rates[1 - half, i].astype(F32)
        east = jnp.where(lane == 0, other[:, cols - 1 :], pltpu.roll(r, 1, 1))
        west = jnp.where(lane == cols - 1, other[:, :1], pltpu.roll(r, cols - 1, 1))
        up = jnp.where(row == 0, before[i : i + 1], pltpu.roll(r, 1, 0))
        down = jnp.where(row == rows - 1, after[i : i + 1], pltpu.roll(r, rows - 1, 0))
        terms.append(east + west + up + down - 4.0 * r)
    return terms


def legendre_body(
    nlon, spectrum, weight, mixing, basis, out, held, arrived, even_s, odd_s, north_s, south_s
):
    groups, total, _ = out.shape
    count = held.shape[0]
    lanes = weight.shape[1]
    tiles = even_s.shape[0]
    _, half_lat, deg = basis.shape
    pops = mixing.shape[0]
    src = weight.shape[0]
    cores = groups // (2 * src)
    piece = half_lat // src
    lots = lanes // piece
    pops_here = lots // 2
    slots = edge_slots(pops_here, nlon, groups)
    pad = tiles * 128 - half_lat
    block = 8
    owner = lax.axis_index("band") * lax.axis_size("lon") + lax.axis_index("lon")
    core = lax.axis_index("pop")
    first_wave = owner * basis.shape[0] + core

    def fetch(r):
        return pltpu.make_async_copy(basis.at[cores * r + core], held.at[r], arrived.at[r])

    @pl.loop(0, count)
    def _(r):
        fetch(r).start()

    wide = lanes // 128 * count
    pieces = [spectrum[g].astype(F32)[wide:] for g in range(groups)]
    passed = []
    for to in range(2 * src):
        step = 1 if to < src else -1
        outward, inward = to - step, to + step
        crossing = to in (src - 1, src)
        for p in range(cores):
            if 0 <= outward < 2 * src:
                before = pieces[outward * cores + p][slots : 2 * slots]
            else:
                before = jnp.zeros((slots, 128), F32)
            after = pieces[inward * cores + p]
            after = after[slots : 2 * slots] if crossing else after[:slots]
            passed.append([before, after])

    def rows_of(p, q):
        b = (q // pops_here) * pops + p * pops_here + q % pops_here
        return slice(b * count, (b + 1) * count)

    for p in range(cores):
        evens, odds = [], []
        for s in range(src):
            north = unpacked(spectrum[s * cores + p], count, lanes)
            south = unpacked(spectrum[(2 * src - 1 - s) * cores + p], count, lanes)
            w = weight[s : s + 1]
            evens.append((w * (north + south)).astype(BF16).astype(F32))
            odds.append((w * (north - south)).astype(BF16).astype(F32))
        for q in range(lots):
            for parts, scratch in ((evens, even_s), (odds, odd_s)):
                strips = [v[:, q * piece : (q + 1) * piece] for v in parts]
                if pad:
                    strips.append(jnp.zeros((count, pad), F32))
                joined = jnp.concatenate(strips, axis=1)
                for t in range(tiles):
                    scratch[t, rows_of(p, q), :] = joined[:, t * 128 : (t + 1) * 128]

    degree = lax.broadcasted_iota(jnp.int32, (2 * pops, deg), 1)

    @pl.loop(0, count // block)
    def _(step):
        for at in range(block):
            fetch(step * block + at).wait()
        todo = []
        for at in range(block):
            r = step * block + at
            m = first_wave + cores * r
            rows = pl.ds(r, 2 * pops, stride=count)
            lhs = jnp.concatenate(
                [
                    jnp.concatenate([scratch[t, rows, :] for t in range(tiles)], axis=1)
                    for scratch in (even_s, odd_s)
                ],
                axis=0,
            )[:, :half_lat].astype(BF16)
            both = jnp.dot(lhs, held[r], preferred_element_type=F32)
            odd = ((degree - m) & 1) == 1
            coeffs = jnp.where(odd, both[2 * pops :], both[: 2 * pops])
            coeffs = jnp.where(degree >= m, coeffs, 0.0)
            mixed = []
            for c in range(2):
                total = None
                for j in range(pops):
                    term = mixing[j] * coeffs[c * pops + j : c * pops + j + 1]
                    total = term if total is None else total + term
                mixed.append(total)
            mixed = jnp.concatenate(mixed, axis=0)
            lhs2 = jnp.concatenate([mixed, jnp.where(odd, -mixed, mixed)], axis=0).astype(BF16)
            todo.append((r, m, rows, lhs2))
        for r, m, rows, lhs2 in todo:
            amplitude = jnp.where(m == 0, 1.0, 2.0)
            field = nt_dot(lhs2, held[r]) * amplitude
            if pad:
                field = jnp.concatenate([field, jnp.zeros((4 * pops, pad), F32)], axis=1)
            for t in range(tiles):
                north_s[t, rows, :] = field[: 2 * pops, t * 128 : (t + 1) * 128]
                south_s[t, rows, :] = field[2 * pops :, t * 128 : (t + 1) * 128]

    for scratch, south in ((north_s, False), (south_s, True)):
        for p in range(cores):
            wide = [
                jnp.concatenate(
                    [scratch[t, rows_of(p, q), :] for t in range(tiles)], axis=1
                )
                for q in range(lots)
            ]
            for s in range(src):
                to = (2 * src - 1 - s if south else s) * cores + p
                strips = [v[:, s * piece : (s + 1) * piece] for v in wide]
                out[to] = packed(jnp.concatenate(strips, axis=1), passed[to], total)


def turned(spectrum, turned_s):
    groups = spectrum.shape[0]
    lanes, deg = turned_s.shape
    order = list(range(0, groups, 2)) + list(range(1, groups, 2))
    blocks = [unpacked(spectrum[g], deg // groups, lanes) for g in order]
    turned_s[...] = jnp.concatenate(blocks, axis=0).T.astype(BF16)


def put_ends(spectrum, turned_s, halo):
    groups = spectrum.shape[0]
    lanes, deg = turned_s.shape
    _, halves, pops, cols = halo.shape
    slots = edge_slots(pops, halves * cols, groups)
    wide = lanes // 128 * (deg // groups)
    pieces = [spectrum[g].astype(F32)[wide:] for g in range(groups)]
    per = cols // 128
    for side in range(2):
        for i in range(pops):
            for h in range(halves):
                for t in range(per):
                    at = (i * halves + h) * per + t
                    row = side * slots + at % slots
                    halo[side, h, i : i + 1, t * 128 : (t + 1) * 128] = pieces[at // slots][
                        row : row + 1
                    ]


def synth_of(both, table, first=0, count=None):
    half = both.shape[0] // 2
    count = half if count is None else count
    waves, cols = table.shape[2:]
    sums = []
    for p in range(2):
        total = None
        for c in range(2):
            at = c * half + first
            some = both[at : at + count, p * waves : (p + 1) * waves]
            term = jnp.dot(some, table[c, p], preferred_element_type=F32)
            total = term if total is None else total + term
        sums.append(total * (time_step / (2 * cols)))
    return sums


def middle_body(
    params, table, spectrum, old, kept, got, fourier, rates, inner, turned_s, halo
):
    halves, pops, rows, cols = rates.shape
    first = lax.axis_index("pop") * pops
    turned(spectrum, turned_s)
    put_ends(spectrum, turned_s, halo)
    even, odd = synth_of(turned_s, table)
    for h in range(halves):
        at = slice(h * cols, (h + 1) * cols)
        lateral = lateral_of(old, h, halo)
        for i in range(pops):
            here_rows = slice(i * rows, (i + 1) * rows)
            v = even[here_rows] + odd[here_rows] if h == 0 else even[here_rows] - odd[here_rows]
            v = v + (time_step * params[3, first + i]) * lateral[i]
            inner[i, :, at] = v
            u = jnp.where(here()[0] == h, kept[i], got[i]).astype(F32) + v
            rates[h, i] = rate_of(params, first + i, u)
    put_fourier(table, rates, fourier)


def put_inner(params, table, rates, halo, inner, both, half, some, out):
    _, pops, rows, cols = rates.shape
    first = lax.axis_index("pop") * pops
    at = pl.ds(pl.multiple_of(half * cols, 128), cols)
    even, odd = synth_of(both, table, some[0] * rows, len(some) * rows)
    synth = even + jnp.where(half == 1, -1.0, 1.0) * odd
    lateral = lateral_of(rates, half, halo, some)
    for k, i in enumerate(some):
        v = synth[k * rows : (k + 1) * rows]
        v = v + (time_step * params[3, first + i]) * lateral[k]
        v = v + (1.0 - time_step * params[2, first + i]) * inner[i, :, at]
        out[k] = v.astype(BF16)


def sent_inner_body(some, params, table, spectrum, rates, inner, out, both, halo):
    turned(spectrum, both)
    put_ends(spectrum, both, halo)
    put_inner(params, table, rates, halo, inner, both, 1 - here()[0], some, out)


def more_inner_body(some, params, table, both, rates, halo, inner, out):
    put_inner(params, table, rates, halo, inner, both, 1 - here()[0], some, out)


def kept_inner_body(some, params, table, both, rates, halo, inner, out):
    put_inner(params, table, rates, halo, inner, both, here()[0], some, out)


def grid_update_body(begin, params, act, drive, kept, got, *refs):
    out = refs[-1]
    pops = begin + pl.num_programs(0) if begin else 2 * pl.num_programs(0)
    i = lax.axis_index("pop") * pops + begin + pl.program_id(0)
    keep = 1.0 - time_step * params[2, i]
    rows = kept.shape[1]
    lon = here()[0]
    for half, inner in ((lon, kept), (1 - lon, got)):
        d = time_step * half_of(drive, 0, half, rows).astype(F32)
        at = pl.ds(pl.multiple_of(half * rows, 16), rows)
        out[0, at, :] = keep * (keep * act[0, at, :] + d) + d + in_wire_order(inner[0])


def by_parts(activity, drive, basis, kernels, conn_block, coupling, rate_params):
    pops_here, lat_here, cols = activity.shape
    owned, half_lat, deg = basis.shape
    bands, lons, cores = (lax.axis_size(a) for a in ("band", "lon", "pop"))
    owners = bands * lons
    groups = owners * cores
    count = owned // cores
    rows = lat_here // lons
    nlat, nlon = bands * lat_here, lons * cols
    pops = pops_here * cores
    lanes = 2 * pops_here * rows
    band, lon, core = (lax.axis_index(a) for a in ("band", "lon", "pop"))
    owner = band * lons + lon
    table = jnp.asarray(fourier_table(nlon, owners, owned))
    weights = lat_weights(nlat).reshape(owners // 2, 1, rows)
    weights = jnp.asarray(np.tile(weights, (1, 2 * pops_here, 1)).reshape(owners // 2, lanes))
    onehot = (conn_block[..., None] == jnp.arange(kernels.shape[0], dtype=jnp.int32)).astype(F32)
    mixing = coupling[..., None] * jnp.einsum(
        "ijb,bn->ijn", onehot, kernels, precision=lax.Precision.HIGHEST
    )
    mixing = jnp.swapaxes(mixing, 0, 1)
    swap = [(0, 1), (1, 0)]

    by_pop = pl.BlockSpec((1, rows, cols), lambda i: (i, 0, 0))
    on_grid = pl.BlockSpec((1, lat_here, cols), lambda i: (i, 0, 0))
    piece = shape(pops_here, rows, cols)
    wire = shape(groups, wire_rows(count, lanes, edge_slots(pops_here, nlon, groups)), 128)
    ends = shape(2, lons, pops_here, cols, dtype=F32)
    both_halves = shape(lons, pops_here, rows, cols)
    state = shape(pops_here, rows, nlon, dtype=F32)

    some = pops_here // 2
    pairs = (list(range(some)), list(range(some, pops_here)))
    got = []
    for k, pair in enumerate(pairs):
        sent = call(
            functools.partial(sent_rates_body, pair[0]),
            shape(some, rows, cols),
            60,
            grid=(1,),
            in_specs=[
                scalars(),
                pl.BlockSpec((some, rows, cols), lambda i, k=k: (k, 1 - lax.axis_index("lon"), 0)),
            ],
            out_specs=pl.BlockSpec((some, rows, cols), lambda i: (0, 0, 0)),
        )(rate_params, activity)
        got.append(lax.ppermute(sent, "lon", swap))
    kept, carried_sent, carried_kept = call(
        own_half_body,
        (piece,) * 3,
        24,
        2 * 10**9,
        10**7,
        in_specs=[scalars()] + [whole()] * 2,
        out_specs=(whole(),) * 3,
    )(rate_params, activity, drive)
    *got, mixing = lax.optimization_barrier((*got, mixing))
    fourier, rates = call(
        first_fourier_body,
        (wire, both_halves),
        24,
        in_specs=[whole()] * 4,
        out_specs=(whole(),) * 2,
    )(table, kept, *got)

    def coupled(fourier, *more):
        spectrum = lax.all_to_all(fourier, EVERYONE, 0, 0, tiled=True)
        spectrum, *more = lax.optimization_barrier((spectrum, *more))
        more = [lax.ppermute(v, "lon", swap) for v in more]
        tiles = -(-half_lat // 128)
        scratch = pltpu.VMEM((tiles, 2 * pops * count, 128), F32)
        synthesis = call(
            functools.partial(legendre_body, nlon),
            wire,
            40,
            5 * 10**9,
            2 * 10**7,
            in_specs=[whole()] * 3 + [pl.BlockSpec(memory_space=pl.ANY)],
            out_specs=whole(),
            scratch_shapes=[
                pltpu.VMEM((count, half_lat, deg), BF16),
                pltpu.SemaphoreType.DMA((count,)),
            ]
            + [scratch] * 4,
        )(spectrum, weights, mixing, basis)
        synthesis, more = lax.optimization_barrier((synthesis, more))
        back = lax.all_to_all(synthesis, EVERYONE, 0, 0, tiled=True)
        return back, more

    back, (carried_got,) = coupled(fourier, carried_sent)
    both = shape(lanes, deg)
    fourier, rates, inner = call(
        middle_body,
        (wire, both_halves, state),
        32,
        in_specs=[scalars()] + [whole()] * 5,
        out_specs=(whole(),) * 3,
        scratch_shapes=[pltpu.VMEM(both.shape, BF16), pltpu.VMEM(ends.shape, F32)],
    )(rate_params, table, back, rates, carried_kept, carried_got)
    back, _ = coupled(fourier)
    sent, both, halo = call(
        functools.partial(sent_inner_body, pairs[0]),
        (shape(some, rows, cols), both, ends),
        24,
        in_specs=[scalars()] + [whole()] * 4,
        out_specs=(whole(),) * 3,
    )(rate_params, table, back, rates, inner)

    def inner_of(body, some, count):
        return call(
            functools.partial(body, some),
            shape(count, rows, cols),
            16,
            10**9,
            5 * 10**6,
            in_specs=[scalars()] + [whole()] * 5,
            out_specs=whole(),
        )(rate_params, table, both, rates, halo, inner)

    got = [lax.ppermute(sent, "lon", swap)]
    got.append(lax.ppermute(inner_of(more_inner_body, pairs[1], len(pairs[1])), "lon", swap))
    kept = inner_of(kept_inner_body, pairs[0] + pairs[1], pops_here)
    out = None
    for pair, there in zip(pairs, got):
        begin = pair[0]

        def on(tail, begin=begin):
            return pl.BlockSpec((1,) + tail, lambda i: (begin + i, 0, 0))

        earlier = [] if out is None else [out]
        out = call(
            functools.partial(grid_update_body, begin),
            shape(*activity.shape, dtype=F32),
            24,
            10**7,
            4 * 10**6,
            grid=(len(pair),),
            in_specs=[
                scalars(),
                on((lat_here, cols)),
                on((lat_here, cols)),
                on((rows, cols)),
                by_pop,
            ]
            + [pl.BlockSpec(memory_space=pl.ANY)] * len(earlier),
            out_specs=on((lat_here, cols)),
            input_output_aliases={5: 0} if earlier else {},
        )(rate_params, activity, drive, kept, there, *earlier)
    return out


def with_halo(shard, sides, width):
    for axis, dim in sides:
        size, length = (lax.axis_size(axis), shard.shape[dim])
        up = [(i, (i + 1) % size) for i in range(size - 1)]
        down = [(j, i) for i, j in up]
        last = lax.slice_in_dim(shard, length - width, length, axis=dim)
        leading = lax.slice_in_dim(shard, 0, width, axis=dim)
        before = lax.ppermute(last, axis, up)
        after = lax.ppermute(leading, axis, down)
        shard = jnp.concatenate([before, shard, after], axis=dim)
    return shard


def plain_table(nlon, deg):
    longitude = jnp.arange(nlon, dtype=jnp.int32)
    wavenumber = jnp.arange(deg, dtype=jnp.int32)
    phase = longitude[:, None] * wavenumber[None, :] % nlon
    angle = phase.astype(jnp.float32) * (2.0 * math.pi / nlon)
    return jnp.stack([jnp.cos(angle), jnp.sin(angle)], axis=1).astype(jnp.bfloat16)


def to_owners(fourier):
    return lax.all_to_all(fourier, ("band", "lon"), split_axis=2, concat_axis=3, tiled=True)


def to_latitudes(synthesis):
    return lax.all_to_all(synthesis, ("band", "lon"), split_axis=3, concat_axis=2, tiled=True)


def by_arrays(activity, drive, basis, kernels, conn_block, coupling, rate_params):
    pop_here = activity.shape[0]
    owned_count = basis.shape[0]
    half_lat = basis.shape[1]
    deg = basis.shape[2]
    nlon = activity.shape[2] * lax.axis_size("lon")
    quarter = deg // 2
    owner_index = lax.axis_index("band") * lax.axis_size("lon") + lax.axis_index("lon")
    pop_first = lax.axis_index("pop") * pop_here
    params = lax.dynamic_slice_in_dim(rate_params, pop_first, pop_here, 1)
    gain_row, thresh, decay_row, lateral = (params[0], params[1], params[2], params[3])
    cos_sin = plain_table(nlon, deg)
    weights = jnp.asarray(lat_weights(2 * half_lat))
    wavenumber = owner_index * owned_count + jnp.arange(owned_count, dtype=jnp.int32)
    degree = jnp.arange(deg, dtype=jnp.int32)
    triangle = degree[None, :] >= wavenumber[:, None]
    slots = jnp.arange(2, dtype=jnp.int32)
    parity_pick = (slots[None, :] == (wavenumber % 2)[:, None])[None, None, :, :, None]
    every_wave = jnp.arange(deg, dtype=jnp.int32)
    amplitude = jnp.where(every_wave == 0, 1.0, 2.0).astype(jnp.bfloat16)
    coup_own = lax.dynamic_slice_in_dim(coupling, pop_first, pop_here, 0)
    block_own = lax.dynamic_slice_in_dim(conn_block, pop_first, pop_here, 0)
    onehot = (block_own[..., None] == jnp.arange(kernels.shape[0], dtype=jnp.int32)).astype(
        jnp.float32
    )
    mixing = coup_own[..., None] * jnp.einsum(
        "ijb,bn->ijn", onehot, kernels, precision=lax.Precision.HIGHEST
    )
    basis_split = basis.reshape(owned_count, half_lat, quarter, 2)
    drive_f32 = drive.astype(jnp.float32)
    activity_now = activity
    for step_index in range(STEPS):
        rates = jax.nn.sigmoid(
            gain_row[:, None, None] * (activity_now - thresh[:, None, None])
        ).astype(jnp.bfloat16)
        lat_rows = lax.all_to_all(rates, "lon", split_axis=1, concat_axis=2, tiled=True)
        fourier = jnp.einsum(
            "ijk,kcm->icmj", lat_rows, cos_sin, preferred_element_type=jnp.float32
        ).astype(jnp.bfloat16)
        spectrum = to_owners(fourier)
        northern = spectrum[..., :half_lat].astype(jnp.float32)
        southern = jnp.flip(spectrum[..., half_lat:], axis=3).astype(jnp.float32)
        even_part = (weights * (northern + southern)).astype(jnp.bfloat16)
        odd_part = (weights * (northern - southern)).astype(jnp.bfloat16)
        operand = jnp.where(parity_pick, even_part[:, :, :, None, :], odd_part[:, :, :, None, :])
        coeffs = jnp.einsum(
            "icmsj,mjqs->icmqs", operand, basis_split, preferred_element_type=jnp.float32
        )
        coeffs = coeffs.reshape(pop_here, 2, owned_count, deg)
        coeffs = jnp.where(triangle[None, None], coeffs, 0.0)
        gathered = lax.all_gather(coeffs.astype(jnp.bfloat16), "pop", axis=0, tiled=True).astype(
            coeffs.dtype
        )
        mixed_spec = jnp.sum(mixing[:, :, None, None, :] * gathered[None], axis=1).astype(
            jnp.bfloat16
        )
        degree_parts = jnp.einsum(
            "icmqs,mjqs->icmsj",
            mixed_spec.reshape(pop_here, 2, owned_count, quarter, 2),
            basis_split,
            preferred_element_type=jnp.float32,
        )
        same_parity = jnp.sum(jnp.where(parity_pick, degree_parts, 0.0), axis=3)
        other_parity = jnp.sum(jnp.where(parity_pick, 0.0, degree_parts), axis=3)
        synthesis = jnp.concatenate(
            [same_parity + other_parity, jnp.flip(same_parity - other_parity, axis=3)], axis=3
        ).astype(jnp.bfloat16)
        returned = to_latitudes(synthesis)
        scaled = returned * amplitude[None, None, :, None]
        synth_field = jnp.einsum(
            "icmj,kcm->ijk", scaled, cos_sin, preferred_element_type=jnp.float32
        ) * (1.0 / nlon)
        padded = with_halo(lat_rows, ((("band", "lon"), 1),), 1).astype(jnp.float32)
        rates_f32 = lat_rows.astype(jnp.float32)
        lateral_term = (
            jnp.roll(rates_f32, 1, axis=2)
            + jnp.roll(rates_f32, -1, axis=2)
            + padded[:, 2:, :]
            + padded[:, :-2, :]
            - 4.0 * rates_f32
        )
        coupled = synth_field + lateral[:, None, None] * lateral_term
        coupled_grid = lax.all_to_all(
            coupled.astype(jnp.bfloat16), "lon", split_axis=2, concat_axis=1, tiled=True
        ).astype(coupled.dtype)
        forcing = -decay_row[:, None, None] * activity_now + coupled_grid + drive_f32
        activity_now = activity_now + time_step * forcing
    return activity_now


def solution(mesh):
    bands, lons, cores = (mesh.shape[a] for a in ("band", "lon", "pop"))

    def local(activity, drive, basis, *rest):
        rows, owned = activity.shape[1] // lons, basis.shape[0]
        fits = (
            bands % 2 == 0
            and activity.shape[0] % 2 == 0
            and lons == 2
            and cores == 2
            and bands * lons * cores % 4 == 0
            and owned % (8 * cores) == 0
            and rows % 16 == 0
            and activity.shape[2] % 128 == 0
            and 2 * activity.shape[0] * rows % 128 == 0
        )
        return (by_parts if fits else by_arrays)(activity, drive, basis, *rest)

    in_specs = (
        P(("subj", "pop"), "band", "lon"),
        P(("subj", "pop"), "band", "lon"),
        P(("subj", "band", "lon"), None, None),
        P(),
        P(),
        P("subj", None),
        P("subj", None),
    )
    out_specs = P(("subj", "pop"), "band", "lon")
    return jax.shard_map(local, mesh=mesh, in_specs=in_specs, out_specs=out_specs, check_vma=False)
```

```python
import functools
import math

import jax
import jax.numpy as jnp
import ml_dtypes
import numpy as np
from jax import lax
from jax.experimental import pallas as pl
from jax.experimental.pallas import tpu as pltpu
from jax.sharding import PartitionSpec as P

STEPS = 2
time_step = 0.5
F32 = jnp.float32
BF16 = jnp.bfloat16
OWNERS = ("band", "lon")
EVERYONE = ("band", "lon", "pop")
MIB = 1 << 20


def call(body, out_shape, vmem_mib, flops=0, nbytes=0, **kw):
    return pl.pallas_call(
        body,
        out_shape=out_shape,
        compiler_params=pltpu.CompilerParams(vmem_limit_bytes=vmem_mib * MIB),
        cost_estimate=pl.CostEstimate(flops=flops, bytes_accessed=nbytes, transcendentals=0),
        **kw,
    )


def whole():
    return pl.BlockSpec(memory_space=pltpu.VMEM)


def scalars():
    return pl.BlockSpec(memory_space=pltpu.SMEM)


def shape(*dims, dtype=BF16):
    return jax.ShapeDtypeStruct(dims, dtype)


def nt_dot(a, b):
    return lax.dot_general(a, b, (((1,), (1,)), ((), ())), preferred_element_type=F32)


def fourier_table(nlon, owners, owned):
    wave = np.arange(owners * owned, dtype=np.int64).reshape(-1, 2).T.reshape(-1)
    phase = wave[:, None] * np.arange(nlon // 2, dtype=np.int64)[None, :] % nlon
    angle = phase.astype(np.float32) * np.float32(2.0 * math.pi / nlon)
    table = np.stack([np.cos(angle), np.sin(angle)]).astype(ml_dtypes.bfloat16)
    return table.reshape(2, 2, -1, nlon // 2)


def lat_weights(nlat):
    row_index = np.arange(nlat // 2, dtype=np.float32)
    colatitude = np.float32(math.pi) * (4.0 * row_index + 3.0) / np.float32(4.0 * nlat + 2.0)
    return (np.float32(math.pi) * np.sin(colatitude) / np.float32(nlat)).astype(np.float32)


def here():
    bands, lons = lax.axis_size("band"), lax.axis_size("lon")
    band, lon = lax.axis_index("band"), lax.axis_index("lon")
    owner, half = band * lons + lon, bands * lons // 2
    at_equator = jnp.logical_or(owner == half - 1, owner == half)
    at_pole = jnp.logical_or(owner == 0, owner == 2 * half - 1)
    return lon, owner >= half, at_equator, at_pole


def in_wire_order(block):
    rows = block.shape[0]
    a = lax.broadcasted_iota(jnp.int32, (rows, rows), 0)
    b = lax.broadcasted_iota(jnp.int32, (rows, rows), 1)
    move = jnp.where(a == jnp.where(here()[1], rows - 1 - b, b), 1.0, 0.0).astype(BF16)
    return jnp.dot(move, block, preferred_element_type=F32)


def rate_of(params, i, u):
    return jax.nn.sigmoid(params[0, i] * (u - params[1, i])).astype(BF16)


def half_of(ref, lead, half, rows):
    return ref[lead, pl.ds(pl.multiple_of(half * rows, 16), rows), :]


def sent_rates_body(begin, params, act, rates):
    count = act.shape[0]
    pops = params.shape[1] // lax.axis_size("pop")
    first = lax.axis_index("pop") * pops + begin
    for i in range(count):
        rates[i] = in_wire_order(rate_of(params, first + i, act[i])).astype(BF16)


def own_half_body(params, act, drive, rates, sent, kept):
    pops, rows, cols = rates.shape
    first = lax.axis_index("pop") * pops
    lon = here()[0]
    for i in range(pops):
        decay = params[2, first + i]
        for half, out in ((1 - lon, sent), (lon, kept)):
            u = half_of(act, i, half, rows)
            d = half_of(drive, i, half, rows).astype(F32)
            c = ((1.0 - time_step * decay) * u + time_step * d).astype(BF16)
            out[i] = in_wire_order(c).astype(BF16)
        r = rate_of(params, first + i, half_of(act, i, lon, rows))
        rates[i] = in_wire_order(r).astype(BF16)


def edge_slots(pops, nlon, groups):
    return -(-pops * (nlon // 128) // groups)


def wire_rows(count, lanes, slots):
    return -(-(count * (lanes // 128) + 2 * slots) // 16) * 16


def packed(sums, extra, total):
    parts = [sums[:, t * 128 : (t + 1) * 128] for t in range(sums.shape[1] // 128)] + extra
    missing = total - sum(v.shape[0] for v in parts)
    if missing:
        parts.append(jnp.zeros((missing, 128), F32))
    return jnp.concatenate(parts, axis=0).astype(BF16)


def unpacked(block, count, lanes):
    block = block.astype(F32)
    parts = [block[t * count : (t + 1) * count] for t in range(lanes // 128)]
    return jnp.concatenate(parts, axis=1)


def put_fourier(table, rates, fourier):
    halves, pops, rows, cols = rates.shape
    groups, total, _ = fourier.shape
    lanes = 2 * pops * rows
    waves = table.shape[2]
    count = 2 * waves // groups
    slots = edge_slots(pops, halves * cols, groups)
    polar, inner = [], []
    for i in range(pops):
        for h in range(halves):
            strip = rates[h, i].astype(F32)
            for t in range(cols // 128):
                at = slice(t * 128, (t + 1) * 128)
                polar.append(strip[:1, at])
                inner.append(strip[rows - 1 :, at])
    nothing = [jnp.zeros((1, 128), F32)] * (slots * groups - len(polar))
    polar, inner = polar + nothing, inner + nothing
    one, two = rates[0].astype(F32), rates[1].astype(F32)
    pack = groups // 4
    block = pack * count
    for p, mix in enumerate((one + two - 1.0, one - two)):
        flat = mix.astype(BF16).reshape(pops * rows, cols)
        for b in range(waves // block):
            parts = []
            for c in range(2):
                t = table[c, p, b * block : (b + 1) * block]
                sums = nt_dot(t, flat)
                if p == 0:
                    sums = sums + jnp.sum(t.astype(F32), axis=1, keepdims=True)
                parts.append(sums)
            joined = jnp.concatenate(parts, axis=1)
            for k in range(pack):
                to = (b * pack + k) * 2 + p
                at = slice(to * slots, (to + 1) * slots)
                sums = joined[k * count : (k + 1) * count]
                fourier[to] = packed(sums, polar[at] + inner[at], total)


def first_fourier_body(table, kept, got, got_more, fourier, rates):
    some = got.shape[0]
    lon = here()[0]
    rates[lon] = kept[...]
    rates[1 - lon, :some] = got[...]
    rates[1 - lon, some:] = got_more[...]
    put_fourier(table, rates, fourier)


def lateral_of(rates, half, halo, some=None):
    _, pops, rows, cols = rates.shape
    before, after = halo[0, half], halo[1, half]
    row = lax.broadcasted_iota(jnp.int32, (rows, cols), 0)
    lane = lax.broadcasted_iota(jnp.int32, (rows, cols), 1)
    terms = []
    for i in some or range(pops):
        r = rates[half, i].astype(F32)
        other = rates[1 - half, i].astype(F32)
        east = jnp.where(lane == 0, other[:, cols - 1 :], pltpu.roll(r, 1, 1))
        west = jnp.where(lane == cols - 1, other[:, :1], pltpu.roll(r, cols - 1, 1))
        up = jnp.where(row == 0, before[i : i + 1], pltpu.roll(r, 1, 0))
        down = jnp.where(row == rows - 1, after[i : i + 1], pltpu.roll(r, rows - 1, 0))
        terms.append(east + west + up + down - 4.0 * r)
    return terms


def legendre_body(
    nlon, spectrum, weight, mixing, basis, out, held, arrived, even_s, odd_s, north_s, south_s
):
    groups, total, _ = out.shape
    count = held.shape[0]
    lanes = weight.shape[1]
    tiles = even_s.shape[0]
    _, half_lat, deg = basis.shape
    pops = mixing.shape[0]
    src = weight.shape[0]
    cores = groups // (2 * src)
    piece = half_lat // src
    lots = lanes // piece
    pops_here = lots // 2
    slots = edge_slots(pops_here, nlon, groups)
    pad = tiles * 128 - half_lat
    block = 8
    owner = lax.axis_index("band") * lax.axis_size("lon") + lax.axis_index("lon")
    core = lax.axis_index("pop")
    first_wave = owner * basis.shape[0] + core

    def fetch(r):
        return pltpu.make_async_copy(basis.at[cores * r + core], held.at[r], arrived.at[r])

    @pl.loop(0, count)
    def _(r):
        fetch(r).start()

    wide = lanes // 128 * count
    pieces = [spectrum[g].astype(F32)[wide:] for g in range(groups)]
    passed = []
    for to in range(2 * src):
        step = 1 if to < src else -1
        outward, inward = to - step, to + step
        crossing = to in (src - 1, src)
        for p in range(cores):
            if 0 <= outward < 2 * src:
                before = pieces[outward * cores + p][slots : 2 * slots]
            else:
                before = jnp.zeros((slots, 128), F32)
            after = pieces[inward * cores + p]
            after = after[slots : 2 * slots] if crossing else after[:slots]
            passed.append([before, after])

    def rows_of(p, q):
        b = (q // pops_here) * pops + p * pops_here + q % pops_here
        return slice(b * count, (b + 1) * count)

    for p in range(cores):
        evens, odds = [], []
        for s in range(src):
            north = unpacked(spectrum[s * cores + p], count, lanes)
            south = unpacked(spectrum[(2 * src - 1 - s) * cores + p], count, lanes)
            w = weight[s : s + 1]
            evens.append((w * (north + south)).astype(BF16).astype(F32))
            odds.append((w * (north - south)).astype(BF16).astype(F32))
        for q in range(lots):
            for parts, scratch in ((evens, even_s), (odds, odd_s)):
                spairs = [v[:, q * piece : (q + 1) * piece] for v in parts]
                if pad:
                    spairs.append(jnp.zeros((count, pad), F32))
                joined = jnp.concatenate(spairs, axis=1)
                for t in range(tiles):
                    scratch[t, rows_of(p, q), :] = joined[:, t * 128 : (t + 1) * 128]

    degree = lax.broadcasted_iota(jnp.int32, (2 * pops, deg), 1)

    def several(start, size):
        for at in range(size):
            fetch(start + at).wait()
        todo = []
        for at in range(size):
            r = start + at
            m = first_wave + cores * r
            rows = pl.ds(r, 2 * pops, stride=count)
            lhs = jnp.concatenate(
                [
                    jnp.concatenate([scratch[t, rows, :] for t in range(tiles)], axis=1)
                    for scratch in (even_s, odd_s)
                ],
                axis=0,
            )[:, :half_lat].astype(BF16)
            both = jnp.dot(lhs, held[r], preferred_element_type=F32)
            odd = ((degree - m) & 1) == 1
            coeffs = jnp.where(odd, both[2 * pops :], both[: 2 * pops])
            coeffs = jnp.where(degree >= m, coeffs, 0.0)
            mixed = []
            for c in range(2):
                total = None
                for j in range(pops):
                    term = mixing[j] * coeffs[c * pops + j : c * pops + j + 1]
                    total = term if total is None else total + term
                mixed.append(total)
            mixed = jnp.concatenate(mixed, axis=0)
            lhs2 = jnp.concatenate([mixed, jnp.where(odd, -mixed, mixed)], axis=0).astype(BF16)
            todo.append((r, m, rows, lhs2))
        for r, m, rows, lhs2 in todo:
            amplitude = jnp.where(m == 0, 1.0, 2.0)
            field = nt_dot(lhs2, held[r]) * amplitude
            if pad:
                field = jnp.concatenate([field, jnp.zeros((4 * pops, pad), F32)], axis=1)
            for t in range(tiles):
                north_s[t, rows, :] = field[: 2 * pops, t * 128 : (t + 1) * 128]
                south_s[t, rows, :] = field[2 * pops :, t * 128 : (t + 1) * 128]

    several(0, block // 2)
    several(block // 2, block // 2)

    @pl.loop(1, count // block)
    def _(step):
        several(step * block, block)

    for scratch, south in ((north_s, False), (south_s, True)):
        for p in range(cores):
            wide = [
                jnp.concatenate(
                    [scratch[t, rows_of(p, q), :] for t in range(tiles)], axis=1
                )
                for q in range(lots)
            ]
            for s in range(src):
                to = (2 * src - 1 - s if south else s) * cores + p
                spairs = [v[:, s * piece : (s + 1) * piece] for v in wide]
                out[to] = packed(jnp.concatenate(spairs, axis=1), passed[to], total)


def turned(spectrum, turned_s):
    groups = spectrum.shape[0]
    lanes, deg = turned_s.shape
    order = list(range(0, groups, 2)) + list(range(1, groups, 2))
    blocks = [unpacked(spectrum[g], deg // groups, lanes) for g in order]
    turned_s[...] = jnp.concatenate(blocks, axis=0).astype(BF16).T


def put_ends(spectrum, turned_s, halo):
    groups = spectrum.shape[0]
    lanes, deg = turned_s.shape
    _, halves, pops, cols = halo.shape
    slots = edge_slots(pops, halves * cols, groups)
    wide = lanes // 128 * (deg // groups)
    pieces = [spectrum[g].astype(F32)[wide:] for g in range(groups)]
    per = cols // 128
    for side in range(2):
        for i in range(pops):
            for h in range(halves):
                for t in range(per):
                    at = (i * halves + h) * per + t
                    row = side * slots + at % slots
                    halo[side, h, i : i + 1, t * 128 : (t + 1) * 128] = pieces[at // slots][
                        row : row + 1
                    ]


def synth_of(both, table, first=0, count=None):
    half = both.shape[0] // 2
    count = half if count is None else count
    waves, cols = table.shape[2:]
    sums = []
    for p in range(2):
        total = None
        for c in range(2):
            at = c * half + first
            some = both[at : at + count, p * waves : (p + 1) * waves]
            term = jnp.dot(some, table[c, p], preferred_element_type=F32)
            total = term if total is None else total + term
        sums.append(total * (time_step / (2 * cols)))
    return sums


def middle_body(
    params, table, spectrum, old, kept, got, fourier, rates, inner, turned_s, halo
):
    halves, pops, rows, cols = rates.shape
    first = lax.axis_index("pop") * pops
    turned(spectrum, turned_s)
    put_ends(spectrum, turned_s, halo)
    even, odd = synth_of(turned_s, table)
    for h in range(halves):
        at = slice(h * cols, (h + 1) * cols)
        lateral = lateral_of(old, h, halo)
        for i in range(pops):
            here_rows = slice(i * rows, (i + 1) * rows)
            v = even[here_rows] + odd[here_rows] if h == 0 else even[here_rows] - odd[here_rows]
            v = v + (time_step * params[3, first + i]) * lateral[i]
            inner[i, :, at] = v
            u = jnp.where(here()[0] == h, kept[i], got[i]).astype(F32) + v
            rates[h, i] = rate_of(params, first + i, u)
    put_fourier(table, rates, fourier)


def put_inner(params, table, rates, halo, inner, both, half, some, out):
    _, pops, rows, cols = rates.shape
    first = lax.axis_index("pop") * pops
    at = pl.ds(pl.multiple_of(half * cols, 128), cols)
    even, odd = synth_of(both, table, some[0] * rows, len(some) * rows)
    synth = even + jnp.where(half == 1, -1.0, 1.0) * odd
    lateral = lateral_of(rates, half, halo, some)
    for k, i in enumerate(some):
        v = synth[k * rows : (k + 1) * rows]
        v = v + (time_step * params[3, first + i]) * lateral[k]
        v = v + (1.0 - time_step * params[2, first + i]) * inner[i, :, at]
        out[k] = v.astype(BF16)


def sent_inner_body(some, params, table, spectrum, rates, inner, out, both, halo):
    turned(spectrum, both)
    put_ends(spectrum, both, halo)
    put_inner(params, table, rates, halo, inner, both, 1 - here()[0], some, out)


def more_inner_body(some, params, table, both, rates, halo, inner, out):
    put_inner(params, table, rates, halo, inner, both, 1 - here()[0], some, out)


def kept_inner_body(some, params, table, both, rates, halo, inner, out):
    put_inner(params, table, rates, halo, inner, both, here()[0], some, out)


def grid_update_body(begin, pops, params, act, drive, inner, *refs):
    out = refs[-1]
    i = lax.axis_index("pop") * pops + begin + pl.program_id(0)
    keep = 1.0 - time_step * params[2, i]
    d = time_step * drive[0].astype(F32)
    out[0] = keep * (keep * act[0] + d) + d + in_wire_order(inner[0])


def by_parts(activity, drive, basis, kernels, conn_block, coupling, rate_params):
    pops_here, lat_here, cols = activity.shape
    owned, half_lat, deg = basis.shape
    bands, lons, cores = (lax.axis_size(a) for a in ("band", "lon", "pop"))
    owners = bands * lons
    groups = owners * cores
    count = owned // cores
    rows = lat_here // lons
    nlat, nlon = bands * lat_here, lons * cols
    pops = pops_here * cores
    lanes = 2 * pops_here * rows
    band, lon, core = (lax.axis_index(a) for a in ("band", "lon", "pop"))
    owner = band * lons + lon
    table = jnp.asarray(fourier_table(nlon, owners, owned))
    weights = lat_weights(nlat).reshape(owners // 2, 1, rows)
    weights = jnp.asarray(np.tile(weights, (1, 2 * pops_here, 1)).reshape(owners // 2, lanes))
    onehot = (conn_block[..., None] == jnp.arange(kernels.shape[0], dtype=jnp.int32)).astype(F32)
    mixing = coupling[..., None] * jnp.einsum(
        "ijb,bn->ijn", onehot, kernels, precision=lax.Precision.HIGHEST
    )
    mixing = jnp.swapaxes(mixing, 0, 1)
    swap = [(0, 1), (1, 0)]

    by_pop = pl.BlockSpec((1, rows, cols), lambda i: (i, 0, 0))
    on_grid = pl.BlockSpec((1, lat_here, cols), lambda i: (i, 0, 0))
    piece = shape(pops_here, rows, cols)
    wire = shape(groups, wire_rows(count, lanes, edge_slots(pops_here, nlon, groups)), 128)
    ends = shape(2, lons, pops_here, cols, dtype=F32)
    both_halves = shape(lons, pops_here, rows, cols)
    state = shape(pops_here, rows, nlon, dtype=F32)

    some = pops_here // 2
    pairs = (list(range(some)), list(range(some, pops_here)))
    got = []
    for k, pair in enumerate(pairs):
        sent = call(
            functools.partial(sent_rates_body, pair[0]),
            shape(some, rows, cols),
            60,
            grid=(1,),
            in_specs=[
                scalars(),
                pl.BlockSpec((some, rows, cols), lambda i, k=k: (k, 1 - lax.axis_index("lon"), 0)),
            ],
            out_specs=whole(),
        )(rate_params, activity)
        got.append(lax.ppermute(sent, "lon", swap))
    kept, carried_sent, carried_kept = call(
        own_half_body,
        (piece,) * 3,
        24,
        2 * 10**9,
        10**7,
        in_specs=[scalars()] + [whole()] * 2,
        out_specs=(whole(),) * 3,
    )(rate_params, activity, drive)
    *got, mixing = lax.optimization_barrier((*got, mixing))
    fourier, rates = call(
        first_fourier_body,
        (wire, both_halves),
        24,
        in_specs=[whole()] * 4,
        out_specs=(whole(),) * 2,
    )(table, kept, *got)

    def coupled(fourier, *more):
        spectrum = lax.all_to_all(fourier, EVERYONE, 0, 0, tiled=True)
        spectrum, *more = lax.optimization_barrier((spectrum, *more))
        more = [lax.ppermute(v, "lon", swap) for v in more]
        tiles = -(-half_lat // 128)
        scratch = pltpu.VMEM((tiles, 2 * pops * count, 128), F32)
        synthesis = call(
            functools.partial(legendre_body, nlon),
            wire,
            40,
            5 * 10**9,
            2 * 10**7,
            in_specs=[whole()] * 3 + [pl.BlockSpec(memory_space=pl.ANY)],
            out_specs=whole(),
            scratch_shapes=[
                pltpu.VMEM((count, half_lat, deg), BF16),
                pltpu.SemaphoreType.DMA((count,)),
            ]
            + [scratch] * 4,
        )(spectrum, weights, mixing, basis)
        synthesis, more = lax.optimization_barrier((synthesis, more))
        back = lax.all_to_all(synthesis, EVERYONE, 0, 0, tiled=True)
        return back, more

    back, (carried_got,) = coupled(fourier, carried_sent)
    both = shape(lanes, deg)
    fourier, rates, inner = call(
        middle_body,
        (wire, both_halves, state),
        32,
        in_specs=[scalars()] + [whole()] * 5,
        out_specs=(whole(),) * 3,
        scratch_shapes=[pltpu.VMEM(both.shape, BF16), pltpu.VMEM(ends.shape, F32)],
    )(rate_params, table, back, rates, carried_kept, carried_got)
    back, _ = coupled(fourier)
    sent, both, halo = call(
        functools.partial(sent_inner_body, pairs[0]),
        (shape(some, rows, cols), both, ends),
        24,
        in_specs=[scalars()] + [whole()] * 4,
        out_specs=(whole(),) * 3,
    )(rate_params, table, back, rates, inner)

    def inner_of(body, which):
        return call(
            functools.partial(body, which),
            shape(len(which), rows, cols),
            16,
            10**9,
            5 * 10**6,
            in_specs=[scalars()] + [whole()] * 5,
            out_specs=whole(),
        )(rate_params, table, both, rates, halo, inner)

    def update(which, half, inner, *earlier):
        begin = which[0]
        block = pl.BlockSpec(
            (1, rows, cols),
            lambda i: (begin + i, jnp.abs(half - lax.axis_index("lon")), 0),
        )
        return call(
            functools.partial(grid_update_body, begin, pops_here),
            shape(*activity.shape, dtype=F32),
            24,
            10**7,
            4 * 10**6,
            grid=(len(which),),
            in_specs=[scalars(), block, block, by_pop]
            + [pl.BlockSpec(memory_space=pl.ANY)] * len(earlier),
            out_specs=block,
            input_output_aliases={4: 0} if earlier else {},
        )(rate_params, activity, drive, inner, *earlier)

    got = [lax.ppermute(sent, "lon", swap)]
    got.append(lax.ppermute(inner_of(more_inner_body, pairs[1]), "lon", swap))
    everyone = pairs[0] + pairs[1]
    out = update(everyone, 0, inner_of(kept_inner_body, everyone))
    for pair, there in zip(pairs, got):
        out = update(pair, 1, there, out)
    return out


def with_halo(shard, sides, width):
    for axis, dim in sides:
        size, length = (lax.axis_size(axis), shard.shape[dim])
        up = [(i, (i + 1) % size) for i in range(size - 1)]
        down = [(j, i) for i, j in up]
        last = lax.slice_in_dim(shard, length - width, length, axis=dim)
        leading = lax.slice_in_dim(shard, 0, width, axis=dim)
        before = lax.ppermute(last, axis, up)
        after = lax.ppermute(leading, axis, down)
        shard = jnp.concatenate([before, shard, after], axis=dim)
    return shard


def plain_table(nlon, deg):
    longitude = jnp.arange(nlon, dtype=jnp.int32)
    wavenumber = jnp.arange(deg, dtype=jnp.int32)
    phase = longitude[:, None] * wavenumber[None, :] % nlon
    angle = phase.astype(jnp.float32) * (2.0 * math.pi / nlon)
    return jnp.stack([jnp.cos(angle), jnp.sin(angle)], axis=1).astype(jnp.bfloat16)


def to_owners(fourier):
    return lax.all_to_all(fourier, ("band", "lon"), split_axis=2, concat_axis=3, tiled=True)


def to_latitudes(synthesis):
    return lax.all_to_all(synthesis, ("band", "lon"), split_axis=3, concat_axis=2, tiled=True)


def by_arrays(activity, drive, basis, kernels, conn_block, coupling, rate_params):
    pop_here = activity.shape[0]
    owned_count = basis.shape[0]
    half_lat = basis.shape[1]
    deg = basis.shape[2]
    nlon = activity.shape[2] * lax.axis_size("lon")
    quarter = deg // 2
    owner_index = lax.axis_index("band") * lax.axis_size("lon") + lax.axis_index("lon")
    pop_first = lax.axis_index("pop") * pop_here
    params = lax.dynamic_slice_in_dim(rate_params, pop_first, pop_here, 1)
    gain_row, thresh, decay_row, lateral = (params[0], params[1], params[2], params[3])
    cos_sin = plain_table(nlon, deg)
    weights = jnp.asarray(lat_weights(2 * half_lat))
    wavenumber = owner_index * owned_count + jnp.arange(owned_count, dtype=jnp.int32)
    degree = jnp.arange(deg, dtype=jnp.int32)
    triangle = degree[None, :] >= wavenumber[:, None]
    slots = jnp.arange(2, dtype=jnp.int32)
    parity_pick = (slots[None, :] == (wavenumber % 2)[:, None])[None, None, :, :, None]
    every_wave = jnp.arange(deg, dtype=jnp.int32)
    amplitude = jnp.where(every_wave == 0, 1.0, 2.0).astype(jnp.bfloat16)
    coup_own = lax.dynamic_slice_in_dim(coupling, pop_first, pop_here, 0)
    block_own = lax.dynamic_slice_in_dim(conn_block, pop_first, pop_here, 0)
    onehot = (block_own[..., None] == jnp.arange(kernels.shape[0], dtype=jnp.int32)).astype(
        jnp.float32
    )
    mixing = coup_own[..., None] * jnp.einsum(
        "ijb,bn->ijn", onehot, kernels, precision=lax.Precision.HIGHEST
    )
    basis_split = basis.reshape(owned_count, half_lat, quarter, 2)
    drive_f32 = drive.astype(jnp.float32)
    activity_now = activity
    for step_index in range(STEPS):
        rates = jax.nn.sigmoid(
            gain_row[:, None, None] * (activity_now - thresh[:, None, None])
        ).astype(jnp.bfloat16)
        lat_rows = lax.all_to_all(rates, "lon", split_axis=1, concat_axis=2, tiled=True)
        fourier = jnp.einsum(
            "ijk,kcm->icmj", lat_rows, cos_sin, preferred_element_type=jnp.float32
        ).astype(jnp.bfloat16)
        spectrum = to_owners(fourier)
        northern = spectrum[..., :half_lat].astype(jnp.float32)
        southern = jnp.flip(spectrum[..., half_lat:], axis=3).astype(jnp.float32)
        even_part = (weights * (northern + southern)).astype(jnp.bfloat16)
        odd_part = (weights * (northern - southern)).astype(jnp.bfloat16)
        operand = jnp.where(parity_pick, even_part[:, :, :, None, :], odd_part[:, :, :, None, :])
        coeffs = jnp.einsum(
            "icmsj,mjqs->icmqs", operand, basis_split, preferred_element_type=jnp.float32
        )
        coeffs = coeffs.reshape(pop_here, 2, owned_count, deg)
        coeffs = jnp.where(triangle[None, None], coeffs, 0.0)
        gathered = lax.all_gather(coeffs.astype(jnp.bfloat16), "pop", axis=0, tiled=True).astype(
            coeffs.dtype
        )
        mixed_spec = jnp.sum(mixing[:, :, None, None, :] * gathered[None], axis=1).astype(
            jnp.bfloat16
        )
        degree_parts = jnp.einsum(
            "icmqs,mjqs->icmsj",
            mixed_spec.reshape(pop_here, 2, owned_count, quarter, 2),
            basis_split,
            preferred_element_type=jnp.float32,
        )
        same_parity = jnp.sum(jnp.where(parity_pick, degree_parts, 0.0), axis=3)
        other_parity = jnp.sum(jnp.where(parity_pick, 0.0, degree_parts), axis=3)
        synthesis = jnp.concatenate(
            [same_parity + other_parity, jnp.flip(same_parity - other_parity, axis=3)], axis=3
        ).astype(jnp.bfloat16)
        returned = to_latitudes(synthesis)
        scaled = returned * amplitude[None, None, :, None]
        synth_field = jnp.einsum(
            "icmj,kcm->ijk", scaled, cos_sin, preferred_element_type=jnp.float32
        ) * (1.0 / nlon)
        padded = with_halo(lat_rows, ((("band", "lon"), 1),), 1).astype(jnp.float32)
        rates_f32 = lat_rows.astype(jnp.float32)
        lateral_term = (
            jnp.roll(rates_f32, 1, axis=2)
            + jnp.roll(rates_f32, -1, axis=2)
            + padded[:, 2:, :]
            + padded[:, :-2, :]
            - 4.0 * rates_f32
        )
        coupled = synth_field + lateral[:, None, None] * lateral_term
        coupled_grid = lax.all_to_all(
            coupled.astype(jnp.bfloat16), "lon", split_axis=2, concat_axis=1, tiled=True
        ).astype(coupled.dtype)
        forcing = -decay_row[:, None, None] * activity_now + coupled_grid + drive_f32
        activity_now = activity_now + time_step * forcing
    return activity_now


def solution(mesh):
    bands, lons, cores = (mesh.shape[a] for a in ("band", "lon", "pop"))

    def local(activity, drive, basis, *rest):
        rows, owned = activity.shape[1] // lons, basis.shape[0]
        fits = (
            bands % 2 == 0
            and activity.shape[0] % 2 == 0
            and lons == 2
            and cores == 2
            and bands * lons * cores % 4 == 0
            and owned % (8 * cores) == 0
            and rows % 16 == 0
            and activity.shape[2] % 128 == 0
            and 2 * activity.shape[0] * rows % 128 == 0
        )
        return (by_parts if fits else by_arrays)(activity, drive, basis, *rest)

    in_specs = (
        P(("subj", "pop"), "band", "lon"),
        P(("subj", "pop"), "band", "lon"),
        P(("subj", "band", "lon"), None, None),
        P(),
        P(),
        P("subj", None),
        P("subj", None),
    )
    out_specs = P(("subj", "pop"), "band", "lon")
    return jax.shard_map(local, mesh=mesh, in_specs=in_specs, out_specs=out_specs, check_vma=False)
```

```python
import functools
import math

import jax
import jax.numpy as jnp
import ml_dtypes
import numpy as np
from jax import lax
from jax.experimental import pallas as pl
from jax.experimental.pallas import tpu as pltpu
from jax.sharding import PartitionSpec as P

STEPS = 2
time_step = 0.5
F32 = jnp.float32
BF16 = jnp.bfloat16
OWNERS = ("band", "lon")
EVERYONE = ("band", "lon", "pop")
MIB = 1 << 20


def call(body, out_shape, vmem_mib, flops=0, nbytes=0, **kw):
    return pl.pallas_call(
        body,
        out_shape=out_shape,
        compiler_params=pltpu.CompilerParams(vmem_limit_bytes=vmem_mib * MIB),
        cost_estimate=pl.CostEstimate(flops=flops, bytes_accessed=nbytes, transcendentals=0),
        **kw,
    )


def whole():
    return pl.BlockSpec(memory_space=pltpu.VMEM)


def scalars():
    return pl.BlockSpec(memory_space=pltpu.SMEM)


def shape(*dims, dtype=BF16):
    return jax.ShapeDtypeStruct(dims, dtype)


def nt_dot(a, b):
    return lax.dot_general(a, b, (((1,), (1,)), ((), ())), preferred_element_type=F32)


def fourier_table(nlon, owners, owned):
    wave = np.arange(owners * owned, dtype=np.int64).reshape(-1, 2).T.reshape(-1)
    phase = wave[:, None] * np.arange(nlon // 2, dtype=np.int64)[None, :] % nlon
    angle = phase.astype(np.float32) * np.float32(2.0 * math.pi / nlon)
    table = np.stack([np.cos(angle), np.sin(angle)]).astype(ml_dtypes.bfloat16)
    return table.reshape(2, 2, -1, nlon // 2)


def lat_weights(nlat):
    row_index = np.arange(nlat // 2, dtype=np.float32)
    colatitude = np.float32(math.pi) * (4.0 * row_index + 3.0) / np.float32(4.0 * nlat + 2.0)
    return (np.float32(math.pi) * np.sin(colatitude) / np.float32(nlat)).astype(np.float32)


def here():
    bands, lons = lax.axis_size("band"), lax.axis_size("lon")
    band, lon = lax.axis_index("band"), lax.axis_index("lon")
    owner, half = band * lons + lon, bands * lons // 2
    at_equator = jnp.logical_or(owner == half - 1, owner == half)
    at_pole = jnp.logical_or(owner == 0, owner == 2 * half - 1)
    return lon, owner >= half, at_equator, at_pole


def in_wire_order(block):
    rows = block.shape[0]
    a = lax.broadcasted_iota(jnp.int32, (rows, rows), 0)
    b = lax.broadcasted_iota(jnp.int32, (rows, rows), 1)
    move = jnp.where(a == jnp.where(here()[1], rows - 1 - b, b), 1.0, 0.0).astype(BF16)
    return jnp.dot(move, block, preferred_element_type=F32)


def rate_of(params, i, u):
    return jax.nn.sigmoid(params[0, i] * (u - params[1, i])).astype(BF16)


def half_of(ref, lead, half, rows):
    return ref[lead, pl.ds(pl.multiple_of(half * rows, 16), rows), :]


def sent_rates_body(begin, params, act, rates):
    count = act.shape[0]
    pops = params.shape[1] // lax.axis_size("pop")
    first = lax.axis_index("pop") * pops + begin
    for i in range(count):
        rates[i] = in_wire_order(rate_of(params, first + i, act[i])).astype(BF16)


def own_half_body(params, act, drive, rates, sent, kept):
    pops, rows, cols = rates.shape
    first = lax.axis_index("pop") * pops
    lon = here()[0]
    for i in range(pops):
        decay = params[2, first + i]
        for half, out in ((1 - lon, sent), (lon, kept)):
            u = half_of(act, i, half, rows)
            d = half_of(drive, i, half, rows).astype(F32)
            c = ((1.0 - time_step * decay) * u + time_step * d).astype(BF16)
            out[i] = in_wire_order(c).astype(BF16)
        r = rate_of(params, first + i, half_of(act, i, lon, rows))
        rates[i] = in_wire_order(r).astype(BF16)


def edge_slots(pops, nlon, groups):
    return -(-pops * (nlon // 128) // groups)


def wire_rows(count, lanes, slots):
    return -(-(count * (lanes // 128) + 2 * slots) // 16) * 16


def packed(sums, extra, total):
    parts = [sums[:, t * 128 : (t + 1) * 128] for t in range(sums.shape[1] // 128)] + extra
    missing = total - sum(v.shape[0] for v in parts)
    if missing:
        parts.append(jnp.zeros((missing, 128), F32))
    return jnp.concatenate(parts, axis=0).astype(BF16)


def unpacked(block, count, lanes):
    block = block.astype(F32)
    parts = [block[t * count : (t + 1) * count] for t in range(lanes // 128)]
    return jnp.concatenate(parts, axis=1)


def put_fourier(table, rates, fourier):
    halves, pops, rows, cols = rates.shape
    groups, total, _ = fourier.shape
    lanes = 2 * pops * rows
    waves = table.shape[2]
    count = 2 * waves // groups
    slots = edge_slots(pops, halves * cols, groups)
    polar, inner = [], []
    for i in range(pops):
        for h in range(halves):
            strip = rates[h, i].astype(F32)
            for t in range(cols // 128):
                at = slice(t * 128, (t + 1) * 128)
                polar.append(strip[:1, at])
                inner.append(strip[rows - 1 :, at])
    nothing = [jnp.zeros((1, 128), F32)] * (slots * groups - len(polar))
    polar, inner = polar + nothing, inner + nothing
    one, two = rates[0].astype(F32), rates[1].astype(F32)
    for p, mix in enumerate((one + two - 1.0, one - two)):
        flat = mix.astype(BF16).reshape(pops * rows, cols)
        t = jnp.concatenate([table[0, p], table[1, p]], axis=0)
        sums = nt_dot(t, flat)
        if p == 0:
            sums = sums + jnp.sum(t.astype(F32), axis=1, keepdims=True)
        for k in range(groups // 2):
            own = slice(k * count, (k + 1) * count)
            joined = jnp.concatenate([sums[:waves][own], sums[waves:][own]], axis=1)
            to = k * 2 + p
            at = slice(to * slots, (to + 1) * slots)
            fourier[to] = packed(joined, polar[at] + inner[at], total)


def first_fourier_body(table, kept, got, got_more, fourier, rates):
    some = got.shape[0]
    lon = here()[0]
    rates[lon] = kept[...]
    rates[1 - lon, :some] = got[...]
    rates[1 - lon, some:] = got_more[...]
    put_fourier(table, rates, fourier)


def lateral_of(rates, half, halo, some=None):
    _, pops, rows, cols = rates.shape
    before, after = halo[0, half], halo[1, half]
    row = lax.broadcasted_iota(jnp.int32, (rows, cols), 0)
    lane = lax.broadcasted_iota(jnp.int32, (rows, cols), 1)
    terms = []
    for i in some or range(pops):
        r = rates[half, i].astype(F32)
        other = rates[1 - half, i].astype(F32)
        east = jnp.where(lane == 0, other[:, cols - 1 :], pltpu.roll(r, 1, 1))
        west = jnp.where(lane == cols - 1, other[:, :1], pltpu.roll(r, cols - 1, 1))
        up = jnp.where(row == 0, before[i : i + 1], pltpu.roll(r, 1, 0))
        down = jnp.where(row == rows - 1, after[i : i + 1], pltpu.roll(r, rows - 1, 0))
        terms.append(east + west + up + down - 4.0 * r)
    return terms


def legendre_body(
    nlon, spectrum, weight, mixing, basis, out, held, arrived, even_s, odd_s, north_s, south_s
):
    groups, total, _ = out.shape
    count = held.shape[0]
    lanes = weight.shape[1]
    tiles = even_s.shape[0]
    _, half_lat, deg = basis.shape
    pops = mixing.shape[0]
    src = weight.shape[0]
    cores = groups // (2 * src)
    piece = half_lat // src
    lots = lanes // piece
    pops_here = lots // 2
    slots = edge_slots(pops_here, nlon, groups)
    pad = tiles * 128 - half_lat
    block = 8
    owner = lax.axis_index("band") * lax.axis_size("lon") + lax.axis_index("lon")
    core = lax.axis_index("pop")
    first_wave = owner * basis.shape[0] + core

    def fetch(r):
        return pltpu.make_async_copy(basis.at[cores * r + core], held.at[r], arrived.at[r])

    @pl.loop(0, count)
    def _(r):
        fetch(r).start()

    wide = lanes // 128 * count
    pieces = [spectrum[g].astype(F32)[wide:] for g in range(groups)]
    passed = []
    for to in range(2 * src):
        step = 1 if to < src else -1
        outward, inward = to - step, to + step
        crossing = to in (src - 1, src)
        for p in range(cores):
            if 0 <= outward < 2 * src:
                before = pieces[outward * cores + p][slots : 2 * slots]
            else:
                before = jnp.zeros((slots, 128), F32)
            after = pieces[inward * cores + p]
            after = after[slots : 2 * slots] if crossing else after[:slots]
            passed.append([before, after])

    def rows_of(p, q):
        b = (q // pops_here) * pops + p * pops_here + q % pops_here
        return slice(b * count, (b + 1) * count)

    for p in range(cores):
        evens, odds = [], []
        for s in range(src):
            north = unpacked(spectrum[s * cores + p], count, lanes)
            south = unpacked(spectrum[(2 * src - 1 - s) * cores + p], count, lanes)
            w = weight[s : s + 1]
            evens.append((w * (north + south)).astype(BF16).astype(F32))
            odds.append((w * (north - south)).astype(BF16).astype(F32))
        for q in range(lots):
            for parts, scratch in ((evens, even_s), (odds, odd_s)):
                spairs = [v[:, q * piece : (q + 1) * piece] for v in parts]
                if pad:
                    spairs.append(jnp.zeros((count, pad), F32))
                joined = jnp.concatenate(spairs, axis=1)
                for t in range(tiles):
                    scratch[t, rows_of(p, q), :] = joined[:, t * 128 : (t + 1) * 128]

    degree = lax.broadcasted_iota(jnp.int32, (2 * pops, deg), 1)

    def several(start, size):
        for at in range(size):
            fetch(start + at).wait()
        todo = []
        for at in range(size):
            r = start + at
            m = first_wave + cores * r
            rows = pl.ds(r, 2 * pops, stride=count)
            lhs = jnp.concatenate(
                [
                    jnp.concatenate([scratch[t, rows, :] for t in range(tiles)], axis=1)
                    for scratch in (even_s, odd_s)
                ],
                axis=0,
            )[:, :half_lat].astype(BF16)
            both = jnp.dot(lhs, held[r], preferred_element_type=F32)
            odd = ((degree - m) & 1) == 1
            coeffs = jnp.where(odd, both[2 * pops :], both[: 2 * pops])
            coeffs = jnp.where(degree >= m, coeffs, 0.0)
            mixed = []
            for c in range(2):
                total = None
                for j in range(pops):
                    term = mixing[j] * coeffs[c * pops + j : c * pops + j + 1]
                    total = term if total is None else total + term
                mixed.append(total)
            mixed = jnp.concatenate(mixed, axis=0)
            lhs2 = jnp.concatenate([mixed, jnp.where(odd, -mixed, mixed)], axis=0).astype(BF16)
            todo.append((r, m, rows, lhs2))
        for r, m, rows, lhs2 in todo:
            amplitude = jnp.where(m == 0, 1.0, 2.0)
            field = nt_dot(lhs2, held[r]) * amplitude
            if pad:
                field = jnp.concatenate([field, jnp.zeros((4 * pops, pad), F32)], axis=1)
            for t in range(tiles):
                north_s[t, rows, :] = field[: 2 * pops, t * 128 : (t + 1) * 128]
                south_s[t, rows, :] = field[2 * pops :, t * 128 : (t + 1) * 128]

    several(0, block // 2)
    several(block // 2, block // 2)

    @pl.loop(1, count // block)
    def _(step):
        several(step * block, block)

    for scratch, south in ((north_s, False), (south_s, True)):
        for p in range(cores):
            wide = [
                jnp.concatenate(
                    [scratch[t, rows_of(p, q), :] for t in range(tiles)], axis=1
                )
                for q in range(lots)
            ]
            for s in range(src):
                to = (2 * src - 1 - s if south else s) * cores + p
                spairs = [v[:, s * piece : (s + 1) * piece] for v in wide]
                out[to] = packed(jnp.concatenate(spairs, axis=1), passed[to], total)


def turned(spectrum, turned_s):
    groups = spectrum.shape[0]
    lanes, deg = turned_s.shape
    order = list(range(0, groups, 2)) + list(range(1, groups, 2))
    blocks = [unpacked(spectrum[g], deg // groups, lanes) for g in order]
    turned_s[...] = jnp.concatenate(blocks, axis=0).astype(BF16).T


def put_ends(spectrum, turned_s, halo):
    groups = spectrum.shape[0]
    lanes, deg = turned_s.shape
    _, halves, pops, cols = halo.shape
    slots = edge_slots(pops, halves * cols, groups)
    wide = lanes // 128 * (deg // groups)
    pieces = [spectrum[g].astype(F32)[wide:] for g in range(groups)]
    per = cols // 128
    for side in range(2):
        for i in range(pops):
            for h in range(halves):
                for t in range(per):
                    at = (i * halves + h) * per + t
                    row = side * slots + at % slots
                    halo[side, h, i : i + 1, t * 128 : (t + 1) * 128] = pieces[at // slots][
                        row : row + 1
                    ]


def synth_of(both, table, first=0, count=None):
    half = both.shape[0] // 2
    count = half if count is None else count
    waves, cols = table.shape[2:]
    sums = []
    for p in range(2):
        total = None
        for c in range(2):
            at = c * half + first
            some = both[at : at + count, p * waves : (p + 1) * waves]
            term = jnp.dot(some, table[c, p], preferred_element_type=F32)
            total = term if total is None else total + term
        sums.append(total * (time_step / (2 * cols)))
    return sums


def middle_body(
    params, table, spectrum, old, kept, got, fourier, rates, inner, turned_s, halo
):
    halves, pops, rows, cols = rates.shape
    first = lax.axis_index("pop") * pops
    turned(spectrum, turned_s)
    put_ends(spectrum, turned_s, halo)
    even, odd = synth_of(turned_s, table)
    for h in range(halves):
        at = slice(h * cols, (h + 1) * cols)
        lateral = lateral_of(old, h, halo)
        for i in range(pops):
            here_rows = slice(i * rows, (i + 1) * rows)
            v = even[here_rows] + odd[here_rows] if h == 0 else even[here_rows] - odd[here_rows]
            v = v + (time_step * params[3, first + i]) * lateral[i]
            inner[i, :, at] = v
            u = jnp.where(here()[0] == h, kept[i], got[i]).astype(F32) + v
            rates[h, i] = rate_of(params, first + i, u)
    put_fourier(table, rates, fourier)


def put_inner(params, table, rates, halo, inner, both, half, some, out):
    _, pops, rows, cols = rates.shape
    first = lax.axis_index("pop") * pops
    at = pl.ds(pl.multiple_of(half * cols, 128), cols)
    even, odd = synth_of(both, table, some[0] * rows, len(some) * rows)
    synth = even + jnp.where(half == 1, -1.0, 1.0) * odd
    lateral = lateral_of(rates, half, halo, some)
    for k, i in enumerate(some):
        v = synth[k * rows : (k + 1) * rows]
        v = v + (time_step * params[3, first + i]) * lateral[k]
        v = v + (1.0 - time_step * params[2, first + i]) * inner[i, :, at]
        out[k] = v.astype(BF16)


def sent_inner_body(some, params, table, spectrum, rates, inner, out, both, halo):
    turned(spectrum, both)
    put_ends(spectrum, both, halo)
    put_inner(params, table, rates, halo, inner, both, 1 - here()[0], some, out)


def more_inner_body(some, params, table, both, rates, halo, inner, out):
    put_inner(params, table, rates, halo, inner, both, 1 - here()[0], some, out)


def kept_inner_body(some, params, table, both, rates, halo, inner, out):
    put_inner(params, table, rates, halo, inner, both, here()[0], some, out)


def grid_update_body(begin, pops, params, act, drive, inner, *refs):
    out = refs[-1]
    i = lax.axis_index("pop") * pops + begin + pl.program_id(0)
    keep = 1.0 - time_step * params[2, i]
    d = time_step * drive[0].astype(F32)
    out[0] = keep * (keep * act[0] + d) + d + in_wire_order(inner[0])


def by_parts(activity, drive, basis, kernels, conn_block, coupling, rate_params):
    pops_here, lat_here, cols = activity.shape
    owned, half_lat, deg = basis.shape
    bands, lons, cores = (lax.axis_size(a) for a in ("band", "lon", "pop"))
    owners = bands * lons
    groups = owners * cores
    count = owned // cores
    rows = lat_here // lons
    nlat, nlon = bands * lat_here, lons * cols
    pops = pops_here * cores
    lanes = 2 * pops_here * rows
    band, lon, core = (lax.axis_index(a) for a in ("band", "lon", "pop"))
    owner = band * lons + lon
    table = jnp.asarray(fourier_table(nlon, owners, owned))
    weights = lat_weights(nlat).reshape(owners // 2, 1, rows)
    weights = jnp.asarray(np.tile(weights, (1, 2 * pops_here, 1)).reshape(owners // 2, lanes))
    onehot = (conn_block[..., None] == jnp.arange(kernels.shape[0], dtype=jnp.int32)).astype(F32)
    mixing = coupling[..., None] * jnp.einsum(
        "ijb,bn->ijn", onehot, kernels, precision=lax.Precision.HIGHEST
    )
    mixing = jnp.swapaxes(mixing, 0, 1)
    swap = [(0, 1), (1, 0)]

    by_pop = pl.BlockSpec((1, rows, cols), lambda i: (i, 0, 0))
    on_grid = pl.BlockSpec((1, lat_here, cols), lambda i: (i, 0, 0))
    piece = shape(pops_here, rows, cols)
    wire = shape(groups, wire_rows(count, lanes, edge_slots(pops_here, nlon, groups)), 128)
    ends = shape(2, lons, pops_here, cols, dtype=F32)
    both_halves = shape(lons, pops_here, rows, cols)
    state = shape(pops_here, rows, nlon, dtype=F32)

    some = pops_here // 2
    pairs = (list(range(some)), list(range(some, pops_here)))
    got = []
    for k, pair in enumerate(pairs):
        sent = call(
            functools.partial(sent_rates_body, pair[0]),
            shape(some, rows, cols),
            60,
            grid=(1,),
            in_specs=[
                scalars(),
                pl.BlockSpec((some, rows, cols), lambda i, k=k: (k, 1 - lax.axis_index("lon"), 0)),
            ],
            out_specs=whole(),
        )(rate_params, activity)
        got.append(lax.ppermute(sent, "lon", swap))
    kept, carried_sent, carried_kept = call(
        own_half_body,
        (piece,) * 3,
        24,
        2 * 10**9,
        10**7,
        in_specs=[scalars()] + [whole()] * 2,
        out_specs=(whole(),) * 3,
    )(rate_params, activity, drive)
    *got, mixing = lax.optimization_barrier((*got, mixing))
    fourier, rates = call(
        first_fourier_body,
        (wire, both_halves),
        24,
        in_specs=[whole()] * 4,
        out_specs=(whole(),) * 2,
    )(table, kept, *got)

    def coupled(fourier, *more):
        spectrum = lax.all_to_all(fourier, EVERYONE, 0, 0, tiled=True)
        spectrum, *more = lax.optimization_barrier((spectrum, *more))
        more = [lax.ppermute(v, "lon", swap) for v in more]
        tiles = -(-half_lat // 128)
        scratch = pltpu.VMEM((tiles, 2 * pops * count, 128), F32)
        synthesis = call(
            functools.partial(legendre_body, nlon),
            wire,
            40,
            5 * 10**9,
            2 * 10**7,
            in_specs=[whole()] * 3 + [pl.BlockSpec(memory_space=pl.ANY)],
            out_specs=whole(),
            scratch_shapes=[
                pltpu.VMEM((count, half_lat, deg), BF16),
                pltpu.SemaphoreType.DMA((count,)),
            ]
            + [scratch] * 4,
        )(spectrum, weights, mixing, basis)
        synthesis, more = lax.optimization_barrier((synthesis, more))
        back = lax.all_to_all(synthesis, EVERYONE, 0, 0, tiled=True)
        return back, more

    back, (carried_got,) = coupled(fourier, carried_sent)
    both = shape(lanes, deg)
    fourier, rates, inner = call(
        middle_body,
        (wire, both_halves, state),
        32,
        in_specs=[scalars()] + [whole()] * 5,
        out_specs=(whole(),) * 3,
        scratch_shapes=[pltpu.VMEM(both.shape, BF16), pltpu.VMEM(ends.shape, F32)],
    )(rate_params, table, back, rates, carried_kept, carried_got)
    back, _ = coupled(fourier)
    sent, both, halo = call(
        functools.partial(sent_inner_body, pairs[0]),
        (shape(some, rows, cols), both, ends),
        24,
        in_specs=[scalars()] + [whole()] * 4,
        out_specs=(whole(),) * 3,
    )(rate_params, table, back, rates, inner)

    def inner_of(body, which):
        return call(
            functools.partial(body, which),
            shape(len(which), rows, cols),
            16,
            10**9,
            5 * 10**6,
            in_specs=[scalars()] + [whole()] * 5,
            out_specs=whole(),
        )(rate_params, table, both, rates, halo, inner)

    def update(which, half, inner, *earlier):
        begin = which[0]
        block = pl.BlockSpec(
            (1, rows, cols),
            lambda i: (begin + i, jnp.abs(half - lax.axis_index("lon")), 0),
        )
        return call(
            functools.partial(grid_update_body, begin, pops_here),
            shape(*activity.shape, dtype=F32),
            24,
            10**7,
            4 * 10**6,
            grid=(len(which),),
            in_specs=[scalars(), block, block, by_pop]
            + [pl.BlockSpec(memory_space=pl.ANY)] * len(earlier),
            out_specs=block,
            input_output_aliases={4: 0} if earlier else {},
        )(rate_params, activity, drive, inner, *earlier)

    got = [lax.ppermute(sent, "lon", swap)]
    got.append(lax.ppermute(inner_of(more_inner_body, pairs[1]), "lon", swap))
    everyone = pairs[0] + pairs[1]
    out = update(everyone, 0, inner_of(kept_inner_body, everyone))
    for pair, there in zip(pairs, got):
        out = update(pair, 1, there, out)
    return out


def with_halo(shard, sides, width):
    for axis, dim in sides:
        size, length = (lax.axis_size(axis), shard.shape[dim])
        up = [(i, (i + 1) % size) for i in range(size - 1)]
        down = [(j, i) for i, j in up]
        last = lax.slice_in_dim(shard, length - width, length, axis=dim)
        leading = lax.slice_in_dim(shard, 0, width, axis=dim)
        before = lax.ppermute(last, axis, up)
        after = lax.ppermute(leading, axis, down)
        shard = jnp.concatenate([before, shard, after], axis=dim)
    return shard


def plain_table(nlon, deg):
    longitude = jnp.arange(nlon, dtype=jnp.int32)
    wavenumber = jnp.arange(deg, dtype=jnp.int32)
    phase = longitude[:, None] * wavenumber[None, :] % nlon
    angle = phase.astype(jnp.float32) * (2.0 * math.pi / nlon)
    return jnp.stack([jnp.cos(angle), jnp.sin(angle)], axis=1).astype(jnp.bfloat16)


def to_owners(fourier):
    return lax.all_to_all(fourier, ("band", "lon"), split_axis=2, concat_axis=3, tiled=True)


def to_latitudes(synthesis):
    return lax.all_to_all(synthesis, ("band", "lon"), split_axis=3, concat_axis=2, tiled=True)


def by_arrays(activity, drive, basis, kernels, conn_block, coupling, rate_params):
    pop_here = activity.shape[0]
    owned_count = basis.shape[0]
    half_lat = basis.shape[1]
    deg = basis.shape[2]
    nlon = activity.shape[2] * lax.axis_size("lon")
    quarter = deg // 2
    owner_index = lax.axis_index("band") * lax.axis_size("lon") + lax.axis_index("lon")
    pop_first = lax.axis_index("pop") * pop_here
    params = lax.dynamic_slice_in_dim(rate_params, pop_first, pop_here, 1)
    gain_row, thresh, decay_row, lateral = (params[0], params[1], params[2], params[3])
    cos_sin = plain_table(nlon, deg)
    weights = jnp.asarray(lat_weights(2 * half_lat))
    wavenumber = owner_index * owned_count + jnp.arange(owned_count, dtype=jnp.int32)
    degree = jnp.arange(deg, dtype=jnp.int32)
    triangle = degree[None, :] >= wavenumber[:, None]
    slots = jnp.arange(2, dtype=jnp.int32)
    parity_pick = (slots[None, :] == (wavenumber % 2)[:, None])[None, None, :, :, None]
    every_wave = jnp.arange(deg, dtype=jnp.int32)
    amplitude = jnp.where(every_wave == 0, 1.0, 2.0).astype(jnp.bfloat16)
    coup_own = lax.dynamic_slice_in_dim(coupling, pop_first, pop_here, 0)
    block_own = lax.dynamic_slice_in_dim(conn_block, pop_first, pop_here, 0)
    onehot = (block_own[..., None] == jnp.arange(kernels.shape[0], dtype=jnp.int32)).astype(
        jnp.float32
    )
    mixing = coup_own[..., None] * jnp.einsum(
        "ijb,bn->ijn", onehot, kernels, precision=lax.Precision.HIGHEST
    )
    basis_split = basis.reshape(owned_count, half_lat, quarter, 2)
    drive_f32 = drive.astype(jnp.float32)
    activity_now = activity
    for step_index in range(STEPS):
        rates = jax.nn.sigmoid(
            gain_row[:, None, None] * (activity_now - thresh[:, None, None])
        ).astype(jnp.bfloat16)
        lat_rows = lax.all_to_all(rates, "lon", split_axis=1, concat_axis=2, tiled=True)
        fourier = jnp.einsum(
            "ijk,kcm->icmj", lat_rows, cos_sin, preferred_element_type=jnp.float32
        ).astype(jnp.bfloat16)
        spectrum = to_owners(fourier)
        northern = spectrum[..., :half_lat].astype(jnp.float32)
        southern = jnp.flip(spectrum[..., half_lat:], axis=3).astype(jnp.float32)
        even_part = (weights * (northern + southern)).astype(jnp.bfloat16)
        odd_part = (weights * (northern - southern)).astype(jnp.bfloat16)
        operand = jnp.where(parity_pick, even_part[:, :, :, None, :], odd_part[:, :, :, None, :])
        coeffs = jnp.einsum(
            "icmsj,mjqs->icmqs", operand, basis_split, preferred_element_type=jnp.float32
        )
        coeffs = coeffs.reshape(pop_here, 2, owned_count, deg)
        coeffs = jnp.where(triangle[None, None], coeffs, 0.0)
        gathered = lax.all_gather(coeffs.astype(jnp.bfloat16), "pop", axis=0, tiled=True).astype(
            coeffs.dtype
        )
        mixed_spec = jnp.sum(mixing[:, :, None, None, :] * gathered[None], axis=1).astype(
            jnp.bfloat16
        )
        degree_parts = jnp.einsum(
            "icmqs,mjqs->icmsj",
            mixed_spec.reshape(pop_here, 2, owned_count, quarter, 2),
            basis_split,
            preferred_element_type=jnp.float32,
        )
        same_parity = jnp.sum(jnp.where(parity_pick, degree_parts, 0.0), axis=3)
        other_parity = jnp.sum(jnp.where(parity_pick, 0.0, degree_parts), axis=3)
        synthesis = jnp.concatenate(
            [same_parity + other_parity, jnp.flip(same_parity - other_parity, axis=3)], axis=3
        ).astype(jnp.bfloat16)
        returned = to_latitudes(synthesis)
        scaled = returned * amplitude[None, None, :, None]
        synth_field = jnp.einsum(
            "icmj,kcm->ijk", scaled, cos_sin, preferred_element_type=jnp.float32
        ) * (1.0 / nlon)
        padded = with_halo(lat_rows, ((("band", "lon"), 1),), 1).astype(jnp.float32)
        rates_f32 = lat_rows.astype(jnp.float32)
        lateral_term = (
            jnp.roll(rates_f32, 1, axis=2)
            + jnp.roll(rates_f32, -1, axis=2)
            + padded[:, 2:, :]
            + padded[:, :-2, :]
            - 4.0 * rates_f32
        )
        coupled = synth_field + lateral[:, None, None] * lateral_term
        coupled_grid = lax.all_to_all(
            coupled.astype(jnp.bfloat16), "lon", split_axis=2, concat_axis=1, tiled=True
        ).astype(coupled.dtype)
        forcing = -decay_row[:, None, None] * activity_now + coupled_grid + drive_f32
        activity_now = activity_now + time_step * forcing
    return activity_now


def solution(mesh):
    bands, lons, cores = (mesh.shape[a] for a in ("band", "lon", "pop"))

    def local(activity, drive, basis, *rest):
        rows, owned = activity.shape[1] // lons, basis.shape[0]
        fits = (
            bands % 2 == 0
            and activity.shape[0] % 2 == 0
            and lons == 2
            and cores == 2
            and bands * lons * cores % 4 == 0
            and owned % (8 * cores) == 0
            and rows % 16 == 0
            and activity.shape[2] % 128 == 0
            and 2 * activity.shape[0] * rows % 128 == 0
        )
        return (by_parts if fits else by_arrays)(activity, drive, basis, *rest)

    in_specs = (
        P(("subj", "pop"), "band", "lon"),
        P(("subj", "pop"), "band", "lon"),
        P(("subj", "band", "lon"), None, None),
        P(),
        P(),
        P("subj", None),
        P("subj", None),
    )
    out_specs = P(("subj", "pop"), "band", "lon")
    return jax.shard_map(local, mesh=mesh, in_specs=in_specs, out_specs=out_specs, check_vma=False)
```
